32 devices in a mesh: lat: 8 (over z, x), lon: 4 (over y, core).
Axes of the slice: x: 2, y: 2, z: 4, core: 2. Of those that a mesh axis runs over, the one named last changes fastest.
Arguments:
- state: float32 [128, 1440, 256], P('lat', 'lon'), may hold values from -6 to 6
- winds: bfloat16 [128, 1440, 128], P('lat', 'lon'), may hold values from -0.44921875 to 0.44921875
- decay: float32 [4], replicated, may hold values from 0.005 to 0.5
- widths: int32 [128], replicated, may hold values from 0 to 480, as said below
Outputs:
- advected: bfloat16 [128, 1440, 256], P('lat', 'lon')
The draws below stay inside these ranges and needn't reach their ends.
Inputs may be any that keep to these rules, and one draw needn't show every extreme that they name: widths is 0 on rows 32 to 95 and at least 1 on the other rows; the first and last rows have exactly 480.
All inputs are finite; a program needn't handle non-finite values.
Results may differ from the reference program's by a relative error of at most 0.0075.
Values may be sent and summed in bfloat16 or wider, within the bound.
No kernel may reach another device: no remote copies, remote signals or barrier semaphores. Data moves between devices by JAX's collectives and lax.ppermute only.
A program may use at most 128 MiB of HBM per device.

```python
import math
import jax
import jax.numpy as jnp
from jax import lax

NLON = 1440
LEVELS = 64
FIELDS = 4
HMAX = 480
ADV_STEPS = 4
NLAT = 128


def draw_widths(key, part):
    index = jnp.arange(NLAT)
    quarter = NLAT // 4
    depth = jnp.where(index < quarter, quarter - index, jnp.where(index >= 3 * quarter, index - 3 * quarter + 1, 0))
    base = 1 + (depth - 1) * (HMAX - 1) // max(quarter - 1, 1)
    jitter = jax.random.randint(key, (NLAT,), 0, 3)
    width = jnp.where(depth == quarter, HMAX, jnp.minimum(base + jitter, HMAX))
    return jnp.where(depth > 0, width, 0).astype(jnp.int32)


def level_of(key, shape, pieces, least, top_value):
    def one(dim, shards_of):
        draws = jax.random.uniform(jax.random.fold_in(jax.random.fold_in(key, 6), dim), (shards_of,), jnp.float32, least / len(pieces), top_value / len(pieces))
        return jnp.repeat(jnp.exp(draws), shape[dim] // shards_of).reshape((-1,) + (1,) * (len(shape) - dim - 1))

    loudness = one(*pieces[0])
    for cut in pieces[1:]:
        loudness = loudness * one(*cut)
    return loudness


def centred(stream_key, dims, deviation, limit, split=(), dtype=jnp.bfloat16):
    level = level_of(stream_key, dims, split, -0.22, 0.18) if split else 1.0
    drawn = jax.random.normal(stream_key, dims, jnp.float32) * deviation * level
    return jnp.minimum(jnp.maximum(drawn, -limit), limit).astype(dtype)


def setup_inputs(seed: int = 0) -> dict:
    splits = jax.random.split(jax.random.key(seed), 5)
    state = centred(splits[0], (NLAT, NLON, FIELDS * LEVELS), 1.0, 6.0, ((0, 8), (1, 4)), jnp.float32)
    winds = jnp.clip(jax.random.uniform(splits[1], (NLAT, NLON, 2 * LEVELS), jnp.float32, -0.44921875, 0.44921875) * level_of(splits[1], (NLAT, NLON, 2 * LEVELS), ((0, 8), (1, 4)), -0.4, 0.0), -0.44921875, 0.44921875).astype(jnp.bfloat16)
    decay = jnp.clip(jnp.exp(jax.random.uniform(splits[2], (FIELDS,), jnp.float32, math.log(0.005), math.log(0.5))), 0.005, 0.5)
    widths = draw_widths(jax.random.fold_in(splits[4], 71), 0)
    return dict(state=state, winds=winds, decay=decay, widths=widths)


def smooth(rows, row_widths, decay):
    low = rows.astype(jnp.bfloat16)
    offsets = jnp.arange(NLON)
    gap = jnp.abs(offsets[:, None] - offsets[None, :])
    gap = jnp.minimum(gap, NLON - gap).astype(jnp.float32)
    first_gap = jnp.minimum(offsets, NLON - offsets).astype(jnp.float32)

    def one_row(item):
        row, width = item
        reach = width.astype(jnp.float32)
        kernel = jnp.where(gap[None] <= reach, jnp.exp(-decay[:, None, None] * gap[None]), 0.0)
        totals = jnp.sum(jnp.where(first_gap[None] <= reach, jnp.exp(-decay[:, None] * first_gap[None]), 0.0), axis=1)
        matrix = (kernel / totals[:, None, None]).astype(jnp.bfloat16)
        shaped = row.reshape(NLON, FIELDS, LEVELS).astype(jnp.float32)
        result = jnp.einsum("fij,ifl->jfl", matrix.astype(jnp.float32), shaped)
        return result.reshape(NLON, FIELDS * LEVELS).astype(jnp.bfloat16)

    return lax.map(one_row, (low, row_widths))


def advect(field, east_courant, north_courant):
    rows = field.shape[0]
    cols = field.shape[1]
    lat_ext = jnp.pad(field, ((2, 2), (0, 0), (0, 0)))
    lon_ext = jnp.concatenate([field[:, -2:], field, field[:, :2]], axis=1)
    north_one = lat_ext[3:rows + 3]
    south_one = lat_ext[1:rows + 1]
    north_two = lat_ext[4:rows + 4]
    south_two = lat_ext[0:rows]
    east_one = lon_ext[:, 3:cols + 3]
    west_one = lon_ext[:, 1:cols + 1]
    east_two = lon_ext[:, 4:cols + 4]
    west_two = lon_ext[:, 0:cols]
    first_x = (8.0 * (east_one - west_one) - (east_two - west_two)) / 12.0
    second_x = (16.0 * (east_one + west_one) - (east_two + west_two) - 30.0 * field) / 12.0
    first_y = (8.0 * (north_one - south_one) - (north_two - south_two)) / 12.0
    second_y = (16.0 * (north_one + south_one) - (north_two + south_two) - 30.0 * field) / 12.0
    return (field - east_courant * first_x + 0.5 * east_courant * east_courant * second_x
            - north_courant * first_y + 0.5 * north_courant * north_courant * second_y)


def reference(state, winds, decay, widths):
    quarter = NLAT // 4
    polar_rows = jnp.concatenate([state[:quarter], state[3 * quarter:]], axis=0)
    polar_widths = jnp.concatenate([widths[:quarter], widths[3 * quarter:]], axis=0)
    smoothed = smooth(polar_rows, polar_widths, decay).astype(jnp.float32)
    field = jnp.concatenate([smoothed[:quarter], state[quarter:3 * quarter], smoothed[quarter:]], axis=0)
    east_courant = jnp.tile(winds[:, :, :LEVELS].astype(jnp.float32), (1, 1, FIELDS))
    north_courant = jnp.tile(winds[:, :, LEVELS:].astype(jnp.float32), (1, 1, FIELDS))
    for step in range(ADV_STEPS):
        field = advect(field, east_courant, north_courant)
    return field.astype(jnp.bfloat16)
```

```python
import functools

import jax
import jax.numpy as jnp
from jax import lax
from jax.experimental import pallas as pl
from jax.experimental.pallas import tpu as pltpu
from jax.sharding import PartitionSpec as P

ADV_STEPS = 4
REACH = 2 * ADV_STEPS
ROUND = 2
HALO = 2 * ROUND
HMAX = 480
LANES = 128
PIECES = 4
VMEM_LIMIT = 56 * 1024 * 1024
PAD = 8
COLS = 48


def tie(*values):
    return lax.optimization_barrier(values)


def round_up(value, unit):
    return -(-value // unit) * unit


def smooth_kernel(geo, first, info_ref, widths_ref, own_ref, sib_ref, opp_ref, diag_ref, q_ref, carry_ref, far_ref, scale_ref,
                  extra_ref, out_ref, cells, east_sum, west_sum):
    @pl.when(info_ref[1] == 1)
    def _():
        smooth_rows(geo, first, info_ref[0] == 1, widths_ref, own_ref, sib_ref, opp_ref, diag_ref,
                    q_ref, carry_ref, far_ref, scale_ref, out_ref, cells, east_sum, west_sum)
        rows = own_ref.shape[0]
        if out_ref.shape[0] > rows:
            out_ref[rows] = extra_ref[0]


def smooth_rows(geo, first, odd, widths_ref, own_ref, sib_ref, opp_ref, diag_ref, q_ref, carry_ref, far_ref, scale_ref,
                out_ref, cells, east_sum, west_sum):
    lon, back, span, seg, ext = geo
    rows, tiles = own_ref.shape[0], own_ref.shape[2] // LANES
    chains = [(r, t) for r in range(rows) for t in range(tiles)]

    def put(ref, start, begin, count):
        @pl.loop(0, rows)
        def _(r):
            for t in range(tiles):
                part = ref[r, pl.ds(begin, count), pl.ds(t * LANES, LANES)]
                cells[r * tiles + t, pl.ds(start, count), :] = part.astype(jnp.float32)

    head = back - lon
    put(opp_ref, 0, lon - head, head)
    put(own_ref, back, 0, lon)
    put(opp_ref, back + 2 * lon, 0, span - REACH - 2 * lon)

    @pl.when(odd)
    def _():
        put(sib_ref, back - lon, 0, lon)
        put(diag_ref, back + lon, 0, lon)

    @pl.when(jnp.logical_not(odd))
    def _():
        put(diag_ref, back - lon, 0, lon)
        put(sib_ref, back + lon, 0, lon)

    q = [jnp.broadcast_to(q_ref[0:1, t * LANES:(t + 1) * LANES], (8, LANES)) for t in range(tiles)]
    jump = [carry_ref[0:1, t * LANES:(t + 1) * LANES] for t in range(tiles)]
    zero = jnp.zeros((8, LANES), jnp.float32)
    none = jnp.zeros((1, LANES), jnp.float32)
    east_base = back - REACH

    for base, total, forward in ((east_base, east_sum, False), (0, west_sum, True)):
        def at(i, forward=forward):
            return i if forward else seg - 1 - i

        def totals(i, acc, base=base):
            return tuple(cells[r * tiles + t, pl.ds(base + at(i), 8, stride=seg), :] + q[t] * acc[n]
                         for n, (r, t) in enumerate(chains))

        acc = lax.fori_loop(0, seg, totals, (zero,) * len(chains), unroll=4)
        start = []
        for n, (r, t) in enumerate(chains):
            carry = none
            parts = [None] * 8
            for k in (range(8) if forward else range(7, -1, -1)):
                parts[k] = carry
                carry = acc[n][k:k + 1] + jump[t] * carry
            start.append(jnp.concatenate(parts, axis=0))

        def sums(i, acc, base=base, total=total):
            new = []
            for n, (r, t) in enumerate(chains):
                v = cells[r * tiles + t, pl.ds(base + at(i), 8, stride=seg), :] + q[t] * acc[n]
                total[r * tiles + t, pl.ds(at(i), 8, stride=seg), :] = v
                new.append(v)
            return tuple(new)

        lax.fori_loop(0, seg, sums, tuple(start), unroll=4)

    step = COLS

    @pl.loop(0, rows)
    def _(r):
        width = widths_ref[first + r]
        for t in range(tiles):
            n = r * tiles + t
            far = jnp.broadcast_to(far_ref[r, 0:1, t * LANES:(t + 1) * LANES], (step, LANES))
            scale = jnp.broadcast_to(scale_ref[r, 0:1, t * LANES:(t + 1) * LANES], (step, LANES))
            for c in range(0, ext, step):
                near = east_sum[n, pl.ds(c, step), :] + west_sum[n, pl.ds(back - REACH + c, step), :]
                cut = east_sum[n, pl.ds(c + 1 + width, step), :] + west_sum[n, pl.ds(back - REACH + c - 1 - width, step), :]
                mid = cells[n, pl.ds(back - REACH + c, step), :]
                out_ref[r, pl.ds(c, step), pl.ds(t * LANES, LANES)] = ((near - mid - far * cut) * scale).astype(jnp.bfloat16)


def smooth_chunk(first, rows, ext, info, widths, own, sib, opp, diag, q, carry, far, scale, extra):
    lon, channels = own.shape[1:]
    tiles = channels // LANES
    back = round_up(HMAX + 1 + REACH, 8)
    span = round_up(ext + HMAX + 1, 8)
    seg = max(back + ext - REACH, span) // 8
    geo = (lon, back, 8 * seg, seg, ext)
    more = 0 if extra is None else 1
    if extra is None:
        extra = jnp.zeros((1, ext, channels), jnp.bfloat16)
    smem, vmem = pl.BlockSpec(memory_space=pltpu.SMEM), pl.BlockSpec(memory_space=pltpu.VMEM)
    part = pl.BlockSpec((rows, lon, channels), lambda i: (first // rows, 0, 0))
    table = pl.BlockSpec((rows, 1, channels), lambda i: (first // rows, 0, 0))
    return pl.pallas_call(
        functools.partial(smooth_kernel, geo, first),
        grid=(1,),
        in_specs=[smem, smem, vmem, part, vmem, vmem, vmem, vmem, table, table, vmem],
        out_specs=pl.BlockSpec((rows + more, ext, channels), lambda i: (0, 0, 0)),
        out_shape=jax.ShapeDtypeStruct((rows + more, ext, channels), jnp.bfloat16),
        scratch_shapes=[
            pltpu.VMEM((rows * tiles, back - REACH + 8 * seg, LANES), jnp.float32),
            pltpu.VMEM((rows * tiles, 8 * seg, LANES), jnp.float32),
            pltpu.VMEM((rows * tiles, 8 * seg, LANES), jnp.float32),
        ],
        compiler_params=pltpu.CompilerParams(vmem_limit_bytes=VMEM_LIMIT),
        cost_estimate=pl.CostEstimate(flops=1000, bytes_accessed=1000, transcendentals=0),
        name="smooth",
    )(info, widths, own, sib, opp, diag, q, carry, far, scale, extra)


def update(src, r, t, c, count, u, v, zero):
    def at(dr, dc):
        return src[r + dr, t, pl.ds(PAD + c + dc + (zero if dc else 0), count), :]

    mid = at(0, 0)
    mid30 = 30.0 * mid
    e1, w1, e2, w2 = at(0, 1), at(0, -1), at(0, 2), at(0, -2)
    n1, s1, n2, s2 = at(1, 0), at(-1, 0), at(2, 0), at(-2, 0)
    first_x = (e2 - w2) - 8.0 * (e1 - w1)
    second_x = 16.0 * (e1 + w1) - (e2 + w2) - mid30
    first_y = (n2 - s2) - 8.0 * (n1 - s1)
    second_y = 16.0 * (n1 + s1) - (n2 + s2) - mid30
    change = u * (first_x + (6.0 * u) * second_x) + v * (first_y + (6.0 * v) * second_y)
    return mid + change


def put_rows(field, ref, base, count, ext):
    @pl.loop(0, count)
    def _(r):
        for t in range(field.shape[1]):
            field[base + r, t, pl.ds(PAD, ext), :] = ref[r, :, pl.ds(t * LANES, LANES)].astype(jnp.float32)


def step_rows(source, winds, zero, first, last, offset, start, stop, store):
    @pl.loop(first, last)
    def _(r):
        for c in range(start, stop, COLS):
            count = min(COLS, stop - c)
            u = winds[r + offset, pl.ds(c, count), pl.ds(0, LANES)].astype(jnp.float32) * (1.0 / 12.0)
            v = winds[r + offset, pl.ds(c, count), pl.ds(LANES, LANES)].astype(jnp.float32) * (1.0 / 12.0)
            for t in range(source.shape[1]):
                store(r, t, c, count, update(source, r + 2, t, c, count, u, v, zero))


class Copies:
    def __init__(self, sems):
        self.sems, self.used = sems, 0

    def start(self, source, target):
        copy = pltpu.make_async_copy(source, target, self.sems.at[self.used])
        self.used += 1
        copy.start()
        return copy

    def either(self, flag, source, other, target):
        sem = self.sems.at[self.used]
        self.used += 1

        @pl.when(flag)
        def _():
            pltpu.make_async_copy(source, target, sem).start()

        @pl.when(jnp.logical_not(flag))
        def _():
            pltpu.make_async_copy(other, target, sem).start()

        return pltpu.make_async_copy(source, target, sem)


def store_in(field):
    def store(r, t, c, count, value):
        field[r, t, pl.ds(PAD + c, count), :] = value

    return store


def store_out(ref):
    def store(r, t, c, count, value):
        ref[r, pl.ds(c - REACH, count), pl.ds(t * LANES, LANES)] = value.astype(jnp.bfloat16)

    return store


def start_own_rows(geo, polar, state_ref, smooth_refs, staged, field, base, first, count, sems):
    lon, part = geo[0], count // len(smooth_refs)

    @pl.when(polar)
    def _():
        for i, ref in enumerate(smooth_refs):
            pltpu.make_async_copy(ref.at[pl.ds(0, part)], staged.at[pl.ds(i * part, part)], sems.at[i]).start()

    @pl.when(jnp.logical_not(polar))
    def _():
        for t in range(field.shape[1]):
            pltpu.make_async_copy(
                state_ref.at[pl.ds(first, count), :, pl.ds(t * LANES, LANES)],
                field.at[pl.ds(base, count), t, pl.ds(PAD + REACH, lon), :], sems.at[t]).start()


def finish_own_rows(geo, polar, state_ref, edge_w_ref, edge_e_ref, smooth_refs, staged, field, base, first, count, sems):
    lon, ext = geo
    part = count // len(smooth_refs)

    @pl.when(polar)
    def _():
        for i, ref in enumerate(smooth_refs):
            pltpu.make_async_copy(ref.at[pl.ds(0, part)], staged.at[pl.ds(i * part, part)], sems.at[i]).wait()
            put_rows(field, staged.at[pl.ds(i * part, part)], base + i * part, part, ext)

    @pl.when(jnp.logical_not(polar))
    def _():
        @pl.loop(0, count)
        def _(r):
            for t in range(field.shape[1]):
                lanes = pl.ds(t * LANES, LANES)
                field[base + r, t, pl.ds(PAD, REACH), :] = edge_w_ref[first + r, :, lanes].astype(jnp.float32)
                field[base + r, t, pl.ds(PAD + REACH + lon, REACH), :] = edge_e_ref[first + r, :, lanes].astype(jnp.float32)

        for t in range(field.shape[1]):
            pltpu.make_async_copy(
                state_ref.at[pl.ds(first, count), :, pl.ds(t * LANES, LANES)],
                field.at[pl.ds(base, count), t, pl.ds(PAD + REACH, lon), :], sems.at[t]).wait()


def border_kernel(north, rows, lon, ext, info_ref, state_ref, edge_w_ref, edge_e_ref, winds_ref, beyond_ref, raw_ref, late_ref,
                  smooth_a_ref, smooth_b_ref, border_ref, level_ref, field_a, field_b, halo_rows, staged, winds, own_sem, sems):
    halo, own, first = (2 * HALO, 0, rows - 2 * HALO) if north else (0, HALO, 0)
    polar, zero = info_ref[1] == 1, info_ref[4]
    smooth_refs = smooth_a_ref, smooth_b_ref
    copies = Copies(sems)
    start_own_rows((lon, ext), polar, state_ref, smooth_refs, staged, field_a, own, first, 2 * HALO, own_sem)
    halo_copy = copies.either(info_ref[3 if north else 2] == 1, late_ref.at[pl.ds(0, HALO)], raw_ref.at[pl.ds(0, HALO)], halo_rows)
    wind_copies = [
        copies.start(winds_ref.at[pl.ds(first + 2 if north else 0, HALO + 2)], winds.at[pl.ds(0 if north else 2, HALO + 2)]),
        copies.start(beyond_ref, winds.at[pl.ds(HALO + 2 if north else 0, 2)]),
    ]
    finish_own_rows((lon, ext), polar, state_ref, edge_w_ref, edge_e_ref, smooth_refs, staged, field_a, own, first, 2 * HALO,
                    own_sem)
    halo_copy.wait()
    put_rows(field_a, halo_rows, halo, HALO, ext)
    for copy in wind_copies:
        copy.wait()
    step_rows(field_a, winds, zero, 0, 2 * HALO, 0, 0, ext, store_in(field_b))

    def store(r, t, c, count, value):
        level_ref[r, t, pl.ds(c, count), :] = value
        border_ref[r, pl.ds(c, count), pl.ds(t * LANES, LANES)] = value.astype(jnp.bfloat16)

    step_rows(field_b, winds, zero, 0, HALO, 2, 0, ext, store)


def border_rows(north, info, state, edges, winds, beyond, raw, late, smooths):
    rows, lon, channels = state.shape
    ext = winds.shape[1]
    tiles = channels // LANES
    vmem, hbm = pl.BlockSpec(memory_space=pltpu.VMEM), pl.BlockSpec(memory_space=pl.ANY)
    operands = [info, state, *edges, winds, beyond, raw, late, *smooths]
    return pl.pallas_call(
        functools.partial(border_kernel, north, rows, lon, ext),
        in_specs=[pl.BlockSpec(memory_space=pltpu.SMEM), hbm, vmem, vmem] + [hbm] * (len(operands) - 4),
        out_specs=[vmem, vmem],
        out_shape=[jax.ShapeDtypeStruct((HALO, ext, channels), jnp.bfloat16),
                   jax.ShapeDtypeStruct((HALO, tiles, ext, LANES), jnp.float32)],
        scratch_shapes=[
            cells_of(3 * HALO, tiles, ext), cells_of(2 * HALO, tiles, ext),
            half_of(HALO, ext, channels), half_of(2 * HALO, ext, channels), half_of(2 * HALO, ext, channels),
            pltpu.SemaphoreType.DMA((2,)), pltpu.SemaphoreType.DMA((3,)),
        ],
        compiler_params=pltpu.CompilerParams(vmem_limit_bytes=VMEM_LIMIT),
        cost_estimate=pl.CostEstimate(flops=1000, bytes_accessed=1000, transcendentals=0),
        name="border_north" if north else "border_south",
    )(*operands)


def interior_kernel(rows, lon, ext, info_ref, state_ref, edge_w_ref, edge_e_ref, winds_ref, level_s_ref, level_n_ref, *rest):
    smooth_refs, rest = rest[:PIECES], rest[PIECES:]
    out_ref, third_s_ref, third_n_ref, field_a, field_b, field_c, part_ref, staged, winds, sem, in_sem, out_sem = rest
    inner = rows - 4
    polar, zero = info_ref[1] == 1, info_ref[4]
    copies = Copies(in_sem)
    start_own_rows((lon, ext), polar, state_ref, smooth_refs, staged, field_a, 0, 0, rows, sem)
    wind_copy = copies.start(winds_ref.at[pl.ds(2, inner)], winds)

    def strip(field, base):
        return field.at[pl.ds(base, HALO), :, pl.ds(PAD, ext), :]

    incoming = [copies.start(ref, strip(field_c, base)) for ref, base in ((level_s_ref, 0), (level_n_ref, rows - HALO))]
    finish_own_rows((lon, ext), polar, state_ref, edge_w_ref, edge_e_ref, smooth_refs, staged, field_a, 0, 0, rows, sem)
    wind_copy.wait()
    step_rows(field_a, winds, zero, 0, inner, 0, 0, ext, store_in(field_b))

    def store(r, t, c, count, value):
        field_c[HALO + r, t, pl.ds(PAD + c, count), :] = value

    step_rows(field_b, winds, zero, 0, inner - 4, 2, 0, ext, store)
    for copy in incoming:
        copy.wait()
    step_rows(field_c, winds, zero, 0, inner, 0, 0, ext, store_in(field_b))
    outgoing = [pltpu.make_async_copy(strip(field_b, base), ref, out_sem.at[i])
                for i, (ref, base) in enumerate(((third_s_ref, 0), (third_n_ref, inner - HALO)))]
    for copy in outgoing:
        copy.start()
    step_rows(field_b, winds, zero, 0, inner - 4, 2, REACH, REACH + lon, store_out(part_ref))
    outgoing.append(pltpu.make_async_copy(part_ref, out_ref.at[pl.ds(HALO, rows - 2 * HALO)], out_sem.at[2]))
    outgoing[2].start()
    for copy in outgoing:
        copy.wait()


def interior(info, state, edges, winds, levels, smooths):
    rows, lon, channels = state.shape
    ext = winds.shape[1]
    tiles = channels // LANES
    vmem, hbm = pl.BlockSpec(memory_space=pltpu.VMEM), pl.BlockSpec(memory_space=pl.ANY)
    third = jax.ShapeDtypeStruct((HALO, tiles, ext, LANES), jnp.float32)
    return pl.pallas_call(
        functools.partial(interior_kernel, rows, lon, ext),
        in_specs=[pl.BlockSpec(memory_space=pltpu.SMEM), hbm, vmem, vmem] + [hbm] * (3 + len(smooths)),
        out_specs=[hbm, hbm, hbm],
        out_shape=[jax.ShapeDtypeStruct((rows, lon, channels), jnp.bfloat16), third, third],
        scratch_shapes=[
            cells_of(rows, tiles, ext), cells_of(rows - 4, tiles, ext), cells_of(rows, tiles, ext),
            half_of(rows - 2 * HALO, lon, channels), half_of(rows, ext, channels), half_of(rows - 4, ext, channels),
            pltpu.SemaphoreType.DMA((len(smooths),)), pltpu.SemaphoreType.DMA((3,)), pltpu.SemaphoreType.DMA((3,)),
        ],
        compiler_params=pltpu.CompilerParams(vmem_limit_bytes=VMEM_LIMIT),
        cost_estimate=pl.CostEstimate(flops=1000, bytes_accessed=1000, transcendentals=0),
        name="interior",
    )(info, state, *edges, winds, *levels, *smooths)


def finish_kernel(rows, lon, ext, _, info_ref, winds_ref, *rest):
    sides, (out_ref, field_a, field_b, winds, halo_rows, part_ref, in_sem, out_sem) = rest[:8], rest[8:]
    zero = info_ref[4]
    incoming, outgoing = [], []
    copies = Copies(in_sem)
    for side in range(2):
        beyond_ref, border_ref, level_ref, third_ref = sides[4 * side:4 * side + 4]
        mine, other = (0, HALO) if side else (HALO, 0)
        wind = winds.at[side]
        incoming.append([
            copies.start(border_ref, halo_rows.at[side]),
            copies.start(level_ref, field_a.at[side, pl.ds(mine, HALO), :, pl.ds(PAD, ext), :]),
            copies.start(third_ref, field_b.at[side, pl.ds(mine, HALO), :, pl.ds(PAD, ext), :]),
            copies.start(winds_ref.at[pl.ds(rows - HALO if side else 0, HALO)], wind.at[pl.ds(0 if side else 2, HALO)]),
            copies.start(beyond_ref, wind.at[pl.ds(HALO if side else 0, 2)]),
        ])
    for side in range(2):
        near, last, wind = field_a.at[side], field_b.at[side], winds.at[side]
        mine, other = (0, HALO) if side else (HALO, 0)
        incoming[side][0].wait()
        put_rows(near, halo_rows.at[side], other, HALO, ext)
        for copy in incoming[side][1:]:
            copy.wait()

        def store(r, t, c, count, value, last=last, base=other):
            last[r + base, t, pl.ds(PAD + c, count), :] = value

        step_rows(near, wind, zero, 0, HALO, 2 if side else 0, 0, ext, store)
        step_rows(last, wind, zero, 0, HALO, 0 if side else 2, REACH, REACH + lon, store_out(part_ref.at[side]))
        place = out_ref.at[pl.ds(rows - HALO if side else 0, HALO)]
        outgoing.append(pltpu.make_async_copy(part_ref.at[side], place, out_sem.at[side]))
        outgoing[-1].start()
    for copy in outgoing:
        copy.wait()


def finish(info, out, winds, south, north):
    rows, lon, channels = out.shape
    ext = winds.shape[1]
    tiles = channels // LANES
    hbm = pl.BlockSpec(memory_space=pl.ANY)
    side = pltpu.VMEM((2, 2 * HALO, tiles, ext + 2 * PAD, LANES), jnp.float32)
    return pl.pallas_call(
        functools.partial(finish_kernel, rows, lon, ext),
        in_specs=[hbm, pl.BlockSpec(memory_space=pltpu.SMEM)] + [hbm] * 9,
        out_specs=hbm,
        out_shape=jax.ShapeDtypeStruct(out.shape, out.dtype),
        input_output_aliases={0: 0},
        scratch_shapes=[
            side, side,
            pltpu.VMEM((2, HALO + 2, ext, channels), jnp.bfloat16),
            pltpu.VMEM((2, HALO, ext, channels), jnp.bfloat16),
            pltpu.VMEM((2, HALO, lon, channels), jnp.bfloat16),
            pltpu.SemaphoreType.DMA((10,)),
            pltpu.SemaphoreType.DMA((2,)),
        ],
        compiler_params=pltpu.CompilerParams(vmem_limit_bytes=VMEM_LIMIT),
        cost_estimate=pl.CostEstimate(flops=1000, bytes_accessed=1000, transcendentals=0),
        name="finish",
    )(out, info, winds, *south, *north)


def half_of(rows, ext, channels):
    return pltpu.VMEM((rows, ext, channels), jnp.bfloat16)


def cells_of(rows, tiles, ext):
    return pltpu.VMEM((rows, tiles, ext + 2 * PAD, LANES), jnp.float32)


def per_device(state, winds, decay, widths):
    rows, lon, channels = state.shape
    fields = decay.shape[0]
    bands, tiles = lax.axis_size("lat"), lax.axis_size("lon")
    lat, lon_at = lax.axis_index("lat"), lax.axis_index("lon")
    quarter = bands // 4
    ext = round_up(lon + 2 * REACH, 16)
    fill = ext - lon - 2 * REACH
    axes = ("lat", "lon")

    def is_polar(band):
        return band < quarter or band >= bands - quarter

    def polar_at(band):
        return ((band >= 0) & (band < quarter)) | ((band >= bands - quarter) & (band < bands))

    info = jnp.stack([lon_at % 2, polar_at(lat), polar_at(lat - 1), polar_at(lat + 1), lat < 0]).astype(jnp.int32)

    def over_lon(flip):
        return [(b * tiles + l, b * tiles + (l ^ flip)) for b in range(bands) if is_polar(b) for l in range(tiles)]

    def over_lat(shift, wanted=lambda band: True):
        return [(b * tiles + l, (b + shift) * tiles + l)
                for b in range(bands) if 0 <= b + shift < bands and wanted(b) for l in range(tiles)]

    def move(cells, pairs):
        return lax.ppermute(cells, axes, pairs)

    count = rows // PIECES
    circle_rows = [0, rows - count, count, rows - 2 * count]

    def joined(cols):
        return jnp.concatenate([state[:, cols].astype(jnp.bfloat16), winds[:, cols]], axis=2)

    east = [(l, (l + 1) % tiles) for l in range(tiles)]
    west = [((l + 1) % tiles, l) for l in range(tiles)]
    head, rear, cells = tie(joined(slice(0, REACH)), joined(slice(lon - REACH, lon)), state)
    from_east = lax.ppermute(head, "lon", west)
    from_west = lax.ppermute(rear, "lon", east)

    def piece(first):
        return lax.slice_in_dim(cells, first, first + count).astype(jnp.bfloat16)

    opp, late, smooths = [None] * PIECES, [None] * 2, {}
    circles = [piece(circle_rows[0])]
    circles[0], cells = tie(circles[0], cells)
    opp[0] = move(circles[0], over_lon(2))
    circles += [piece(f) for f in circle_rows[1:]]
    edge_w, edge_e = from_west[:, :, :channels], from_east[:, :, :channels]

    def extend(inner, before, after):
        parts = [before, inner, after, jnp.zeros((inner.shape[0], fill, inner.shape[2]), inner.dtype)]
        return jnp.concatenate(parts, axis=1)

    winds_ext = extend(winds, from_west[:, :, channels:], from_east[:, :, channels:])

    def border(first, wind_first):
        of = slice(first, first + HALO)
        wind = [winds_ext[wind_first + i:wind_first + i + 1] for i in range(2)]
        ends = extend(cells[of].astype(jnp.bfloat16), edge_w[of], edge_e[of])
        return jnp.concatenate([ends, jnp.concatenate(wind, axis=2)], axis=0)

    def is_plain(band):
        return not is_polar(band)

    north_rows, south_rows = border(rows - HALO, rows - 2), border(0, 0)
    raw_s = move(north_rows, over_lat(1, is_plain))
    raw_n = move(south_rows, over_lat(-1, is_plain))
    behind = (south_rows[HALO:], north_rows[HALO:], None, None)

    def spread(wind):
        half = wind.shape[-1] // 2
        return jnp.concatenate([wind[..., :half]] * 2 + [wind[..., half:]] * 2, axis=-1)

    winds_all = spread(winds_ext)

    def beyond(is_late, late_rows, raw_rows):
        both = jnp.where(is_late, late_rows[HALO], raw_rows[HALO])
        return spread(jnp.stack([both[:, :LANES], both[:, LANES:]]))

    sib = move(cells.astype(jnp.bfloat16), over_lon(1))
    circles[1], winds_ext = tie(circles[1], winds_ext)
    opp[1] = move(circles[1], over_lon(2))

    own_widths = lax.dynamic_slice_in_dim(widths, lat * rows, rows)
    rate = jnp.repeat(decay, channels // fields)[None, :]
    reach = own_widths.astype(jnp.float32)[:, None]
    q = jnp.exp(-rate)
    back = round_up(HMAX + 1 + REACH, 8)
    seg = max(back + ext - REACH, round_up(ext + HMAX + 1, 8)) // 8
    carry = jnp.exp(-rate * seg)
    far = jnp.exp(-rate * (reach + 1.0))[:, None, :]
    total = (-jnp.expm1(-rate * (reach + 1.0)) - q * jnp.expm1(-rate * reach)) / -jnp.expm1(-rate)
    scale = (1.0 / total)[:, None, :]

    edges = edge_w, edge_e
    for i, f in enumerate(circle_rows):
        if i == 1:
            opp[i], raw_n, winds_all = tie(opp[i], raw_n, winds_all)
        if i == 2:
            opp[i], late[0], raw_s = tie(opp[i], late[0], raw_s)
        if i == 3:
            opp[i], late[1] = tie(opp[i], late[1])
        if i + 2 < PIECES:
            opp[i], circles[i + 2] = tie(opp[i], circles[i + 2])
            opp[i + 2] = move(circles[i + 2], over_lon(2))
        diag = move(opp[i], over_lon(1))
        smooth = smooth_chunk(f, count, ext, info, own_widths, circles[i], sib, opp[i], diag,
                              q, carry, far, scale, behind[i])
        smooths[f] = smooth
        if i + 1 < PIECES:
            smooth, opp[i + 1] = tie(smooth, opp[i + 1])
        if i < 2:
            late[i] = move(smooths[f], over_lat((-1, 1)[i], is_polar))
        if i == 2:
            wind_s = beyond(polar_at(lat - 1), late[1], raw_s)
            low_rows, level_s = border_rows(False, info, state, edges, winds_all, wind_s, raw_s, late[1],
                                            (smooths[0], smooths[f]))
            to_south = move(low_rows, over_lat(-1))

    smooths = [smooths[f] for f in sorted(smooths)]
    wind_n = beyond(polar_at(lat + 1), late[0], raw_n)
    top_rows, level_n = border_rows(True, info, state, edges, winds_all, wind_n, raw_n, late[0], smooths[2:])
    to_north = move(top_rows, over_lat(1))
    level_s, to_south, level_n = tie(level_s, to_south, level_n)
    out, third_s, third_n = interior(info, state, edges, winds_all, (level_s, level_n), smooths)
    return finish(info, out, winds_all, (wind_s, to_north, level_s, third_s), (wind_n, to_south, level_n, third_n))


def solution(mesh):
    in_specs = (P("lat", "lon", None), P("lat", "lon", None), P(), P())
    out_specs = P("lat", "lon", None)
    return jax.shard_map(
        per_device, mesh=mesh, in_specs=in_specs, out_specs=out_specs, check_vma=False
    )
```

```python
import functools

import jax
import jax.numpy as jnp
from jax import lax
from jax.experimental import pallas as pl
from jax.experimental.pallas import tpu as pltpu
from jax.sharding import PartitionSpec as P

ADV_STEPS = 4
REACH = 2 * ADV_STEPS
ROUND = 2
HALO = 2 * ROUND
HMAX = 480
LANES = 128
VMEM_LIMIT = 56 * 1024 * 1024
PAD = 8
COLS = 48


def tie(*values):
    return lax.optimization_barrier(values)


def round_up(value, unit):
    return -(-value // unit) * unit


def smooth_kernel(geo, sends, info_ref, widths_ref, *refs):
    ins, extra_refs, outs, scratch = refs[:8], refs[8:8 + sends], refs[8 + sends:9 + 2 * sends], refs[9 + 2 * sends:]

    @pl.when(info_ref[1] == 1)
    def _():
        smooth_rows(geo, info_ref[0] == 1, widths_ref, *ins, *outs[:1], outs[1:], *scratch)
        for ref, extra_ref in zip(outs[1:], extra_refs):
            ref[HALO] = extra_ref[0]


def smooth_rows(geo, odd, widths_ref, own_ref, sib_ref, opp_ref, diag_ref, q_ref, carry_ref, far_ref, scale_ref,
                level_ref, border_refs, cells, east_sum, west_sum):
    lon, back, span, seg, ext = geo
    rows, tiles = own_ref.shape[0], own_ref.shape[2] // LANES
    chains = [(r, t) for r in range(rows) for t in range(tiles)]

    def put(ref, start, begin, count):
        @pl.loop(0, rows)
        def _(r):
            for t in range(tiles):
                part = ref[r, pl.ds(begin, count), pl.ds(t * LANES, LANES)]
                cells[r * tiles + t, pl.ds(start, count), :] = part.astype(jnp.float32)

    head = back - lon
    put(opp_ref, 0, lon - head, head)
    put(own_ref, back, 0, lon)
    put(opp_ref, back + 2 * lon, 0, span - REACH - 2 * lon)

    @pl.when(odd)
    def _():
        put(sib_ref, back - lon, 0, lon)
        put(diag_ref, back + lon, 0, lon)

    @pl.when(jnp.logical_not(odd))
    def _():
        put(diag_ref, back - lon, 0, lon)
        put(sib_ref, back + lon, 0, lon)

    q = [jnp.broadcast_to(q_ref[0:1, t * LANES:(t + 1) * LANES], (8, LANES)) for t in range(tiles)]
    jump = [carry_ref[0:1, t * LANES:(t + 1) * LANES] for t in range(tiles)]
    zero = jnp.zeros((8, LANES), jnp.float32)
    none = jnp.zeros((1, LANES), jnp.float32)
    east_base = back - REACH

    for base, total, forward in ((east_base, east_sum, False), (0, west_sum, True)):
        def at(i, forward=forward):
            return i if forward else seg - 1 - i

        def totals(i, acc, base=base):
            return tuple(cells[r * tiles + t, pl.ds(base + at(i), 8, stride=seg), :] + q[t] * acc[n]
                         for n, (r, t) in enumerate(chains))

        acc = lax.fori_loop(0, seg, totals, (zero,) * len(chains), unroll=4)
        start = []
        for n, (r, t) in enumerate(chains):
            carry = none
            parts = [None] * 8
            for k in (range(8) if forward else range(7, -1, -1)):
                parts[k] = carry
                carry = acc[n][k:k + 1] + jump[t] * carry
            start.append(jnp.concatenate(parts, axis=0))

        def sums(i, acc, base=base, total=total):
            new = []
            for n, (r, t) in enumerate(chains):
                v = cells[r * tiles + t, pl.ds(base + at(i), 8, stride=seg), :] + q[t] * acc[n]
                total[r * tiles + t, pl.ds(at(i), 8, stride=seg), :] = v
                new.append(v)
            return tuple(new)

        lax.fori_loop(0, seg, sums, tuple(start), unroll=4)

    step = COLS

    def one_row(r, border_ref, border_row):
        width = widths_ref[r]
        for t in range(tiles):
            n = r * tiles + t
            far = jnp.broadcast_to(far_ref[r, 0:1, t * LANES:(t + 1) * LANES], (step, LANES))
            scale = jnp.broadcast_to(scale_ref[r, 0:1, t * LANES:(t + 1) * LANES], (step, LANES))
            for c in range(0, ext, step):
                near = east_sum[n, pl.ds(c, step), :] + west_sum[n, pl.ds(back - REACH + c, step), :]
                cut = east_sum[n, pl.ds(c + 1 + width, step), :] + west_sum[n, pl.ds(back - REACH + c - 1 - width, step), :]
                mid = cells[n, pl.ds(back - REACH + c, step), :]
                value = ((near - mid - far * cut) * scale).astype(jnp.bfloat16)
                level_ref[r, t, pl.ds(c, step), :] = value.astype(jnp.float32)
                if border_ref is not None:
                    border_ref[border_row, pl.ds(c, step), pl.ds(t * LANES, LANES)] = value

    if border_refs:
        for i, ref in enumerate(border_refs):
            @pl.loop(0, HALO)
            def _(r, i=i, ref=ref):
                one_row(i * HALO + r, ref, r)
    else:
        @pl.loop(0, rows)
        def _(r):
            one_row(r, None, None)


def smooth_piece(first, rows, ext, info, widths, own, sib, opp, diag, q, carry, far, scale, extras):
    lon, channels = own.shape[1:]
    tiles = channels // LANES
    back = round_up(HMAX + 1 + REACH, 8)
    span = round_up(ext + HMAX + 1, 8)
    seg = max(back + ext - REACH, span) // 8
    geo = (lon, back, 8 * seg, seg, ext)
    smem, vmem = pl.BlockSpec(memory_space=pltpu.SMEM), pl.BlockSpec(memory_space=pltpu.VMEM)
    part = pl.BlockSpec((rows, lon, channels), lambda i: (first // rows, 0, 0))
    table = pl.BlockSpec((rows, 1, channels), lambda i: (first // rows, 0, 0))
    border = jax.ShapeDtypeStruct((HALO + 1, ext, channels), jnp.bfloat16)
    of_rows = slice(first, first + rows)
    return pl.pallas_call(
        functools.partial(smooth_kernel, geo, len(extras)),
        grid=(1,),
        in_specs=[smem, smem, vmem, part, vmem, vmem, vmem, vmem, table, table] + [vmem] * len(extras),
        out_specs=[vmem] * (1 + len(extras)),
        out_shape=[jax.ShapeDtypeStruct((rows, tiles, ext, LANES), jnp.float32)] + [border] * len(extras),
        scratch_shapes=[
            pltpu.VMEM((rows * tiles, back - REACH + 8 * seg, LANES), jnp.float32),
            pltpu.VMEM((rows * tiles, 8 * seg, LANES), jnp.float32),
            pltpu.VMEM((rows * tiles, 8 * seg, LANES), jnp.float32),
        ],
        compiler_params=pltpu.CompilerParams(vmem_limit_bytes=VMEM_LIMIT),
        cost_estimate=pl.CostEstimate(flops=1000, bytes_accessed=1000, transcendentals=0),
        name="smooth",
    )(info, widths[of_rows], own, sib, opp, diag, q, carry, far, scale, *extras)


def update(src, r, t, c, count, u, v, zero):
    def at(dr, dc):
        return src[r + dr, t, pl.ds(PAD + c + dc + (zero if dc else 0), count), :]

    mid = at(0, 0)
    mid30 = 30.0 * mid
    e1, w1, e2, w2 = at(0, 1), at(0, -1), at(0, 2), at(0, -2)
    n1, s1, n2, s2 = at(1, 0), at(-1, 0), at(2, 0), at(-2, 0)
    first_x = (e2 - w2) - 8.0 * (e1 - w1)
    second_x = 16.0 * (e1 + w1) - (e2 + w2) - mid30
    first_y = (n2 - s2) - 8.0 * (n1 - s1)
    second_y = 16.0 * (n1 + s1) - (n2 + s2) - mid30
    change = u * (first_x + (6.0 * u) * second_x) + v * (first_y + (6.0 * v) * second_y)
    return mid + change


def put_rows(field, ref, base, count, ext):
    @pl.loop(0, count)
    def _(r):
        for t in range(field.shape[1]):
            field[base + r, t, pl.ds(PAD, ext), :] = ref[r, :, pl.ds(t * LANES, LANES)].astype(jnp.float32)


def step_rows(source, winds, zero, first, last, offset, start, stop, store):
    @pl.loop(first, last)
    def _(r):
        for c in range(start, stop, COLS):
            count = min(COLS, stop - c)
            u = winds[r + offset, pl.ds(c, count), pl.ds(0, LANES)].astype(jnp.float32) * (1.0 / 12.0)
            v = winds[r + offset, pl.ds(c, count), pl.ds(LANES, LANES)].astype(jnp.float32) * (1.0 / 12.0)
            for t in range(source.shape[1]):
                store(r, t, c, count, update(source, r + 2, t, c, count, u, v, zero))


class Copies:
    def __init__(self, sems):
        self.sems, self.used = sems, 0

    def start(self, source, target):
        copy = pltpu.make_async_copy(source, target, self.sems.at[self.used])
        self.used += 1
        copy.start()
        return copy

    def either(self, flag, source, other, target):
        sem = self.sems.at[self.used]
        self.used += 1

        @pl.when(flag)
        def _():
            pltpu.make_async_copy(source, target, sem).start()

        @pl.when(jnp.logical_not(flag))
        def _():
            pltpu.make_async_copy(other, target, sem).start()

        return pltpu.make_async_copy(source, target, sem)


def store_in(field):
    def store(r, t, c, count, value):
        field[r, t, pl.ds(PAD + c, count), :] = value

    return store


def store_out(ref):
    def store(r, t, c, count, value):
        ref[r, pl.ds(c - REACH, count), pl.ds(t * LANES, LANES)] = value.astype(jnp.bfloat16)

    return store


class OwnRows:
    def __init__(self, polar, lon, ext, state_ref, edge_w_ref, edge_e_ref, parts, field, base, first, sems):
        tiles, count = field.shape[1], HALO * len(parts)
        self.polar, self.edges = polar, (edge_w_ref, edge_e_ref)
        self.place = (field, base, first, count, lon)
        self.smooth, self.plain = [], []
        for i, (ref, start) in enumerate(parts):
            target = field.at[pl.ds(base + i * HALO, HALO), :, pl.ds(PAD, ext), :]
            self.smooth.append(pltpu.make_async_copy(ref.at[pl.ds(start, HALO)], target, sems.at[i]))
        for t in range(tiles):
            self.plain.append(pltpu.make_async_copy(
                state_ref.at[pl.ds(first, count), :, pl.ds(t * LANES, LANES)],
                field.at[pl.ds(base, count), t, pl.ds(PAD + REACH, lon), :], sems.at[t]))
        self.each(lambda copy: copy.start())

    def each(self, act):
        @pl.when(self.polar)
        def _():
            for copy in self.smooth:
                act(copy)

        @pl.when(jnp.logical_not(self.polar))
        def _():
            for copy in self.plain:
                act(copy)

    def wait(self):
        field, base, first, count, lon = self.place
        edge_w_ref, edge_e_ref = self.edges

        @pl.when(jnp.logical_not(self.polar))
        def _():
            @pl.loop(0, count)
            def _(r):
                for t in range(field.shape[1]):
                    lanes = pl.ds(t * LANES, LANES)
                    field[base + r, t, pl.ds(PAD, REACH), :] = edge_w_ref[first + r, :, lanes].astype(jnp.float32)
                    field[base + r, t, pl.ds(PAD + REACH + lon, REACH), :] = edge_e_ref[first + r, :, lanes].astype(jnp.float32)

        self.each(lambda copy: copy.wait())


def strip(field, base, ext):
    return field.at[pl.ds(base, HALO), :, pl.ds(PAD, ext), :]


def border_kernel(north, rows, lon, ext, info_ref, state_ref, edge_w_ref, edge_e_ref, winds_ref, beyond_ref, raw_ref, late_ref,
                  smooth_a_ref, smooth_b_ref, border_ref, level_ref, one_ref, field_a, field_b, halo_rows, winds, own_sem, sems):
    halo, own, first = (2 * HALO, 0, rows - 2 * HALO) if north else (0, HALO, 0)
    zero = info_ref[4]
    parts = ((smooth_b_ref, 0), (smooth_a_ref, HALO)) if north else ((smooth_a_ref, 0), (smooth_b_ref, 0))
    copies = Copies(sems)
    halo_copy = copies.either(info_ref[3 if north else 2] == 1, late_ref.at[pl.ds(0, HALO)], raw_ref.at[pl.ds(0, HALO)], halo_rows)
    mine = OwnRows(info_ref[1] == 1, lon, ext, state_ref, edge_w_ref, edge_e_ref, parts, field_a, own, first, own_sem)
    wind_copies = [
        copies.start(winds_ref.at[pl.ds(first + 2 if north else 0, HALO + 2)], winds.at[pl.ds(0 if north else 2, HALO + 2)]),
        copies.start(beyond_ref, winds.at[pl.ds(HALO + 2 if north else 0, 2)]),
    ]
    halo_copy.wait()
    put_rows(field_a, halo_rows, halo, HALO, ext)
    mine.wait()
    for copy in wind_copies:
        copy.wait()
    step_rows(field_a, winds, zero, 0, 2 * HALO, 0, 0, ext, store_in(field_b))
    one_copy = copies.start(strip(field_b, 0 if north else HALO, ext), one_ref)

    def store(r, t, c, count, value):
        level_ref[r, t, pl.ds(c, count), :] = value
        border_ref[r, pl.ds(c, count), pl.ds(t * LANES, LANES)] = value.astype(jnp.bfloat16)

    step_rows(field_b, winds, zero, 0, HALO, 2, 0, ext, store)
    one_copy.wait()


def border_rows(north, info, state, edges, winds, beyond, raw, late, smooths):
    rows, lon, channels = state.shape
    ext = winds.shape[1]
    tiles = channels // LANES
    vmem, hbm = pl.BlockSpec(memory_space=pltpu.VMEM), pl.BlockSpec(memory_space=pl.ANY)
    level = jax.ShapeDtypeStruct((HALO, tiles, ext, LANES), jnp.float32)
    return pl.pallas_call(
        functools.partial(border_kernel, north, rows, lon, ext),
        in_specs=[pl.BlockSpec(memory_space=pltpu.SMEM), hbm, vmem, vmem] + [hbm] * 6,
        out_specs=[vmem, vmem, hbm],
        out_shape=[jax.ShapeDtypeStruct((HALO, ext, channels), jnp.bfloat16), level, level],
        scratch_shapes=[
            cells_of(3 * HALO, tiles, ext), cells_of(2 * HALO, tiles, ext),
            half_of(HALO, ext, channels), half_of(2 * HALO, ext, channels),
            pltpu.SemaphoreType.DMA((2,)), pltpu.SemaphoreType.DMA((4,)),
        ],
        compiler_params=pltpu.CompilerParams(vmem_limit_bytes=VMEM_LIMIT),
        cost_estimate=pl.CostEstimate(flops=1000, bytes_accessed=1000, transcendentals=0),
        name="border_north" if north else "border_south",
    )(info, state, *edges, winds, beyond, raw, late, *smooths)


def interior_kernel(rows, lon, ext, info_ref, state_ref, edge_w_ref, edge_e_ref, winds_ref, level_s_ref, level_n_ref,
                    one_s_ref, one_n_ref, smooth_s_ref, smooth_n_ref, out_ref, third_s_ref, third_n_ref,
                    field_a, field_b, field_c, part_ref, winds, sem, in_sem, out_sem):
    inner = rows - 4
    zero = info_ref[4]
    copies = Copies(in_sem)
    mine = OwnRows(info_ref[1] == 1, lon, ext, state_ref, edge_w_ref, edge_e_ref,
                   ((smooth_s_ref, 0), (smooth_n_ref, 0)), field_a, 0, HALO, sem)
    wind_copy = copies.start(winds_ref.at[pl.ds(2, inner)], winds)
    incoming = [copies.start(ref, strip(field, base, ext)) for ref, field, base in (
        (one_s_ref, field_b, 0), (one_n_ref, field_b, inner - HALO), (level_s_ref, field_c, 0), (level_n_ref, field_c, rows - HALO))]
    mine.wait()
    wind_copy.wait()

    def store(r, t, c, count, value):
        field_b[HALO + r, t, pl.ds(PAD + c, count), :] = value

    step_rows(field_a, winds, zero, 0, inner - 2 * HALO, HALO, 0, ext, store)
    for copy in incoming:
        copy.wait()

    def store(r, t, c, count, value):
        field_c[HALO + r, t, pl.ds(PAD + c, count), :] = value

    step_rows(field_b, winds, zero, 0, inner - 4, 2, 0, ext, store)
    step_rows(field_c, winds, zero, 0, inner, 0, 0, ext, store_in(field_b))
    outgoing = [pltpu.make_async_copy(strip(field_b, base, ext), ref, out_sem.at[i])
                for i, (ref, base) in enumerate(((third_s_ref, 0), (third_n_ref, inner - HALO)))]
    for copy in outgoing:
        copy.start()
    step_rows(field_b, winds, zero, 0, inner - 4, 2, REACH, REACH + lon, store_out(part_ref))
    outgoing.append(pltpu.make_async_copy(part_ref, out_ref.at[pl.ds(HALO, rows - 2 * HALO)], out_sem.at[2]))
    outgoing[2].start()
    for copy in outgoing:
        copy.wait()


def interior(info, state, edges, winds, levels, ones, smooths):
    rows, lon, channels = state.shape
    ext = winds.shape[1]
    tiles = channels // LANES
    vmem, hbm = pl.BlockSpec(memory_space=pltpu.VMEM), pl.BlockSpec(memory_space=pl.ANY)
    third = jax.ShapeDtypeStruct((HALO, tiles, ext, LANES), jnp.float32)
    return pl.pallas_call(
        functools.partial(interior_kernel, rows, lon, ext),
        in_specs=[pl.BlockSpec(memory_space=pltpu.SMEM), hbm, vmem, vmem] + [hbm] * 7,
        out_specs=[hbm, hbm, hbm],
        out_shape=[jax.ShapeDtypeStruct((rows, lon, channels), jnp.bfloat16), third, third],
        scratch_shapes=[
            cells_of(rows - 2 * HALO, tiles, ext), cells_of(rows - 4, tiles, ext), cells_of(rows, tiles, ext),
            half_of(rows - 2 * HALO, lon, channels), half_of(rows - 4, ext, channels),
            pltpu.SemaphoreType.DMA((2,)), pltpu.SemaphoreType.DMA((5,)), pltpu.SemaphoreType.DMA((3,)),
        ],
        compiler_params=pltpu.CompilerParams(vmem_limit_bytes=VMEM_LIMIT),
        cost_estimate=pl.CostEstimate(flops=1000, bytes_accessed=1000, transcendentals=0),
        name="interior",
    )(info, state, *edges, winds, *levels, *ones, *smooths)


def finish_kernel(north, rows, lon, ext, _, info_ref, winds_ref, beyond_ref, border_ref, level_ref, third_ref,
                  out_ref, near, last, winds, halo_rows, part_ref, in_sem, out_sem):
    zero = info_ref[4]
    mine, other = (0, HALO) if north else (HALO, 0)
    copies = Copies(in_sem)
    halo_copy = copies.start(border_ref, halo_rows)
    incoming = [
        copies.start(level_ref, strip(near, mine, ext)),
        copies.start(third_ref, strip(last, mine, ext)),
        copies.start(winds_ref.at[pl.ds(rows - HALO if north else 0, HALO)], winds.at[pl.ds(0 if north else 2, HALO)]),
        copies.start(beyond_ref, winds.at[pl.ds(HALO if north else 0, 2)]),
    ]
    halo_copy.wait()
    put_rows(near, halo_rows, other, HALO, ext)
    for copy in incoming:
        copy.wait()

    def store(r, t, c, count, value):
        last[r + other, t, pl.ds(PAD + c, count), :] = value

    step_rows(near, winds, zero, 0, HALO, 2 if north else 0, 0, ext, store)
    step_rows(last, winds, zero, 0, HALO, 0 if north else 2, REACH, REACH + lon, store_out(part_ref))
    copy = pltpu.make_async_copy(part_ref, out_ref.at[pl.ds(rows - HALO if north else 0, HALO)], out_sem.at[0])
    copy.start()
    copy.wait()


def finish(north, info, out, winds, beyond, border, level, third):
    rows, lon, channels = out.shape
    ext = winds.shape[1]
    tiles = channels // LANES
    hbm = pl.BlockSpec(memory_space=pl.ANY)
    return pl.pallas_call(
        functools.partial(finish_kernel, north, rows, lon, ext),
        in_specs=[hbm, pl.BlockSpec(memory_space=pltpu.SMEM)] + [hbm] * 5,
        out_specs=hbm,
        out_shape=jax.ShapeDtypeStruct(out.shape, out.dtype),
        input_output_aliases={0: 0},
        scratch_shapes=[
            cells_of(2 * HALO, tiles, ext), cells_of(2 * HALO, tiles, ext),
            half_of(HALO + 2, ext, channels), half_of(HALO, ext, channels), half_of(HALO, lon, channels),
            pltpu.SemaphoreType.DMA((5,)),
            pltpu.SemaphoreType.DMA((1,)),
        ],
        compiler_params=pltpu.CompilerParams(vmem_limit_bytes=VMEM_LIMIT),
        cost_estimate=pl.CostEstimate(flops=1000, bytes_accessed=1000, transcendentals=0),
        name="finish_north" if north else "finish_south",
    )(out, info, winds, beyond, border, level, third)


def half_of(rows, ext, channels):
    return pltpu.VMEM((rows, ext, channels), jnp.bfloat16)


def cells_of(rows, tiles, ext):
    return pltpu.VMEM((rows, tiles, ext + 2 * PAD, LANES), jnp.float32)


def per_device(state, winds, decay, widths):
    rows, lon, channels = state.shape
    fields = decay.shape[0]
    bands, tiles = lax.axis_size("lat"), lax.axis_size("lon")
    lat, lon_at = lax.axis_index("lat"), lax.axis_index("lon")
    quarter = bands // 4
    ext = round_up(lon + 2 * REACH, 16)
    fill = ext - lon - 2 * REACH
    axes = ("lat", "lon")

    def is_polar(band):
        return band < quarter or band >= bands - quarter

    def polar_at(band):
        return ((band >= 0) & (band < quarter)) | ((band >= bands - quarter) & (band < bands))

    info = jnp.stack([lon_at % 2, polar_at(lat), polar_at(lat - 1), polar_at(lat + 1), lat < 0]).astype(jnp.int32)

    def over_lon(flip):
        return [(b * tiles + l, b * tiles + (l ^ flip)) for b in range(bands) if is_polar(b) for l in range(tiles)]

    def over_lat(shift, wanted=lambda band: True):
        return [(b * tiles + l, (b + shift) * tiles + l)
                for b in range(bands) if 0 <= b + shift < bands and wanted(b) for l in range(tiles)]

    def move(cells, pairs):
        return lax.ppermute(cells, axes, pairs)

    inner = rows - 2 * HALO
    order = [(0, HALO), (rows - HALO, HALO), (HALO, inner)]
    sizes = [2 * HALO, inner // 2, inner // 2]
    starts = [0, 2 * HALO, 2 * HALO + inner // 2]

    def ordered(values):
        return jnp.concatenate([values[f:f + n] for f, n in order], axis=0)

    def joined(cols):
        return jnp.concatenate([state[:, cols].astype(jnp.bfloat16), winds[:, cols]], axis=2)

    east = [(l, (l + 1) % tiles) for l in range(tiles)]
    west = [((l + 1) % tiles, l) for l in range(tiles)]
    head, rear, cells = tie(joined(slice(0, REACH)), joined(slice(lon - REACH, lon)), state)
    from_east = lax.ppermute(head, "lon", west)
    from_west = lax.ppermute(rear, "lon", east)

    opp = [None] * len(sizes)
    circles = [ordered(cells)[:2 * HALO].astype(jnp.bfloat16)]
    circles[0], cells = tie(circles[0], cells)
    opp[0] = move(circles[0], over_lon(2))
    low = ordered(cells).astype(jnp.bfloat16)
    circles += [low[f:f + n] for f, n in zip(starts[1:], sizes[1:])]

    edge_w, edge_e = from_west[:, :, :channels], from_east[:, :, :channels]

    def extend(inner, before, after):
        parts = [before, inner, after, jnp.zeros((inner.shape[0], fill, inner.shape[2]), inner.dtype)]
        return jnp.concatenate(parts, axis=1)

    winds_ext = extend(winds, from_west[:, :, channels:], from_east[:, :, channels:])

    def border(first, wind_first):
        of = slice(first, first + HALO)
        wind = [winds_ext[wind_first + i:wind_first + i + 1] for i in range(2)]
        ends = extend(cells[of].astype(jnp.bfloat16), edge_w[of], edge_e[of])
        return jnp.concatenate([ends, jnp.concatenate(wind, axis=2)], axis=0)

    def is_plain(band):
        return not is_polar(band)

    north_rows, south_rows = border(rows - HALO, rows - 2), border(0, 0)
    raw_s = move(north_rows, over_lat(1, is_plain))
    raw_n = move(south_rows, over_lat(-1, is_plain))
    behind = south_rows[HALO:], north_rows[HALO:]

    def spread(wind):
        half = wind.shape[-1] // 2
        return jnp.concatenate([wind[..., :half]] * 2 + [wind[..., half:]] * 2, axis=-1)

    winds_all = spread(winds_ext)

    def beyond(is_late, late_rows, raw_rows):
        both = jnp.where(is_late, late_rows[HALO], raw_rows[HALO])
        return spread(jnp.stack([both[:, :LANES], both[:, LANES:]]))

    sib = move(low, over_lon(1))
    circles[1], winds_ext = tie(circles[1], winds_ext)
    opp[1] = move(circles[1], over_lon(2))

    own_widths = ordered(lax.dynamic_slice_in_dim(widths, lat * rows, rows))
    rate = jnp.repeat(decay, channels // fields)[None, :]
    reach = own_widths.astype(jnp.float32)[:, None]
    q = jnp.exp(-rate)
    back = round_up(HMAX + 1 + REACH, 8)
    seg = max(back + ext - REACH, round_up(ext + HMAX + 1, 8)) // 8
    carry = jnp.exp(-rate * seg)
    far = jnp.exp(-rate * (reach + 1.0))[:, None, :]
    total = (-jnp.expm1(-rate * (reach + 1.0)) - q * jnp.expm1(-rate * reach)) / -jnp.expm1(-rate)
    scale = (1.0 / total)[:, None, :]

    edges = edge_w, edge_e
    smooths = []
    for i, (f, n) in enumerate(zip(starts, sizes)):
        if i == 0:
            opp[i], raw_n = tie(opp[i], raw_n)
        if i == 1:
            opp[i], raw_s, winds_all = tie(opp[i], raw_s, winds_all)
        if i == 2:
            opp[i], late_s, late_n = tie(opp[i], late_s, late_n)
        if i + 1 < len(sizes) and opp[i + 1] is None:
            opp[i], circles[i + 1] = tie(opp[i], circles[i + 1])
            opp[i + 1] = move(circles[i + 1], over_lon(2))
        diag = move(opp[i], over_lon(1))
        smooth, *ends = smooth_piece(f, n, ext, info, own_widths, circles[i], sib, opp[i], diag,
                                     q, carry, far, scale, behind if i == 0 else ())
        smooths.append(smooth)
        if i + 1 < len(sizes):
            smooth, opp[i + 1] = tie(smooth, opp[i + 1])
        if i == 0:
            late_n, late_s = move(ends[0], over_lat(-1, is_polar)), move(ends[1], over_lat(1, is_polar))
        if i == 1:
            wind_s = beyond(polar_at(lat - 1), late_s, raw_s)
            low_rows, level_s, one_s = border_rows(False, info, state, edges, winds_all, wind_s, raw_s, late_s, smooths[:2])
            to_south = move(low_rows, over_lat(-1))

    wind_n = beyond(polar_at(lat + 1), late_n, raw_n)
    top_rows, level_n, one_n = border_rows(True, info, state, edges, winds_all, wind_n, raw_n, late_n, (smooths[0], smooths[2]))
    to_north = move(top_rows, over_lat(1))
    level_s, to_south, level_n = tie(level_s, to_south, level_n)
    out, third_s, third_n = interior(info, state, edges, winds_all, (level_s, level_n), (one_s, one_n), smooths[1:])
    out = finish(True, info, out, winds_all, wind_n, to_south, level_n, third_n)
    return finish(False, info, out, winds_all, wind_s, to_north, level_s, third_s)


def solution(mesh):
    in_specs = (P("lat", "lon", None), P("lat", "lon", None), P(), P())
    out_specs = P("lat", "lon", None)
    return jax.shard_map(
        per_device, mesh=mesh, in_specs=in_specs, out_specs=out_specs, check_vma=False
    )
```

```python
import functools

import jax
import jax.numpy as jnp
from jax import lax
from jax.experimental import pallas as pl
from jax.experimental.pallas import tpu as pltpu
from jax.sharding import PartitionSpec as P

ADV_STEPS = 4
REACH = 2 * ADV_STEPS
ROUND = 2
HALO = 2 * ROUND
HMAX = 480
LANES = 128
MIB = 1024 * 1024
ODD, POLAR, OUTER_LATE, INNER_LATE, ZERO, LOW_HALF, MIDDLE = range(7)
PAD = 8
COLS = 48


def tie(*values):
    return lax.optimization_barrier(values)


def round_up(value, unit):
    return -(-value // unit) * unit


def smooth_kernel(geo, sends, info_ref, widths_ref, *refs):
    ins, extra_refs, outs, scratch = refs[:8], refs[8:8 + sends], refs[8 + sends:9 + 2 * sends], refs[9 + 2 * sends:]

    @pl.when(info_ref[POLAR] == 1)
    def _():
        smooth_rows(geo, info_ref[ODD] == 1, widths_ref, *ins, *outs[:1], outs[1:], *scratch)
        for ref, extra_ref in zip(outs[1:], extra_refs):
            ref[HALO] = extra_ref[0]


def smooth_rows(geo, odd, widths_ref, own_ref, sib_ref, opp_ref, diag_ref, q_ref, carry_ref, far_ref, scale_ref,
                level_ref, border_refs, cells, east_sum, west_sum):
    lon, back, span, seg, ext = geo
    rows, tiles = own_ref.shape[0], own_ref.shape[2] // LANES
    chains = [(r, t) for r in range(rows) for t in range(tiles)]

    def put(ref, start, begin, count):
        @pl.loop(0, rows)
        def _(r):
            for t in range(tiles):
                part = ref[r, pl.ds(begin, count), pl.ds(t * LANES, LANES)]
                cells[r * tiles + t, pl.ds(start, count), :] = part.astype(jnp.float32)

    head = back - lon
    put(opp_ref, 0, lon - head, head)
    put(own_ref, back, 0, lon)
    put(opp_ref, back + 2 * lon, 0, span - REACH - 2 * lon)

    @pl.when(odd)
    def _():
        put(sib_ref, back - lon, 0, lon)
        put(diag_ref, back + lon, 0, lon)

    @pl.when(jnp.logical_not(odd))
    def _():
        put(diag_ref, back - lon, 0, lon)
        put(sib_ref, back + lon, 0, lon)

    q = [jnp.broadcast_to(q_ref[0:1, t * LANES:(t + 1) * LANES], (8, LANES)) for t in range(tiles)]
    jump = [carry_ref[0:1, t * LANES:(t + 1) * LANES] for t in range(tiles)]
    zero = jnp.zeros((8, LANES), jnp.float32)
    none = jnp.zeros((1, LANES), jnp.float32)
    east_base = back - REACH

    for base, total, forward in ((east_base, east_sum, False), (0, west_sum, True)):
        def at(i, forward=forward):
            return i if forward else seg - 1 - i

        def totals(i, acc, base=base):
            return tuple(cells[r * tiles + t, pl.ds(base + at(i), 8, stride=seg), :] + q[t] * acc[n]
                         for n, (r, t) in enumerate(chains))

        acc = lax.fori_loop(0, seg, totals, (zero,) * len(chains), unroll=4)
        start = []
        for n, (r, t) in enumerate(chains):
            carry = none
            parts = [None] * 8
            for k in (range(8) if forward else range(7, -1, -1)):
                parts[k] = carry
                carry = acc[n][k:k + 1] + jump[t] * carry
            start.append(jnp.concatenate(parts, axis=0))

        def sums(i, acc, base=base, total=total):
            new = []
            for n, (r, t) in enumerate(chains):
                v = cells[r * tiles + t, pl.ds(base + at(i), 8, stride=seg), :] + q[t] * acc[n]
                total[r * tiles + t, pl.ds(at(i), 8, stride=seg), :] = v
                new.append(v)
            return tuple(new)

        lax.fori_loop(0, seg, sums, tuple(start), unroll=4)

    step = COLS

    def one_row(r, border_ref, border_row):
        width = widths_ref[r]
        for t in range(tiles):
            n = r * tiles + t
            far = jnp.broadcast_to(far_ref[r, 0:1, t * LANES:(t + 1) * LANES], (step, LANES))
            scale = jnp.broadcast_to(scale_ref[r, 0:1, t * LANES:(t + 1) * LANES], (step, LANES))
            for c in range(0, ext, step):
                near = east_sum[n, pl.ds(c, step), :] + west_sum[n, pl.ds(back - REACH + c, step), :]
                cut = east_sum[n, pl.ds(c + 1 + width, step), :] + west_sum[n, pl.ds(back - REACH + c - 1 - width, step), :]
                mid = cells[n, pl.ds(back - REACH + c, step), :]
                value = ((near - mid - far * cut) * scale).astype(jnp.bfloat16)
                level_ref[r, t, pl.ds(c, step), :] = value.astype(jnp.float32)
                if border_ref is not None:
                    border_ref[border_row, pl.ds(c, step), pl.ds(t * LANES, LANES)] = value

    @pl.loop(0, rows)
    def _(r):
        one_row(r, border_refs[0] if border_refs else None, r)


def smooth_piece(piece, rows, ext, info, widths, own, sib, opp, diag, q, carry, far, scale, extras):
    lon, channels = own.shape[1:]
    tiles = channels // LANES
    back = round_up(HMAX + 1 + REACH, 8)
    span = round_up(ext + HMAX + 1, 8)
    seg = max(back + ext - REACH, span) // 8
    geo = (lon, back, 8 * seg, seg, ext)
    smem, vmem = pl.BlockSpec(memory_space=pltpu.SMEM), pl.BlockSpec(memory_space=pltpu.VMEM)
    part = pl.BlockSpec((rows, lon, channels), lambda i: (piece % 2, 0, 0))
    table = pl.BlockSpec((rows, 1, channels), lambda i: (piece, 0, 0))
    border = jax.ShapeDtypeStruct((HALO + 1, ext, channels), jnp.bfloat16)
    of_rows = slice(piece * rows, (piece + 1) * rows)
    return pl.pallas_call(
        functools.partial(smooth_kernel, geo, len(extras)),
        grid=(1,),
        in_specs=[smem, smem, vmem, part, vmem, vmem, vmem, vmem, table, table] + [vmem] * len(extras),
        out_specs=[vmem] * (1 + len(extras)),
        out_shape=[jax.ShapeDtypeStruct((rows, tiles, ext, LANES), jnp.float32)] + [border] * len(extras),
        scratch_shapes=[
            pltpu.VMEM((rows * tiles, back - REACH + 8 * seg, LANES), jnp.float32),
            pltpu.VMEM((rows * tiles, 8 * seg, LANES), jnp.float32),
            pltpu.VMEM((rows * tiles, 8 * seg, LANES), jnp.float32),
        ],
        compiler_params=pltpu.CompilerParams(vmem_limit_bytes=28 * MIB),
        cost_estimate=pl.CostEstimate(flops=1000, bytes_accessed=1000, transcendentals=0),
        name="smooth",
    )(info, widths[of_rows], own, sib, opp, diag, q, carry, far, scale, *extras)


def update(src, r, t, c, count, u, v, zero):
    def at(dr, dc):
        return src[r + dr, t, pl.ds(PAD + c + dc + (zero if dc else 0), count), :]

    mid = at(0, 0)
    mid30 = 30.0 * mid
    e1, w1, e2, w2 = at(0, 1), at(0, -1), at(0, 2), at(0, -2)
    n1, s1, n2, s2 = at(1, 0), at(-1, 0), at(2, 0), at(-2, 0)
    first_x = (e2 - w2) - 8.0 * (e1 - w1)
    second_x = 16.0 * (e1 + w1) - (e2 + w2) - mid30
    first_y = (n2 - s2) - 8.0 * (n1 - s1)
    second_y = 16.0 * (n1 + s1) - (n2 + s2) - mid30
    change = u * (first_x + (6.0 * u) * second_x) + v * (first_y + (6.0 * v) * second_y)
    return mid + change


def put_rows(field, ref, base, count, ext):
    @pl.loop(0, count)
    def _(r):
        for t in range(field.shape[1]):
            field[base + r, t, pl.ds(PAD, ext), :] = ref[r, :, pl.ds(t * LANES, LANES)].astype(jnp.float32)


def step_rows(source, winds, zero, first, last, offset, start, stop, store):
    half = LANES // 2
    eastward = lax.broadcasted_iota(jnp.int32, (COLS, LANES), 1) < half

    @pl.loop(first, last)
    def _(r):
        for c in range(start, stop, COLS):
            count = min(COLS, stop - c)
            both = winds[r + offset, pl.ds(c, count), :].astype(jnp.float32) * (1.0 / 12.0)
            swapped = pltpu.roll(both, half, 1)
            u = jnp.where(eastward[:count], both, swapped)
            v = jnp.where(eastward[:count], swapped, both)
            for t in range(source.shape[1]):
                store(r, t, c, count, update(source, r + 2, t, c, count, u, v, zero))


class Copies:
    def __init__(self, sems):
        self.sems, self.used = sems, 0

    def start(self, source, target):
        copy = pltpu.make_async_copy(source, target, self.sems.at[self.used])
        self.used += 1
        copy.start()
        return copy

    def either(self, flag, source, other, target):
        sem = self.sems.at[self.used]
        self.used += 1

        @pl.when(flag)
        def _():
            pltpu.make_async_copy(source, target, sem).start()

        @pl.when(jnp.logical_not(flag))
        def _():
            pltpu.make_async_copy(other, target, sem).start()

        return pltpu.make_async_copy(source, target, sem)


def store_in(field):
    def store(r, t, c, count, value):
        field[r, t, pl.ds(PAD + c, count), :] = value

    return store


def store_out(ref):
    def store(r, t, c, count, value):
        ref[r, pl.ds(c - REACH, count), pl.ds(t * LANES, LANES)] = value.astype(jnp.bfloat16)

    return store


class OwnRows:
    def __init__(self, polar, lon, ext, state_ref, edge_w_ref, edge_e_ref, parts, field, base, first, sems, started=False):
        tiles, count = field.shape[1], HALO * len(parts)
        self.polar, self.edges = polar, (edge_w_ref, edge_e_ref)
        self.place = (field, base, first, count, lon)
        self.smooth, self.plain = [], []
        for i, (ref, start) in enumerate(parts):
            target = field.at[pl.ds(base + i * HALO, HALO), :, pl.ds(PAD, ext), :]
            self.smooth.append(pltpu.make_async_copy(ref.at[pl.ds(start, HALO)], target, sems.at[i]))
        for t in range(tiles):
            self.plain.append(pltpu.make_async_copy(
                state_ref.at[pl.ds(first, count), :, pl.ds(t * LANES, LANES)],
                field.at[pl.ds(base, count), t, pl.ds(PAD + REACH, lon), :], sems.at[t]))
        if not started:
            self.each(lambda copy: copy.start())

    def each(self, act):
        @pl.when(self.polar)
        def _():
            for copy in self.smooth:
                act(copy)

        @pl.when(jnp.logical_not(self.polar))
        def _():
            for copy in self.plain:
                act(copy)

    def wait(self):
        field, base, first, count, lon = self.place
        edge_w_ref, edge_e_ref = self.edges

        @pl.when(jnp.logical_not(self.polar))
        def _():
            @pl.loop(0, count)
            def _(r):
                for t in range(field.shape[1]):
                    lanes = pl.ds(t * LANES, LANES)
                    field[base + r, t, pl.ds(PAD, REACH), :] = edge_w_ref[first + r, :, lanes].astype(jnp.float32)
                    field[base + r, t, pl.ds(PAD + REACH + lon, REACH), :] = edge_e_ref[first + r, :, lanes].astype(jnp.float32)

        self.each(lambda copy: copy.wait())


def strip(field, base, ext):
    return field.at[pl.ds(base, HALO), :, pl.ds(PAD, ext), :]


def winds_beyond(copies, is_late, late_ref, raw_ref, winds, row):
    def part(ref, i):
        return ref.at[HALO, :, pl.ds(i * LANES, LANES)]

    return [copies.either(is_late, part(late_ref, i), part(raw_ref, i), winds.at[row + i]) for i in range(2)]


def on_side(info_ref, outer, body):
    @pl.when(info_ref[LOW_HALF] == 1)
    def _():
        body(not outer)

    @pl.when(info_ref[LOW_HALF] == 0)
    def _():
        body(outer)


def border_kernel(outer, rows, lon, ext, info_ref, state_ref, edge_w_ref, edge_e_ref, winds_ref, raw_ref, late_ref,
                  near_ref, far_ref, border_ref, level_ref, one_ref, field_a, field_b, halo_rows, winds, own_sem, sems):
    zero = info_ref[ZERO]
    is_late = info_ref[OUTER_LATE if outer else INNER_LATE] == 1

    def store_both(r, t, c, count, value):
        level_ref[r, t, pl.ds(c, count), :] = value
        border_ref[r, pl.ds(c, count), pl.ds(t * LANES, LANES)] = value.astype(jnp.bfloat16)

    def body(north):
        halo, own, first = (2 * HALO, 0, rows - 2 * HALO) if north else (0, HALO, 0)
        parts = ((far_ref, 0), (near_ref, 0)) if north else ((near_ref, 0), (far_ref, 0))
        copies = Copies(sems)
        halo_copy = copies.either(is_late, late_ref.at[pl.ds(0, HALO)], raw_ref.at[pl.ds(0, HALO)], halo_rows)
        mine = OwnRows(info_ref[POLAR] == 1, lon, ext, state_ref, edge_w_ref, edge_e_ref, parts, field_a, own, first, own_sem)
        wind_copies = [
            copies.start(winds_ref.at[pl.ds(first + 2 if north else 0, HALO + 2)], winds.at[pl.ds(0 if north else 2, HALO + 2)]),
            *winds_beyond(copies, is_late, late_ref, raw_ref, winds, HALO + 2 if north else 0),
        ]
        halo_copy.wait()
        put_rows(field_a, halo_rows, halo, HALO, ext)
        mine.wait()
        for copy in wind_copies:
            copy.wait()

    def pass_on(north):
        pltpu.make_async_copy(strip(field_b, 0 if north else HALO, ext), one_ref, sems.at[4]).start()

    on_side(info_ref, outer, body)
    step_rows(field_a, winds, zero, 0, 2 * HALO, 0, 0, ext, store_in(field_b))
    on_side(info_ref, outer, pass_on)
    step_rows(field_b, winds, zero, 0, HALO, 2, 0, ext, store_both)
    pltpu.make_async_copy(strip(field_b, 0, ext), one_ref, sems.at[4]).wait()


def border_rows(outer, info, state, edges, winds, raw, late, near, far):
    rows, lon, channels = state.shape
    ext = winds.shape[1]
    tiles = channels // LANES
    vmem, hbm = pl.BlockSpec(memory_space=pltpu.VMEM), pl.BlockSpec(memory_space=pl.ANY)
    level = jax.ShapeDtypeStruct((HALO, tiles, ext, LANES), jnp.float32)
    return pl.pallas_call(
        functools.partial(border_kernel, outer, rows, lon, ext),
        in_specs=[pl.BlockSpec(memory_space=pltpu.SMEM), hbm, vmem, vmem] + [hbm] * 5,
        out_specs=[vmem, vmem, hbm],
        out_shape=[jax.ShapeDtypeStruct((HALO, ext, channels), jnp.bfloat16), level, level],
        scratch_shapes=[
            cells_of(3 * HALO, tiles, ext), cells_of(2 * HALO, tiles, ext),
            half_of(HALO, ext, channels), half_of(2 * HALO, ext, LANES),
            pltpu.SemaphoreType.DMA((2,)), pltpu.SemaphoreType.DMA((5,)),
        ],
        compiler_params=pltpu.CompilerParams(vmem_limit_bytes=20 * MIB),
        cost_estimate=pl.CostEstimate(flops=1000, bytes_accessed=1000, transcendentals=0),
        name="border_outer" if outer else "border_inner",
    )(info, state, *edges, winds, raw, late, near, far)


def interior_kernel(rows, lon, ext, info_ref, state_ref, edge_w_ref, edge_e_ref, winds_ref, level_o_ref, level_i_ref,
                    one_o_ref, one_i_ref, smooth_o_ref, smooth_i_ref, out_ref, third_o_ref, third_i_ref,
                    field_a, field_b, field_c, part_ref, winds, sem, in_sem, out_sem):
    inner = rows - 4
    zero, low_half = info_ref[ZERO], info_ref[LOW_HALF] == 1

    def start(south, north):
        OwnRows(info_ref[POLAR] == 1, lon, ext, state_ref, edge_w_ref, edge_e_ref,
                ((south[0], 0), (north[0], 0)), field_a, 0, HALO, sem)
        copies = Copies(in_sem)
        copies.start(winds_ref.at[pl.ds(2, inner)], winds)
        for one, two, at_one, at_two in ((south[1], south[2], 0, 0), (north[1], north[2], inner - HALO, rows - HALO)):
            copies.start(one, strip(field_b, at_one, ext))
            copies.start(two, strip(field_c, at_two, ext))

    outer_refs, inner_refs = (smooth_o_ref, one_o_ref, level_o_ref), (smooth_i_ref, one_i_ref, level_i_ref)

    @pl.when(low_half)
    def _():
        start(outer_refs, inner_refs)

    @pl.when(jnp.logical_not(low_half))
    def _():
        start(inner_refs, outer_refs)

    OwnRows(info_ref[POLAR] == 1, lon, ext, state_ref, edge_w_ref, edge_e_ref,
            ((smooth_o_ref, 0), (smooth_i_ref, 0)), field_a, 0, HALO, sem, started=True).wait()
    pltpu.make_async_copy(winds_ref.at[pl.ds(2, inner)], winds, in_sem.at[0]).wait()

    def store(r, t, c, count, value):
        field_b[HALO + r, t, pl.ds(PAD + c, count), :] = value

    step_rows(field_a, winds, zero, 0, inner - 2 * HALO, HALO, 0, ext, store)
    for i in range(4):
        pltpu.make_async_copy(one_o_ref, strip(field_b, 0, ext), in_sem.at[1 + i]).wait()

    def store(r, t, c, count, value):
        field_c[HALO + r, t, pl.ds(PAD + c, count), :] = value

    step_rows(field_b, winds, zero, 0, inner - 4, 2, 0, ext, store)
    step_rows(field_c, winds, zero, 0, inner, 0, 0, ext, store_in(field_b))

    def hand_on(south_ref, north_ref):
        for i, (ref, base) in enumerate(((south_ref, 0), (north_ref, inner - HALO))):
            pltpu.make_async_copy(strip(field_b, base, ext), ref, out_sem.at[i]).start()

    @pl.when(low_half)
    def _():
        hand_on(third_o_ref, third_i_ref)

    @pl.when(jnp.logical_not(low_half))
    def _():
        hand_on(third_i_ref, third_o_ref)

    step_rows(field_b, winds, zero, 0, inner - 4, 2, REACH, REACH + lon, store_out(part_ref))
    copy = pltpu.make_async_copy(part_ref, out_ref.at[pl.ds(HALO, rows - 2 * HALO)], out_sem.at[2])
    copy.start()
    for i in range(2):
        pltpu.make_async_copy(strip(field_b, 0, ext), third_o_ref, out_sem.at[i]).wait()
    copy.wait()


def interior(info, state, edges, winds, levels, ones, smooths):
    rows, lon, channels = state.shape
    ext = winds.shape[1]
    tiles = channels // LANES
    vmem, hbm = pl.BlockSpec(memory_space=pltpu.VMEM), pl.BlockSpec(memory_space=pl.ANY)
    third = jax.ShapeDtypeStruct((HALO, tiles, ext, LANES), jnp.float32)
    return pl.pallas_call(
        functools.partial(interior_kernel, rows, lon, ext),
        in_specs=[pl.BlockSpec(memory_space=pltpu.SMEM), hbm, vmem, vmem] + [hbm] * 7,
        out_specs=[hbm, hbm, hbm],
        out_shape=[jax.ShapeDtypeStruct((rows, lon, channels), jnp.bfloat16), third, third],
        scratch_shapes=[
            cells_of(rows - 2 * HALO, tiles, ext), cells_of(rows - 4, tiles, ext), cells_of(rows, tiles, ext),
            half_of(rows - 2 * HALO, lon, channels), half_of(rows - 4, ext, LANES),
            pltpu.SemaphoreType.DMA((2,)), pltpu.SemaphoreType.DMA((5,)), pltpu.SemaphoreType.DMA((3,)),
        ],
        compiler_params=pltpu.CompilerParams(vmem_limit_bytes=24 * MIB),
        cost_estimate=pl.CostEstimate(flops=1000, bytes_accessed=1000, transcendentals=0),
        name="interior",
    )(info, state, *edges, winds, *levels, *ones, *smooths)


def finish_kernel(outer, rows, lon, ext, _, info_ref, winds_ref, raw_ref, late_ref, border_ref, across_ref, level_ref, third_ref,
                  out_ref, near, last, winds, halo_rows, part_ref, in_sem, out_sem):
    zero = info_ref[ZERO]

    def body(north):
        mine, other = (0, HALO) if north else (HALO, 0)
        copies = Copies(in_sem)
        halo_copy = copies.either(info_ref[MIDDLE] == 1, across_ref, border_ref, halo_rows)
        incoming = [
            copies.start(level_ref, strip(near, mine, ext)),
            copies.start(third_ref, strip(last, mine, ext)),
            copies.start(winds_ref.at[pl.ds(rows - HALO if north else 0, HALO)], winds.at[pl.ds(0 if north else 2, HALO)]),
            *winds_beyond(copies, info_ref[OUTER_LATE if outer else INNER_LATE] == 1, late_ref, raw_ref, winds, HALO if north else 0),
        ]
        halo_copy.wait()
        put_rows(near, halo_rows, other, HALO, ext)
        for copy in incoming:
            copy.wait()

        def store(r, t, c, count, value):
            last[r + other, t, pl.ds(PAD + c, count), :] = value

        step_rows(near, winds, zero, 0, HALO, 2 if north else 0, 0, ext, store)
        step_rows(last, winds, zero, 0, HALO, 0 if north else 2, REACH, REACH + lon, store_out(part_ref))
        copy = pltpu.make_async_copy(part_ref, out_ref.at[pl.ds(rows - HALO if north else 0, HALO)], out_sem.at[0])
        copy.start()
        copy.wait()

    on_side(info_ref, outer, body)


def finish(outer, info, out, winds, raw, late, border, across, level, third):
    rows, lon, channels = out.shape
    ext = winds.shape[1]
    tiles = channels // LANES
    hbm = pl.BlockSpec(memory_space=pl.ANY)
    return pl.pallas_call(
        functools.partial(finish_kernel, outer, rows, lon, ext),
        in_specs=[hbm, pl.BlockSpec(memory_space=pltpu.SMEM)] + [hbm] * 7,
        out_specs=hbm,
        out_shape=jax.ShapeDtypeStruct(out.shape, out.dtype),
        input_output_aliases={0: 0},
        scratch_shapes=[
            cells_of(2 * HALO, tiles, ext), cells_of(2 * HALO, tiles, ext),
            half_of(HALO + 2, ext, LANES), half_of(HALO, ext, channels), half_of(HALO, lon, channels),
            pltpu.SemaphoreType.DMA((6,)),
            pltpu.SemaphoreType.DMA((1,)),
        ],
        compiler_params=pltpu.CompilerParams(vmem_limit_bytes=16 * MIB),
        cost_estimate=pl.CostEstimate(flops=1000, bytes_accessed=1000, transcendentals=0),
        name="finish_outer" if outer else "finish_inner",
    )(out, info, winds, raw, late, border, across, level, third)


def half_of(rows, ext, channels):
    return pltpu.VMEM((rows, ext, channels), jnp.bfloat16)


def cells_of(rows, tiles, ext):
    return pltpu.VMEM((rows, tiles, ext + 2 * PAD, LANES), jnp.float32)


def per_device(state, winds, decay, widths):
    rows, lon, channels = state.shape
    fields = decay.shape[0]
    bands, tiles = lax.axis_size("lat"), lax.axis_size("lon")
    lat, lon_at = lax.axis_index("lat"), lax.axis_index("lon")
    quarter = bands // 4
    ext = round_up(lon + 2 * REACH, 16)
    fill = ext - lon - 2 * REACH
    axes = ("lat", "lon")

    middle = bands // 2

    def is_polar(band):
        return band < quarter or band >= bands - quarter

    def is_plain(band):
        return not is_polar(band)

    def inward(band):
        return band + 1 if band < middle else band - 1

    def outward(band):
        return band - 1 if band < middle else band + 1

    def over_lon(flip):
        return [(b * tiles + l, b * tiles + (l ^ flip)) for b in range(bands) if is_polar(b) for l in range(tiles)]

    def over_lat(to, wanted=lambda band: True):
        return [(b * tiles + l, to(b) * tiles + l) for b in range(bands)
                if wanted(b) and 0 <= to(b) < bands and (to(b) < middle) == (b < middle) for l in range(tiles)]

    across = [(b * tiles + l, inward(b) * tiles + l) for b in (middle - 1, middle) for l in range(tiles)]

    def move(cells, pairs):
        return lax.ppermute(cells, axes, pairs)

    low_half = lat < middle
    at_middle = (lat == middle - 1) | (lat == middle)
    polar = (lat < quarter) | (lat >= bands - quarter)
    outer_late = (lat <= quarter) | (lat >= bands - quarter - 1)
    inner_late = (lat < quarter - 1) | (lat > bands - quarter)
    info = jnp.stack([lon_at % 2, polar, outer_late, inner_late, lat < 0, low_half, at_middle]).astype(jnp.int32)

    count = HALO
    starts = [jnp.where(low_half, f, rows - count - f) for f in (0, rows - count, count, rows - 2 * count)]

    def rows_of(values, i):
        return lax.dynamic_slice_in_dim(values, starts[i], count)

    def ordered(values):
        return jnp.concatenate([rows_of(values, i) for i in range(len(starts))], axis=0)

    def joined(cols):
        return jnp.concatenate([state[:, cols].astype(jnp.bfloat16), winds[:, cols]], axis=2)

    east = [(l, (l + 1) % tiles) for l in range(tiles)]
    west = [((l + 1) % tiles, l) for l in range(tiles)]
    head, rear, cells = tie(joined(slice(0, REACH)), joined(slice(lon - REACH, lon)), state)
    from_east = lax.ppermute(head, "lon", west)
    from_west = lax.ppermute(rear, "lon", east)

    opp = [None] * len(starts)
    circles = [rows_of(cells, 0).astype(jnp.bfloat16)]
    circles[0], cells = tie(circles[0], cells)
    opp[0] = move(circles[0], over_lon(2))
    circles += [rows_of(cells, i).astype(jnp.bfloat16) for i in range(1, len(starts))]

    edge_w, edge_e = from_west[:, :, :channels], from_east[:, :, :channels]

    def extend(inner, before, after):
        parts = [before, inner, after, jnp.zeros((inner.shape[0], fill, inner.shape[2]), inner.dtype)]
        return jnp.concatenate(parts, axis=1)

    winds_ext = extend(winds, from_west[:, :, channels:], from_east[:, :, channels:])

    def border(i, wind_first):
        wind = lax.dynamic_slice_in_dim(winds_ext, wind_first, 2)
        ends = extend(rows_of(cells, i).astype(jnp.bfloat16), rows_of(edge_w, i), rows_of(edge_e, i))
        return jnp.concatenate([ends, jnp.concatenate([wind[:1], wind[1:]], axis=2)], axis=0)

    outer_rows = border(0, jnp.where(low_half, 0, rows - 2))
    inner_rows = border(1, jnp.where(low_half, rows - 2, 0))
    raw_out = move(outer_rows, over_lat(outward, is_plain))
    raw_in = move(inner_rows, over_lat(inward, is_plain))
    raw_across = move(inner_rows, across)
    behind = outer_rows[HALO:], inner_rows[HALO:]

    circles[1], outer_rows = tie(circles[1], outer_rows)
    sib = [move(jnp.concatenate(circles[:2], axis=0), over_lon(1)), None]
    opp[1] = move(circles[1], over_lon(2))

    own_widths = ordered(lax.dynamic_slice_in_dim(widths, lat * rows, rows))
    rate = jnp.repeat(decay, channels // fields)[None, :]
    reach = own_widths.astype(jnp.float32)[:, None]
    q = jnp.exp(-rate)
    back = round_up(HMAX + 1 + REACH, 8)
    seg = max(back + ext - REACH, round_up(ext + HMAX + 1, 8)) // 8
    carry = jnp.exp(-rate * seg)
    far = jnp.exp(-rate * (reach + 1.0))[:, None, :]
    total = (-jnp.expm1(-rate * (reach + 1.0)) - q * jnp.expm1(-rate * reach)) / -jnp.expm1(-rate)
    scale = (1.0 / total)[:, None, :]

    edges = edge_w, edge_e
    smooths, late = [], []
    for i in range(len(starts)):
        if i == 1:
            opp[i], raw_out = tie(opp[i], raw_out)
        if i == 2:
            opp[i], late[0], raw_in = tie(opp[i], late[0], raw_in)
        if i == 3:
            opp[i], late[1] = tie(opp[i], late[1])
        if i + 2 < len(starts):
            opp[i], circles[i + 2] = tie(opp[i], circles[i + 2])
            opp[i + 2] = move(circles[i + 2], over_lon(2))
        diag = move(opp[i], over_lon(1))
        if i == 1:
            sib[1] = move(jnp.concatenate(circles[2:], axis=0), over_lon(1))
        smooth, *ends = smooth_piece(i, count, ext, info, own_widths, circles[i], sib[i // 2], opp[i], diag,
                                     q, carry, far, scale, behind[i:i + 1])
        smooths.append(smooth)
        if i + 1 < len(starts):
            smooth, opp[i + 1] = tie(smooth, opp[i + 1])
        if ends:
            late.append(move(ends[0], over_lat((outward, inward)[i], is_polar)))
        if i == 2:
            outer_rows, level_o, one_o = border_rows(
                True, info, state, edges, winds_ext, raw_in, late[1], smooths[0], smooths[2])
            going_out = move(outer_rows, over_lat(outward))

    raw_inner = jnp.where(at_middle, raw_across, raw_out)
    inner_rows, level_i, one_i = border_rows(
        False, info, state, edges, winds_ext, raw_inner, late[0], smooths[1], smooths[3])
    going_in = move(inner_rows, over_lat(inward))
    going_across = move(inner_rows, across)
    out, third_o, third_i = interior(info, state, edges, winds_ext, (level_o, level_i), (one_o, one_i), smooths[2:])
    out = finish(False, info, out, winds_ext, raw_inner, late[0], going_out, going_across, level_i, third_i)
    return finish(True, info, out, winds_ext, raw_in, late[1], going_in, going_in, level_o, third_o)


def solution(mesh):
    in_specs = (P("lat", "lon", None), P("lat", "lon", None), P(), P())
    out_specs = P("lat", "lon", None)
    return jax.shard_map(
        per_device, mesh=mesh, in_specs=in_specs, out_specs=out_specs, check_vma=False
    )
```

```python
import functools

import jax
import jax.numpy as jnp
from jax import lax
from jax.experimental import pallas as pl
from jax.experimental.pallas import tpu as pltpu
from jax.sharding import PartitionSpec as P

ADV_STEPS = 4
REACH = 2 * ADV_STEPS
ROUND = 2
HALO = 2 * ROUND
HMAX = 480
LANES = 128
MIB = 1024 * 1024
ODD, POLAR, OUTER_FROM, INNER_FROM, ZERO, LOW_HALF = range(6)
PAD = 8
COLS = 48


def tie(*values):
    return lax.optimization_barrier(values)


def round_up(value, unit):
    return -(-value // unit) * unit


def smooth_kernel(geo, sends, info_ref, widths_ref, own_ref, sib_ref, opp_ref, *refs):
    diag_ref, refs = refs[0], refs[1:]
    ins, extra_refs, outs, scratch = refs[:4], refs[4:4 + sends], refs[4 + sends:5 + 2 * sends], refs[5 + 2 * sends:]
    ins = (own_ref, sib_ref, opp_ref, diag_ref) + ins

    @pl.when(info_ref[POLAR] == 1)
    def _():
        smooth_rows(geo, info_ref[ODD] == 1, widths_ref, *ins, *outs[:1], outs[1:], *scratch)
        for ref, extra_ref in zip(outs[1:], extra_refs):
            ref[HALO] = extra_ref[0]


def smooth_rows(geo, odd, widths_ref, own_ref, sib_ref, opp_ref, diag_ref, q_ref, carry_ref, far_ref, scale_ref,
                level_ref, border_refs, cells, east_sum, west_sum):
    lon, back, span, seg, ext = geo
    rows, tiles = own_ref.shape[0], own_ref.shape[2] // LANES
    chains = [(r, t) for r in range(rows) for t in range(tiles)]

    def put(ref, start, begin, count):
        @pl.loop(0, rows)
        def _(r):
            for t in range(tiles):
                part = ref[r, pl.ds(begin, count), pl.ds(t * LANES, LANES)]
                cells[r * tiles + t, pl.ds(start, count), :] = part.astype(jnp.float32)

    head = back - lon
    put(opp_ref, 0, lon - head, head)
    put(own_ref, back, 0, lon)
    put(opp_ref, back + 2 * lon, 0, span - REACH - 2 * lon)

    @pl.when(odd)
    def _():
        put(sib_ref, back - lon, 0, lon)
        put(diag_ref, back + lon, 0, lon)

    @pl.when(jnp.logical_not(odd))
    def _():
        put(diag_ref, back - lon, 0, lon)
        put(sib_ref, back + lon, 0, lon)

    q = [jnp.broadcast_to(q_ref[0:1, t * LANES:(t + 1) * LANES], (8, LANES)) for t in range(tiles)]
    jump = [carry_ref[0:1, t * LANES:(t + 1) * LANES] for t in range(tiles)]
    zero = jnp.zeros((8, LANES), jnp.float32)
    none = jnp.zeros((1, LANES), jnp.float32)
    east_base = back - REACH

    for base, total, forward in ((east_base, east_sum, False), (0, west_sum, True)):
        def at(i, forward=forward):
            return i if forward else seg - 1 - i

        def totals(i, acc, base=base):
            return tuple(cells[r * tiles + t, pl.ds(base + at(i), 8, stride=seg), :] + q[t] * acc[n]
                         for n, (r, t) in enumerate(chains))

        acc = lax.fori_loop(0, seg, totals, (zero,) * len(chains), unroll=4)
        start = []
        for n, (r, t) in enumerate(chains):
            carry = none
            parts = [None] * 8
            for k in (range(8) if forward else range(7, -1, -1)):
                parts[k] = carry
                carry = acc[n][k:k + 1] + jump[t] * carry
            start.append(jnp.concatenate(parts, axis=0))

        def sums(i, acc, base=base, total=total):
            new = []
            for n, (r, t) in enumerate(chains):
                v = cells[r * tiles + t, pl.ds(base + at(i), 8, stride=seg), :] + q[t] * acc[n]
                total[r * tiles + t, pl.ds(at(i), 8, stride=seg), :] = v
                new.append(v)
            return tuple(new)

        lax.fori_loop(0, seg, sums, tuple(start), unroll=4)

    step = COLS

    def one_row(r, border_ref, border_row):
        width = widths_ref[r]
        for t in range(tiles):
            n = r * tiles + t
            far = jnp.broadcast_to(far_ref[r, 0:1, t * LANES:(t + 1) * LANES], (step, LANES))
            scale = jnp.broadcast_to(scale_ref[r, 0:1, t * LANES:(t + 1) * LANES], (step, LANES))
            for c in range(0, ext, step):
                near = east_sum[n, pl.ds(c, step), :] + west_sum[n, pl.ds(back - REACH + c, step), :]
                cut = east_sum[n, pl.ds(c + 1 + width, step), :] + west_sum[n, pl.ds(back - REACH + c - 1 - width, step), :]
                mid = cells[n, pl.ds(back - REACH + c, step), :]
                value = ((near - mid - far * cut) * scale).astype(jnp.bfloat16)
                level_ref[r, t, pl.ds(c, step), :] = value.astype(jnp.float32)
                if border_ref is not None:
                    border_ref[border_row, pl.ds(c, step), pl.ds(t * LANES, LANES)] = value

    @pl.loop(0, rows)
    def _(r):
        one_row(r, border_refs[0] if border_refs else None, r)


def smooth_piece(piece, place, rows, ext, info, widths, own, sib, opp, diag, q, carry, far, scale, extras):
    lon, channels = own.shape[1:]
    tiles = channels // LANES
    back = round_up(HMAX + 1 + REACH, 8)
    span = round_up(ext + HMAX + 1, 8)
    seg = max(back + ext - REACH, span) // 8
    geo = (lon, back, 8 * seg, seg, ext)
    smem, vmem = pl.BlockSpec(memory_space=pltpu.SMEM), pl.BlockSpec(memory_space=pltpu.VMEM)
    pair = pl.BlockSpec((rows, lon, channels), lambda i: (piece % 2, 0, 0))
    part = pl.BlockSpec((rows, lon, channels), lambda i: (place, 0, 0))
    table = pl.BlockSpec((rows, 1, channels), lambda i: (piece, 0, 0))
    border = jax.ShapeDtypeStruct((HALO + 1, ext, channels), jnp.bfloat16)
    of_rows = slice(piece * rows, (piece + 1) * rows)
    return pl.pallas_call(
        functools.partial(smooth_kernel, geo, len(extras)),
        grid=(1,),
        in_specs=[smem, smem, part, pair, part, part, vmem, vmem, table, table] + [vmem] * len(extras),
        out_specs=[vmem] * (1 + len(extras)),
        out_shape=[jax.ShapeDtypeStruct((rows, tiles, ext, LANES), jnp.float32)] + [border] * len(extras),
        scratch_shapes=[
            pltpu.VMEM((rows * tiles, back - REACH + 8 * seg, LANES), jnp.float32),
            pltpu.VMEM((rows * tiles, 8 * seg, LANES), jnp.float32),
            pltpu.VMEM((rows * tiles, 8 * seg, LANES), jnp.float32),
        ],
        compiler_params=pltpu.CompilerParams(vmem_limit_bytes=28 * MIB),
        cost_estimate=pl.CostEstimate(flops=1000, bytes_accessed=1000, transcendentals=0),
        name="smooth",
    )(info, widths[of_rows], own, sib, opp, diag, q, carry, far, scale, *extras)


def update(src, r, t, c, count, u, v, zero):
    def at(dr, dc):
        return src[r + dr, t, pl.ds(PAD + c + dc + (zero if dc else 0), count), :]

    mid = at(0, 0)
    mid30 = 30.0 * mid
    e1, w1, e2, w2 = at(0, 1), at(0, -1), at(0, 2), at(0, -2)
    n1, s1, n2, s2 = at(1, 0), at(-1, 0), at(2, 0), at(-2, 0)
    first_x = (e2 - w2) - 8.0 * (e1 - w1)
    second_x = 16.0 * (e1 + w1) - (e2 + w2) - mid30
    first_y = (n2 - s2) - 8.0 * (n1 - s1)
    second_y = 16.0 * (n1 + s1) - (n2 + s2) - mid30
    change = u * (first_x + (6.0 * u) * second_x) + v * (first_y + (6.0 * v) * second_y)
    return mid + change


def put_rows(field, ref, base, count, ext):
    @pl.loop(0, count)
    def _(r):
        for t in range(field.shape[1]):
            field[base + r, t, pl.ds(PAD, ext), :] = ref[r, :, pl.ds(t * LANES, LANES)].astype(jnp.float32)


def step_rows(source, winds, zero, first, last, offset, start, stop, store):
    half = LANES // 2
    eastward = lax.broadcasted_iota(jnp.int32, (COLS, LANES), 1) < half

    @pl.loop(first, last)
    def _(r):
        for c in range(start, stop, COLS):
            count = min(COLS, stop - c)
            both = winds[r + offset, pl.ds(c, count), :].astype(jnp.float32) * (1.0 / 12.0)
            swapped = pltpu.roll(both, half, 1)
            u = jnp.where(eastward[:count], both, swapped)
            v = jnp.where(eastward[:count], swapped, both)
            for t in range(source.shape[1]):
                store(r, t, c, count, update(source, r + 2, t, c, count, u, v, zero))


class Copies:
    def __init__(self, sems):
        self.sems, self.used = sems, 0

    def start(self, source, target):
        copy = pltpu.make_async_copy(source, target, self.sems.at[self.used])
        self.used += 1
        copy.start()
        return copy

    def one_of(self, choice, sources, target):
        sem = self.sems.at[self.used]
        self.used += 1
        for i, source in enumerate(sources):
            @pl.when(choice == i)
            def _(source=source):
                pltpu.make_async_copy(source, target, sem).start()

        return pltpu.make_async_copy(sources[0], target, sem)


def store_in(field):
    def store(r, t, c, count, value):
        field[r, t, pl.ds(PAD + c, count), :] = value

    return store


def store_out(ref):
    def store(r, t, c, count, value):
        ref[r, pl.ds(c - REACH, count), pl.ds(t * LANES, LANES)] = value.astype(jnp.bfloat16)

    return store


class OwnRows:
    def __init__(self, polar, lon, ext, state_ref, edge_w_ref, edge_e_ref, parts, field, base, first, sems, started=False):
        tiles, count = field.shape[1], HALO * len(parts)
        self.polar, self.edges = polar, (edge_w_ref, edge_e_ref)
        self.place = (field, base, first, count, lon)
        self.smooth, self.plain = [], []
        for i, (ref, start) in enumerate(parts):
            target = field.at[pl.ds(base + i * HALO, HALO), :, pl.ds(PAD, ext), :]
            self.smooth.append(pltpu.make_async_copy(ref.at[pl.ds(start, HALO)], target, sems.at[i]))
        for t in range(tiles):
            self.plain.append(pltpu.make_async_copy(
                state_ref.at[pl.ds(first, count), :, pl.ds(t * LANES, LANES)],
                field.at[pl.ds(base, count), t, pl.ds(PAD + REACH, lon), :], sems.at[t]))
        if not started:
            self.each(lambda copy: copy.start())

    def each(self, act):
        @pl.when(self.polar)
        def _():
            for copy in self.smooth:
                act(copy)

        @pl.when(jnp.logical_not(self.polar))
        def _():
            for copy in self.plain:
                act(copy)

    def wait(self):
        field, base, first, count, lon = self.place
        edge_w_ref, edge_e_ref = self.edges

        @pl.when(jnp.logical_not(self.polar))
        def _():
            @pl.loop(0, count)
            def _(r):
                for t in range(field.shape[1]):
                    lanes = pl.ds(t * LANES, LANES)
                    field[base + r, t, pl.ds(PAD, REACH), :] = edge_w_ref[first + r, :, lanes].astype(jnp.float32)
                    field[base + r, t, pl.ds(PAD + REACH + lon, REACH), :] = edge_e_ref[first + r, :, lanes].astype(jnp.float32)

        self.each(lambda copy: copy.wait())


def strip(field, base, ext):
    return field.at[pl.ds(base, HALO), :, pl.ds(PAD, ext), :]


def winds_beyond(copies, origin, refs, winds, row):
    return [copies.one_of(origin, [ref.at[HALO, :, pl.ds(i * LANES, LANES)] for ref in refs], winds.at[row + i]) for i in range(2)]


def on_side(info_ref, outer, body):
    @pl.when(info_ref[LOW_HALF] == 1)
    def _():
        body(not outer)

    @pl.when(info_ref[LOW_HALF] == 0)
    def _():
        body(outer)


def border_kernel(outer, rows, lon, ext, info_ref, state_ref, edge_w_ref, edge_e_ref, winds_ref, late_ref, raw_ref, across_ref,
                  near_ref, far_ref, border_ref, level_ref, one_ref, field_a, field_b, halo_rows, winds, own_sem, sems):
    zero = info_ref[ZERO]
    origin, origins = info_ref[OUTER_FROM if outer else INNER_FROM], (late_ref, raw_ref, across_ref)

    def store_both(r, t, c, count, value):
        level_ref[r, t, pl.ds(c, count), :] = value
        border_ref[r, pl.ds(c, count), pl.ds(t * LANES, LANES)] = value.astype(jnp.bfloat16)

    def body(north):
        halo, own, first = (2 * HALO, 0, rows - 2 * HALO) if north else (0, HALO, 0)
        parts = ((far_ref, 0), (near_ref, 0)) if north else ((near_ref, 0), (far_ref, 0))
        copies = Copies(sems)
        halo_copy = copies.one_of(origin, [ref.at[pl.ds(0, HALO)] for ref in origins], halo_rows)
        mine = OwnRows(info_ref[POLAR] == 1, lon, ext, state_ref, edge_w_ref, edge_e_ref, parts, field_a, own, first, own_sem)
        wind_copies = [
            copies.start(winds_ref.at[pl.ds(first + 2 if north else 0, HALO + 2)], winds.at[pl.ds(0 if north else 2, HALO + 2)]),
            *winds_beyond(copies, origin, origins, winds, HALO + 2 if north else 0),
        ]
        halo_copy.wait()
        put_rows(field_a, halo_rows, halo, HALO, ext)
        mine.wait()
        for copy in wind_copies:
            copy.wait()

    def pass_on(north):
        pltpu.make_async_copy(strip(field_b, 0 if north else HALO, ext), one_ref, sems.at[4]).start()

    on_side(info_ref, outer, body)
    step_rows(field_a, winds, zero, 0, 2 * HALO, 0, 0, ext, store_in(field_b))
    on_side(info_ref, outer, pass_on)
    step_rows(field_b, winds, zero, 0, HALO, 2, 0, ext, store_both)
    pltpu.make_async_copy(strip(field_b, 0, ext), one_ref, sems.at[4]).wait()


def border_rows(outer, info, state, edges, winds, origins, near, far):
    rows, lon, channels = state.shape
    ext = winds.shape[1]
    tiles = channels // LANES
    vmem, hbm = pl.BlockSpec(memory_space=pltpu.VMEM), pl.BlockSpec(memory_space=pl.ANY)
    level = jax.ShapeDtypeStruct((HALO, tiles, ext, LANES), jnp.float32)
    return pl.pallas_call(
        functools.partial(border_kernel, outer, rows, lon, ext),
        in_specs=[pl.BlockSpec(memory_space=pltpu.SMEM), hbm, vmem, vmem] + [hbm] * 6,
        out_specs=[vmem, vmem, hbm],
        out_shape=[jax.ShapeDtypeStruct((HALO, ext, channels), jnp.bfloat16), level, level],
        scratch_shapes=[
            cells_of(3 * HALO, tiles, ext), cells_of(2 * HALO, tiles, ext),
            half_of(HALO, ext, channels), half_of(2 * HALO, ext, LANES),
            pltpu.SemaphoreType.DMA((2,)), pltpu.SemaphoreType.DMA((5,)),
        ],
        compiler_params=pltpu.CompilerParams(vmem_limit_bytes=20 * MIB),
        cost_estimate=pl.CostEstimate(flops=1000, bytes_accessed=1000, transcendentals=0),
        name="border_outer" if outer else "border_inner",
    )(info, state, *edges, winds, *origins, near, far)


def interior_kernel(rows, lon, ext, info_ref, state_ref, edge_w_ref, edge_e_ref, winds_ref, level_o_ref, level_i_ref,
                    one_o_ref, one_i_ref, smooth_o_ref, smooth_i_ref, out_ref, third_o_ref, third_i_ref,
                    field_a, field_b, field_c, part_ref, winds, sem, in_sem, out_sem):
    inner = rows - 4
    zero, low_half = info_ref[ZERO], info_ref[LOW_HALF] == 1

    def start(south, north):
        OwnRows(info_ref[POLAR] == 1, lon, ext, state_ref, edge_w_ref, edge_e_ref,
                ((south[0], 0), (north[0], 0)), field_a, 0, HALO, sem)
        copies = Copies(in_sem)
        copies.start(winds_ref.at[pl.ds(2, inner)], winds)
        for one, two, at_one, at_two in ((south[1], south[2], 0, 0), (north[1], north[2], inner - HALO, rows - HALO)):
            copies.start(one, strip(field_b, at_one, ext))
            copies.start(two, strip(field_c, at_two, ext))

    outer_refs, inner_refs = (smooth_o_ref, one_o_ref, level_o_ref), (smooth_i_ref, one_i_ref, level_i_ref)

    @pl.when(low_half)
    def _():
        start(outer_refs, inner_refs)

    @pl.when(jnp.logical_not(low_half))
    def _():
        start(inner_refs, outer_refs)

    OwnRows(info_ref[POLAR] == 1, lon, ext, state_ref, edge_w_ref, edge_e_ref,
            ((smooth_o_ref, 0), (smooth_i_ref, 0)), field_a, 0, HALO, sem, started=True).wait()
    pltpu.make_async_copy(winds_ref.at[pl.ds(2, inner)], winds, in_sem.at[0]).wait()

    def store(r, t, c, count, value):
        field_b[HALO + r, t, pl.ds(PAD + c, count), :] = value

    step_rows(field_a, winds, zero, 0, inner - 2 * HALO, HALO, 0, ext, store)
    for i in range(4):
        pltpu.make_async_copy(one_o_ref, strip(field_b, 0, ext), in_sem.at[1 + i]).wait()

    def store(r, t, c, count, value):
        field_c[HALO + r, t, pl.ds(PAD + c, count), :] = value

    step_rows(field_b, winds, zero, 0, inner - 4, 2, 0, ext, store)
    step_rows(field_c, winds, zero, 0, inner, 0, 0, ext, store_in(field_b))

    def hand_on(south_ref, north_ref):
        for i, (ref, base) in enumerate(((south_ref, 0), (north_ref, inner - HALO))):
            pltpu.make_async_copy(strip(field_b, base, ext), ref, out_sem.at[i]).start()

    @pl.when(low_half)
    def _():
        hand_on(third_o_ref, third_i_ref)

    @pl.when(jnp.logical_not(low_half))
    def _():
        hand_on(third_i_ref, third_o_ref)

    step_rows(field_b, winds, zero, 0, inner - 4, 2, REACH, REACH + lon, store_out(part_ref))
    copy = pltpu.make_async_copy(part_ref, out_ref.at[pl.ds(HALO, rows - 2 * HALO)], out_sem.at[2])
    copy.start()
    for i in range(2):
        pltpu.make_async_copy(strip(field_b, 0, ext), third_o_ref, out_sem.at[i]).wait()
    copy.wait()


def interior(info, state, edges, winds, levels, ones, smooths):
    rows, lon, channels = state.shape
    ext = winds.shape[1]
    tiles = channels // LANES
    vmem, hbm = pl.BlockSpec(memory_space=pltpu.VMEM), pl.BlockSpec(memory_space=pl.ANY)
    third = jax.ShapeDtypeStruct((HALO, tiles, ext, LANES), jnp.float32)
    return pl.pallas_call(
        functools.partial(interior_kernel, rows, lon, ext),
        in_specs=[pl.BlockSpec(memory_space=pltpu.SMEM), hbm, vmem, vmem] + [hbm] * 7,
        out_specs=[hbm, hbm, hbm],
        out_shape=[jax.ShapeDtypeStruct((rows, lon, channels), jnp.bfloat16), third, third],
        scratch_shapes=[
            cells_of(rows - 2 * HALO, tiles, ext), cells_of(rows - 4, tiles, ext), cells_of(rows, tiles, ext),
            half_of(rows - 2 * HALO, lon, channels), half_of(rows - 4, ext, LANES),
            pltpu.SemaphoreType.DMA((2,)), pltpu.SemaphoreType.DMA((5,)), pltpu.SemaphoreType.DMA((3,)),
        ],
        compiler_params=pltpu.CompilerParams(vmem_limit_bytes=24 * MIB),
        cost_estimate=pl.CostEstimate(flops=1000, bytes_accessed=1000, transcendentals=0),
        name="interior",
    )(info, state, *edges, winds, *levels, *ones, *smooths)


def finish_kernel(outer, rows, lon, ext, _, info_ref, winds_ref, late_ref, raw_ref, across_raw_ref, border_ref, across_ref, level_ref, third_ref,
                  out_ref, near, last, winds, halo_rows, part_ref, in_sem, out_sem):
    zero = info_ref[ZERO]

    def body(north):
        mine, other = (0, HALO) if north else (HALO, 0)
        copies = Copies(in_sem)
        origin = info_ref[OUTER_FROM if outer else INNER_FROM]
        halo_copy = copies.one_of(origin, (border_ref, border_ref, across_ref), halo_rows)
        incoming = [
            copies.start(level_ref, strip(near, mine, ext)),
            copies.start(third_ref, strip(last, mine, ext)),
            copies.start(winds_ref.at[pl.ds(rows - HALO if north else 0, HALO)], winds.at[pl.ds(0 if north else 2, HALO)]),
            *winds_beyond(copies, origin, (late_ref, raw_ref, across_raw_ref), winds, HALO if north else 0),
        ]
        halo_copy.wait()
        put_rows(near, halo_rows, other, HALO, ext)
        for copy in incoming:
            copy.wait()

        def store(r, t, c, count, value):
            last[r + other, t, pl.ds(PAD + c, count), :] = value

        step_rows(near, winds, zero, 0, HALO, 2 if north else 0, 0, ext, store)
        step_rows(last, winds, zero, 0, HALO, 0 if north else 2, REACH, REACH + lon, store_out(part_ref))
        copy = pltpu.make_async_copy(part_ref, out_ref.at[pl.ds(rows - HALO if north else 0, HALO)], out_sem.at[0])
        copy.start()
        copy.wait()

    on_side(info_ref, outer, body)


def finish(outer, info, out, winds, origins, border, across, level, third):
    rows, lon, channels = out.shape
    ext = winds.shape[1]
    tiles = channels // LANES
    hbm = pl.BlockSpec(memory_space=pl.ANY)
    return pl.pallas_call(
        functools.partial(finish_kernel, outer, rows, lon, ext),
        in_specs=[hbm, pl.BlockSpec(memory_space=pltpu.SMEM)] + [hbm] * 8,
        out_specs=hbm,
        out_shape=jax.ShapeDtypeStruct(out.shape, out.dtype),
        input_output_aliases={0: 0},
        scratch_shapes=[
            cells_of(2 * HALO, tiles, ext), cells_of(2 * HALO, tiles, ext),
            half_of(HALO + 2, ext, LANES), half_of(HALO, ext, channels), half_of(HALO, lon, channels),
            pltpu.SemaphoreType.DMA((6,)),
            pltpu.SemaphoreType.DMA((1,)),
        ],
        compiler_params=pltpu.CompilerParams(vmem_limit_bytes=16 * MIB),
        cost_estimate=pl.CostEstimate(flops=1000, bytes_accessed=1000, transcendentals=0),
        name="finish_outer" if outer else "finish_inner",
    )(out, info, winds, *origins, border, across, level, third)


def half_of(rows, ext, channels):
    return pltpu.VMEM((rows, ext, channels), jnp.bfloat16)


def cells_of(rows, tiles, ext):
    return pltpu.VMEM((rows, tiles, ext + 2 * PAD, LANES), jnp.float32)


def per_device(state, winds, decay, widths):
    rows, lon, channels = state.shape
    fields = decay.shape[0]
    bands, tiles = lax.axis_size("lat"), lax.axis_size("lon")
    lat, lon_at = lax.axis_index("lat"), lax.axis_index("lon")
    quarter = bands // 4
    ext = round_up(lon + 2 * REACH, 16)
    fill = ext - lon - 2 * REACH
    axes = ("lat", "lon")

    middle = bands // 2

    def is_polar(band):
        return band < quarter or band >= bands - quarter

    def is_plain(band):
        return not is_polar(band)

    def inward(band):
        return band + 1 if band < middle else band - 1

    def outward(band):
        return band - 1 if band < middle else band + 1

    def over_lon(flip):
        return [(b * tiles + l, b * tiles + (l ^ flip)) for b in range(bands) if is_polar(b) for l in range(tiles)]

    def over_lat(to, wanted=lambda band: True):
        return [(b * tiles + l, to(b) * tiles + l) for b in range(bands)
                if wanted(b) and 0 <= to(b) < bands and (to(b) < middle) == (b < middle) for l in range(tiles)]

    across = [(b * tiles + l, inward(b) * tiles + l) for b in (middle - 1, middle) for l in range(tiles)]

    def move(cells, pairs):
        return lax.ppermute(cells, axes, pairs)

    low_half = lat < middle
    at_middle = (lat == middle - 1) | (lat == middle)
    polar = (lat < quarter) | (lat >= bands - quarter)
    outer_from = jnp.where((lat <= quarter) | (lat >= bands - quarter - 1), 0, 1)
    inner_from = jnp.where((lat < quarter - 1) | (lat > bands - quarter), 0, jnp.where(at_middle, 2, 1))
    numbers = [lon_at % 2, polar, outer_from, inner_from, lat < 0, low_half]
    info = jnp.stack([jnp.asarray(n, jnp.int32) for n in numbers])

    count = HALO
    starts = [jnp.where(low_half, f, rows - count - f) for f in (0, rows - count, count, rows - 2 * count)]

    def rows_of(values, i):
        return lax.dynamic_slice_in_dim(values, starts[i], count)

    def ordered(values):
        return jnp.concatenate([rows_of(values, i) for i in range(len(starts))], axis=0)

    def joined(cols):
        return jnp.concatenate([state[:, cols].astype(jnp.bfloat16), winds[:, cols]], axis=2)

    east = [(l, (l + 1) % tiles) for l in range(tiles)]
    west = [((l + 1) % tiles, l) for l in range(tiles)]
    head, rear, cells = tie(joined(slice(0, REACH)), joined(slice(lon - REACH, lon)), state)
    from_east = lax.ppermute(head, "lon", west)
    from_west = lax.ppermute(rear, "lon", east)

    opp = [None] * len(starts)
    circles = [rows_of(cells, 0).astype(jnp.bfloat16)]
    circles[0], cells = tie(circles[0], cells)
    opp[0] = move(circles[0], over_lon(2))
    circles += [rows_of(cells, i).astype(jnp.bfloat16) for i in range(1, len(starts))]

    edge_w, edge_e = from_west[:, :, :channels], from_east[:, :, :channels]

    def extend(inner, before, after):
        parts = [before, inner, after, jnp.zeros((inner.shape[0], fill, inner.shape[2]), inner.dtype)]
        return jnp.concatenate(parts, axis=1)

    winds_ext = extend(winds, from_west[:, :, channels:], from_east[:, :, channels:])

    def border(i, wind_first):
        wind = lax.dynamic_slice_in_dim(winds_ext, wind_first, 2)
        ends = extend(rows_of(cells, i).astype(jnp.bfloat16), rows_of(edge_w, i), rows_of(edge_e, i))
        return jnp.concatenate([ends, jnp.concatenate([wind[:1], wind[1:]], axis=2)], axis=0)

    outer_rows = border(0, jnp.where(low_half, 0, rows - 2))
    inner_rows = border(1, jnp.where(low_half, rows - 2, 0))
    raw_out = move(outer_rows, over_lat(outward, is_plain))
    raw_in = move(inner_rows, over_lat(inward, is_plain))
    raw_across = move(inner_rows, across)
    behind = outer_rows[HALO:], inner_rows[HALO:]

    circles[1], outer_rows = tie(circles[1], outer_rows)
    sib = move(jnp.concatenate(circles[:2], axis=0), over_lon(1))
    opp[1] = move(circles[1], over_lon(2))

    own_widths = ordered(lax.dynamic_slice_in_dim(widths, lat * rows, rows))
    rate = jnp.repeat(decay, channels // fields)[None, :]
    reach = own_widths.astype(jnp.float32)[:, None]
    q = jnp.exp(-rate)
    back = round_up(HMAX + 1 + REACH, 8)
    seg = max(back + ext - REACH, round_up(ext + HMAX + 1, 8)) // 8
    carry = jnp.exp(-rate * seg)
    far = jnp.exp(-rate * (reach + 1.0))[:, None, :]
    total = (-jnp.expm1(-rate * (reach + 1.0)) - q * jnp.expm1(-rate * reach)) / -jnp.expm1(-rate)
    scale = (1.0 / total)[:, None, :]

    edges = edge_w, edge_e
    smooths, late = [], []

    def smoothed(i, place, own, sib, opp, diag):
        return smooth_piece(i, place, count, ext, info, own_widths, own, sib, opp, diag, q, carry, far, scale, behind[i:i + 1])

    for i in range(2):
        if i == 0:
            opp[0], last_two = tie(opp[0], jnp.concatenate(circles[2:], axis=0))
            last_opp = move(last_two, over_lon(2))
        diag = move(opp[i], over_lon(1))
        smooth, ends = smoothed(i, 0, circles[i], sib, opp[i], diag)
        smooths.append(smooth)
        if i == 1:
            ends, raw_out = tie(ends, raw_out)
        late.append(move(ends, over_lat((outward, inward)[i], is_polar)))
        if i == 0:
            smooth, opp[1] = tie(smooth, opp[1])
        else:
            smooth, last_opp = tie(smooth, last_opp)

    last_opp, late[0], late[1], raw_in = tie(last_opp, late[0], late[1], raw_in)
    last_sib = move(last_two, over_lon(1))
    diag = move(last_opp, over_lon(1))
    smooths += smoothed(2, 0, last_two, last_sib, last_opp, diag)
    outer_rows, level_o, one_o = border_rows(
        True, info, state, edges, winds_ext, (late[1], raw_in, raw_in), smooths[0], smooths[2])
    going_out = move(outer_rows, over_lat(outward))
    smooths += smoothed(3, 1, last_two, last_sib, last_opp, diag)
    inner_origins, outer_origins = (late[0], raw_out, raw_across), (late[1], raw_in, raw_in)
    inner_rows, level_i, one_i = border_rows(
        False, info, state, edges, winds_ext, inner_origins, smooths[1], smooths[3])
    going_in = move(inner_rows, over_lat(inward))
    going_across = move(inner_rows, across)
    out, third_o, third_i = interior(info, state, edges, winds_ext, (level_o, level_i), (one_o, one_i), smooths[2:])
    out = finish(False, info, out, winds_ext, inner_origins, going_out, going_across, level_i, third_i)
    return finish(True, info, out, winds_ext, outer_origins, going_in, going_in, level_o, third_o)


def solution(mesh):
    in_specs = (P("lat", "lon", None), P("lat", "lon", None), P(), P())
    out_specs = P("lat", "lon", None)
    return jax.shard_map(
        per_device, mesh=mesh, in_specs=in_specs, out_specs=out_specs, check_vma=False
    )
```

```python
import functools

import jax
import jax.numpy as jnp
from jax import lax
from jax.experimental import pallas as pl
from jax.experimental.pallas import tpu as pltpu
from jax.sharding import PartitionSpec as P

ADV_STEPS = 4
REACH = 2 * ADV_STEPS
ROUND = 2
HALO = 2 * ROUND
HMAX = 480
LANES = 128
MIB = 1024 * 1024
ODD, POLAR, OUTER_FROM, INNER_FROM, ZERO, LOW_HALF = range(6)
PAD = 8
COLS = 48


def tie(*values):
    return lax.optimization_barrier(values)


def round_up(value, unit):
    return -(-value // unit) * unit


def smooth_kernel(geo, sends, info_ref, widths_ref, own_ref, sib_ref, opp_ref, *refs):
    diag_ref, refs = refs[0], refs[1:]
    ins, extra_refs, outs, scratch = refs[:4], refs[4:4 + sends], refs[4 + sends:5 + 2 * sends], refs[5 + 2 * sends:]
    ins = (own_ref, sib_ref, opp_ref, diag_ref) + ins

    @pl.when(info_ref[POLAR] == 1)
    def _():
        smooth_rows(geo, info_ref[ODD] == 1, widths_ref, *ins, *outs[:1], outs[1:], *scratch)
        for ref, extra_ref in zip(outs[1:], extra_refs):
            ref[HALO] = extra_ref[0]


def smooth_rows(geo, odd, widths_ref, own_ref, sib_ref, opp_ref, diag_ref, q_ref, carry_ref, far_ref, scale_ref,
                level_ref, border_refs, cells, east_sum, west_sum):
    lon, back, span, seg, ext = geo
    rows, tiles = own_ref.shape[0], own_ref.shape[2] // LANES
    chains = [(r, t) for r in range(rows) for t in range(tiles)]

    def put(ref, start, begin, count):
        @pl.loop(0, rows)
        def _(r):
            for t in range(tiles):
                part = ref[r, pl.ds(begin, count), pl.ds(t * LANES, LANES)]
                cells[r * tiles + t, pl.ds(start, count), :] = part.astype(jnp.float32)

    head = back - lon
    put(opp_ref, 0, lon - head, head)
    put(own_ref, back, 0, lon)
    put(opp_ref, back + 2 * lon, 0, span - REACH - 2 * lon)

    @pl.when(odd)
    def _():
        put(sib_ref, back - lon, 0, lon)
        put(diag_ref, back + lon, 0, lon)

    @pl.when(jnp.logical_not(odd))
    def _():
        put(diag_ref, back - lon, 0, lon)
        put(sib_ref, back + lon, 0, lon)

    q = [jnp.broadcast_to(q_ref[0:1, t * LANES:(t + 1) * LANES], (8, LANES)) for t in range(tiles)]
    jump = [carry_ref[0:1, t * LANES:(t + 1) * LANES] for t in range(tiles)]
    zero = jnp.zeros((8, LANES), jnp.float32)
    none = jnp.zeros((1, LANES), jnp.float32)
    east_base = back - REACH

    for base, total, forward in ((east_base, east_sum, False), (0, west_sum, True)):
        def at(i, forward=forward):
            return i if forward else seg - 1 - i

        def totals(i, acc, base=base):
            return tuple(cells[r * tiles + t, pl.ds(base + at(i), 8, stride=seg), :] + q[t] * acc[n]
                         for n, (r, t) in enumerate(chains))

        acc = lax.fori_loop(0, seg, totals, (zero,) * len(chains), unroll=4)
        start = []
        for n, (r, t) in enumerate(chains):
            carry = none
            parts = [None] * 8
            for k in (range(8) if forward else range(7, -1, -1)):
                parts[k] = carry
                carry = acc[n][k:k + 1] + jump[t] * carry
            start.append(jnp.concatenate(parts, axis=0))

        def sums(i, acc, base=base, total=total):
            new = []
            for n, (r, t) in enumerate(chains):
                v = cells[r * tiles + t, pl.ds(base + at(i), 8, stride=seg), :] + q[t] * acc[n]
                total[r * tiles + t, pl.ds(at(i), 8, stride=seg), :] = v
                new.append(v)
            return tuple(new)

        lax.fori_loop(0, seg, sums, tuple(start), unroll=4)

    step = COLS

    def one_row(r, border_ref, border_row):
        width = widths_ref[r]
        for t in range(tiles):
            n = r * tiles + t
            far = jnp.broadcast_to(far_ref[r, 0:1, t * LANES:(t + 1) * LANES], (step, LANES))
            scale = jnp.broadcast_to(scale_ref[r, 0:1, t * LANES:(t + 1) * LANES], (step, LANES))
            for c in range(0, ext, step):
                near = east_sum[n, pl.ds(c, step), :] + west_sum[n, pl.ds(back - REACH + c, step), :]
                cut = east_sum[n, pl.ds(c + 1 + width, step), :] + west_sum[n, pl.ds(back - REACH + c - 1 - width, step), :]
                mid = cells[n, pl.ds(back - REACH + c, step), :]
                value = ((near - mid - far * cut) * scale).astype(jnp.bfloat16)
                level_ref[r, t, pl.ds(c, step), :] = value.astype(jnp.float32)
                if border_ref is not None:
                    border_ref[border_row, pl.ds(c, step), pl.ds(t * LANES, LANES)] = value

    @pl.loop(0, rows)
    def _(r):
        one_row(r, border_refs[0] if border_refs else None, r)


def smooth_piece(piece, place, rows, ext, info, widths, own, sib, opp, diag, q, carry, far, scale, extras):
    lon, channels = own.shape[1:]
    tiles = channels // LANES
    back = round_up(HMAX + 1 + REACH, 8)
    span = round_up(ext + HMAX + 1, 8)
    seg = max(back + ext - REACH, span) // 8
    geo = (lon, back, 8 * seg, seg, ext)
    smem, vmem = pl.BlockSpec(memory_space=pltpu.SMEM), pl.BlockSpec(memory_space=pltpu.VMEM)
    pair = pl.BlockSpec((rows, lon, channels), lambda i: (piece % 2, 0, 0))
    part = pl.BlockSpec((rows, lon, channels), lambda i: (place, 0, 0))
    table = pl.BlockSpec((rows, 1, channels), lambda i: (piece, 0, 0))
    border = jax.ShapeDtypeStruct((HALO + 1, ext, channels), jnp.bfloat16)
    of_rows = slice(piece * rows, (piece + 1) * rows)
    return pl.pallas_call(
        functools.partial(smooth_kernel, geo, len(extras)),
        grid=(1,),
        in_specs=[smem, smem, part, pair, part, part, vmem, vmem, table, table] + [vmem] * len(extras),
        out_specs=[vmem] * (1 + len(extras)),
        out_shape=[jax.ShapeDtypeStruct((rows, tiles, ext, LANES), jnp.float32)] + [border] * len(extras),
        scratch_shapes=[
            pltpu.VMEM((rows * tiles, back - REACH + 8 * seg, LANES), jnp.float32),
            pltpu.VMEM((rows * tiles, 8 * seg, LANES), jnp.float32),
            pltpu.VMEM((rows * tiles, 8 * seg, LANES), jnp.float32),
        ],
        compiler_params=pltpu.CompilerParams(vmem_limit_bytes=28 * MIB),
        cost_estimate=pl.CostEstimate(flops=1000, bytes_accessed=1000, transcendentals=0),
        name="smooth",
    )(info, widths[of_rows], own, sib, opp, diag, q, carry, far, scale, *extras)


def update(src, r, t, c, count, u, v, zero):
    def at(dr, dc):
        return src[r + dr, t, pl.ds(PAD + c + dc + (zero if dc else 0), count), :]

    mid = at(0, 0)
    mid30 = 30.0 * mid
    e1, w1, e2, w2 = at(0, 1), at(0, -1), at(0, 2), at(0, -2)
    n1, s1, n2, s2 = at(1, 0), at(-1, 0), at(2, 0), at(-2, 0)
    first_x = (e2 - w2) - 8.0 * (e1 - w1)
    second_x = 16.0 * (e1 + w1) - (e2 + w2) - mid30
    first_y = (n2 - s2) - 8.0 * (n1 - s1)
    second_y = 16.0 * (n1 + s1) - (n2 + s2) - mid30
    change = u * (first_x + (6.0 * u) * second_x) + v * (first_y + (6.0 * v) * second_y)
    return mid + change


def put_rows(field, ref, base, count, ext):
    @pl.loop(0, count)
    def _(r):
        for t in range(field.shape[1]):
            field[base + r, t, pl.ds(PAD, ext), :] = ref[r, :, pl.ds(t * LANES, LANES)].astype(jnp.float32)


def step_rows(source, winds, zero, first, last, offset, start, stop, store):
    half = LANES // 2
    eastward = lax.broadcasted_iota(jnp.int32, (COLS, LANES), 1) < half

    @pl.loop(first, last)
    def _(r):
        for c in range(start, stop, COLS):
            count = min(COLS, stop - c)
            both = winds[r + offset, pl.ds(c, count), :].astype(jnp.float32) * (1.0 / 12.0)
            swapped = pltpu.roll(both, half, 1)
            u = jnp.where(eastward[:count], both, swapped)
            v = jnp.where(eastward[:count], swapped, both)
            for t in range(source.shape[1]):
                store(r, t, c, count, update(source, r + 2, t, c, count, u, v, zero))


class Copies:
    def __init__(self, sems):
        self.sems, self.used = sems, 0

    def start(self, source, target):
        copy = pltpu.make_async_copy(source, target, self.sems.at[self.used])
        self.used += 1
        copy.start()
        return copy

    def one_of(self, choice, sources, target):
        sem = self.sems.at[self.used]
        self.used += 1
        for i, source in enumerate(sources):
            @pl.when(choice == i)
            def _(source=source):
                pltpu.make_async_copy(source, target, sem).start()

        return pltpu.make_async_copy(sources[0], target, sem)


def store_in(field):
    def store(r, t, c, count, value):
        field[r, t, pl.ds(PAD + c, count), :] = value

    return store


def store_out(ref):
    def store(r, t, c, count, value):
        ref[r, pl.ds(c - REACH, count), pl.ds(t * LANES, LANES)] = value.astype(jnp.bfloat16)

    return store


class OwnRows:
    def __init__(self, polar, lon, ext, state_ref, edge_w_ref, edge_e_ref, parts, field, base, first, sems, started=False):
        tiles, count = field.shape[1], HALO * len(parts)
        self.polar, self.edges = polar, (edge_w_ref, edge_e_ref)
        self.place = (field, base, first, count, lon)
        self.smooth, self.plain = [], []
        for i, (ref, start) in enumerate(parts):
            target = field.at[pl.ds(base + i * HALO, HALO), :, pl.ds(PAD, ext), :]
            self.smooth.append(pltpu.make_async_copy(ref.at[pl.ds(start, HALO)], target, sems.at[i]))
        for t in range(tiles):
            self.plain.append(pltpu.make_async_copy(
                state_ref.at[pl.ds(first, count), :, pl.ds(t * LANES, LANES)],
                field.at[pl.ds(base, count), t, pl.ds(PAD + REACH, lon), :], sems.at[t]))
        if not started:
            self.each(lambda copy: copy.start())

    def each(self, act):
        @pl.when(self.polar)
        def _():
            for copy in self.smooth:
                act(copy)

        @pl.when(jnp.logical_not(self.polar))
        def _():
            for copy in self.plain:
                act(copy)

    def wait(self):
        field, base, first, count, lon = self.place
        edge_w_ref, edge_e_ref = self.edges

        @pl.when(jnp.logical_not(self.polar))
        def _():
            @pl.loop(0, count)
            def _(r):
                for t in range(field.shape[1]):
                    lanes = pl.ds(t * LANES, LANES)
                    field[base + r, t, pl.ds(PAD, REACH), :] = edge_w_ref[first + r, :, lanes].astype(jnp.float32)
                    field[base + r, t, pl.ds(PAD + REACH + lon, REACH), :] = edge_e_ref[first + r, :, lanes].astype(jnp.float32)

        self.each(lambda copy: copy.wait())


def strip(field, base, ext):
    return field.at[pl.ds(base, HALO), :, pl.ds(PAD, ext), :]


def winds_beyond(copies, origin, refs, winds, row):
    return [copies.one_of(origin, [ref.at[HALO, :, pl.ds(i * LANES, LANES)] for ref in refs], winds.at[row + i]) for i in range(2)]


def on_side(info_ref, outer, body):
    @pl.when(info_ref[LOW_HALF] == 1)
    def _():
        body(not outer)

    @pl.when(info_ref[LOW_HALF] == 0)
    def _():
        body(outer)


def border_kernel(outer, rows, lon, ext, info_ref, state_ref, edge_w_ref, edge_e_ref, winds_ref, late_ref, raw_ref, across_ref,
                  near_ref, far_ref, border_ref, level_ref, one_ref, field_a, field_b, halo_rows, winds, own_sem, sems):
    zero = info_ref[ZERO]
    origin, origins = info_ref[OUTER_FROM if outer else INNER_FROM], (late_ref, raw_ref, across_ref)

    def store_both(r, t, c, count, value):
        level_ref[r, t, pl.ds(c, count), :] = value
        border_ref[r, pl.ds(c, count), pl.ds(t * LANES, LANES)] = value.astype(jnp.bfloat16)

    def body(north):
        halo, own, first = (2 * HALO, 0, rows - 2 * HALO) if north else (0, HALO, 0)
        parts = ((far_ref, 0), (near_ref, 0)) if north else ((near_ref, 0), (far_ref, 0))
        copies = Copies(sems)
        halo_copy = copies.one_of(origin, [ref.at[pl.ds(0, HALO)] for ref in origins], halo_rows)
        mine = OwnRows(info_ref[POLAR] == 1, lon, ext, state_ref, edge_w_ref, edge_e_ref, parts, field_a, own, first, own_sem)
        wind_copies = [
            copies.start(winds_ref.at[pl.ds(first + 2 if north else 0, HALO + 2)], winds.at[pl.ds(0 if north else 2, HALO + 2)]),
            *winds_beyond(copies, origin, origins, winds, HALO + 2 if north else 0),
        ]
        halo_copy.wait()
        put_rows(field_a, halo_rows, halo, HALO, ext)
        mine.wait()
        for copy in wind_copies:
            copy.wait()

    def pass_on(north):
        pltpu.make_async_copy(strip(field_b, 0 if north else HALO, ext), one_ref, sems.at[4]).start()

    on_side(info_ref, outer, body)
    step_rows(field_a, winds, zero, 0, 2 * HALO, 0, 0, ext, store_in(field_b))
    on_side(info_ref, outer, pass_on)
    step_rows(field_b, winds, zero, 0, HALO, 2, 0, ext, store_both)
    pltpu.make_async_copy(strip(field_b, 0, ext), one_ref, sems.at[4]).wait()


def border_rows(outer, info, state, edges, winds, origins, near, far):
    rows, lon, channels = state.shape
    ext = winds.shape[1]
    tiles = channels // LANES
    vmem, hbm = pl.BlockSpec(memory_space=pltpu.VMEM), pl.BlockSpec(memory_space=pl.ANY)
    level = jax.ShapeDtypeStruct((HALO, tiles, ext, LANES), jnp.float32)
    return pl.pallas_call(
        functools.partial(border_kernel, outer, rows, lon, ext),
        in_specs=[pl.BlockSpec(memory_space=pltpu.SMEM), hbm, vmem, vmem] + [hbm] * 6,
        out_specs=[vmem, vmem, hbm],
        out_shape=[jax.ShapeDtypeStruct((HALO, ext, channels), jnp.bfloat16), level, level],
        scratch_shapes=[
            cells_of(3 * HALO, tiles, ext), cells_of(2 * HALO, tiles, ext),
            half_of(HALO, ext, channels), half_of(2 * HALO, ext, LANES),
            pltpu.SemaphoreType.DMA((2,)), pltpu.SemaphoreType.DMA((5,)),
        ],
        compiler_params=pltpu.CompilerParams(vmem_limit_bytes=20 * MIB),
        cost_estimate=pl.CostEstimate(flops=1000, bytes_accessed=1000, transcendentals=0),
        name="border_outer" if outer else "border_inner",
    )(info, state, *edges, winds, *origins, near, far)


def interior_kernel(rows, lon, ext, info_ref, state_ref, edge_w_ref, edge_e_ref, winds_ref, level_o_ref, level_i_ref,
                    one_o_ref, one_i_ref, smooth_o_ref, smooth_i_ref, out_ref, third_o_ref, third_i_ref,
                    field_a, field_b, field_c, part_ref, winds, sem, in_sem, out_sem):
    inner = rows - 4
    zero, low_half = info_ref[ZERO], info_ref[LOW_HALF] == 1

    def start(south, north):
        OwnRows(info_ref[POLAR] == 1, lon, ext, state_ref, edge_w_ref, edge_e_ref,
                ((south[0], 0), (north[0], 0)), field_a, 0, HALO, sem)
        copies = Copies(in_sem)
        copies.start(winds_ref.at[pl.ds(2, inner)], winds)
        for one, two, at_one, at_two in ((south[1], south[2], 0, 0), (north[1], north[2], inner - HALO, rows - HALO)):
            copies.start(one, strip(field_b, at_one, ext))
            copies.start(two, strip(field_c, at_two, ext))

    outer_refs, inner_refs = (smooth_o_ref, one_o_ref, level_o_ref), (smooth_i_ref, one_i_ref, level_i_ref)

    @pl.when(low_half)
    def _():
        start(outer_refs, inner_refs)

    @pl.when(jnp.logical_not(low_half))
    def _():
        start(inner_refs, outer_refs)

    OwnRows(info_ref[POLAR] == 1, lon, ext, state_ref, edge_w_ref, edge_e_ref,
            ((smooth_o_ref, 0), (smooth_i_ref, 0)), field_a, 0, HALO, sem, started=True).wait()
    pltpu.make_async_copy(winds_ref.at[pl.ds(2, inner)], winds, in_sem.at[0]).wait()

    def store(r, t, c, count, value):
        field_b[HALO + r, t, pl.ds(PAD + c, count), :] = value

    step_rows(field_a, winds, zero, 0, inner - 2 * HALO, HALO, 0, ext, store)
    for i in range(4):
        pltpu.make_async_copy(one_o_ref, strip(field_b, 0, ext), in_sem.at[1 + i]).wait()

    def store(r, t, c, count, value):
        field_c[HALO + r, t, pl.ds(PAD + c, count), :] = value

    step_rows(field_b, winds, zero, 0, inner - 4, 2, 0, ext, store)
    step_rows(field_c, winds, zero, 0, inner, 0, 0, ext, store_in(field_b))

    def hand_on(south_ref, north_ref):
        for i, (ref, base) in enumerate(((south_ref, 0), (north_ref, inner - HALO))):
            pltpu.make_async_copy(strip(field_b, base, ext), ref, out_sem.at[i]).start()

    @pl.when(low_half)
    def _():
        hand_on(third_o_ref, third_i_ref)

    @pl.when(jnp.logical_not(low_half))
    def _():
        hand_on(third_i_ref, third_o_ref)

    half = (rows - 2 * HALO) // 2
    results = []
    for i in range(2):
        step_rows(field_b, winds, zero, i * half, (i + 1) * half, 2, REACH, REACH + lon, store_out(part_ref))
        results.append(pltpu.make_async_copy(
            part_ref.at[pl.ds(i * half, half)], out_ref.at[pl.ds(HALO + i * half, half)], out_sem.at[2 + i]))
        results[i].start()
    for i in range(2):
        pltpu.make_async_copy(strip(field_b, 0, ext), third_o_ref, out_sem.at[i]).wait()
    for copy in results:
        copy.wait()


def interior(info, state, edges, winds, levels, ones, smooths):
    rows, lon, channels = state.shape
    ext = winds.shape[1]
    tiles = channels // LANES
    vmem, hbm = pl.BlockSpec(memory_space=pltpu.VMEM), pl.BlockSpec(memory_space=pl.ANY)
    third = jax.ShapeDtypeStruct((HALO, tiles, ext, LANES), jnp.float32)
    return pl.pallas_call(
        functools.partial(interior_kernel, rows, lon, ext),
        in_specs=[pl.BlockSpec(memory_space=pltpu.SMEM), hbm, vmem, vmem] + [hbm] * 7,
        out_specs=[hbm, hbm, hbm],
        out_shape=[jax.ShapeDtypeStruct((rows, lon, channels), jnp.bfloat16), third, third],
        scratch_shapes=[
            cells_of(rows - 2 * HALO, tiles, ext), cells_of(rows - 4, tiles, ext), cells_of(rows, tiles, ext),
            half_of(rows - 2 * HALO, lon, channels), half_of(rows - 4, ext, LANES),
            pltpu.SemaphoreType.DMA((2,)), pltpu.SemaphoreType.DMA((5,)), pltpu.SemaphoreType.DMA((4,)),
        ],
        compiler_params=pltpu.CompilerParams(vmem_limit_bytes=24 * MIB),
        cost_estimate=pl.CostEstimate(flops=1000, bytes_accessed=1000, transcendentals=0),
        name="interior",
    )(info, state, *edges, winds, *levels, *ones, *smooths)


def finish_kernel(outer, rows, lon, ext, _, info_ref, winds_ref, late_ref, raw_ref, across_raw_ref, border_ref, across_ref, level_ref, third_ref,
                  out_ref, near, last, winds, halo_rows, part_ref, in_sem, out_sem):
    zero = info_ref[ZERO]

    def body(north):
        mine, other = (0, HALO) if north else (HALO, 0)
        copies = Copies(in_sem)
        origin = info_ref[OUTER_FROM if outer else INNER_FROM]
        halo_copy = copies.one_of(origin, (border_ref, border_ref, across_ref), halo_rows)
        incoming = [
            copies.start(level_ref, strip(near, mine, ext)),
            copies.start(third_ref, strip(last, mine, ext)),
            copies.start(winds_ref.at[pl.ds(rows - HALO if north else 0, HALO)], winds.at[pl.ds(0 if north else 2, HALO)]),
            *winds_beyond(copies, origin, (late_ref, raw_ref, across_raw_ref), winds, HALO if north else 0),
        ]
        halo_copy.wait()
        put_rows(near, halo_rows, other, HALO, ext)
        for copy in incoming:
            copy.wait()

        def store(r, t, c, count, value):
            last[r + other, t, pl.ds(PAD + c, count), :] = value

        step_rows(near, winds, zero, 0, HALO, 2 if north else 0, 0, ext, store)
        results, half = [], HALO // 2
        for i in range(2):
            step_rows(last, winds, zero, i * half, (i + 1) * half, 0 if north else 2, REACH, REACH + lon, store_out(part_ref))
            place = out_ref.at[pl.ds((rows - HALO if north else 0) + i * half, half)]
            results.append(pltpu.make_async_copy(part_ref.at[pl.ds(i * half, half)], place, out_sem.at[i]))
            results[i].start()
        for copy in results:
            copy.wait()

    on_side(info_ref, outer, body)


def finish(outer, info, out, winds, origins, border, across, level, third):
    rows, lon, channels = out.shape
    ext = winds.shape[1]
    tiles = channels // LANES
    hbm = pl.BlockSpec(memory_space=pl.ANY)
    return pl.pallas_call(
        functools.partial(finish_kernel, outer, rows, lon, ext),
        in_specs=[hbm, pl.BlockSpec(memory_space=pltpu.SMEM)] + [hbm] * 8,
        out_specs=hbm,
        out_shape=jax.ShapeDtypeStruct(out.shape, out.dtype),
        input_output_aliases={0: 0},
        scratch_shapes=[
            cells_of(2 * HALO, tiles, ext), cells_of(2 * HALO, tiles, ext),
            half_of(HALO + 2, ext, LANES), half_of(HALO, ext, channels), half_of(HALO, lon, channels),
            pltpu.SemaphoreType.DMA((6,)),
            pltpu.SemaphoreType.DMA((2,)),
        ],
        compiler_params=pltpu.CompilerParams(vmem_limit_bytes=16 * MIB),
        cost_estimate=pl.CostEstimate(flops=1000, bytes_accessed=1000, transcendentals=0),
        name="finish_outer" if outer else "finish_inner",
    )(out, info, winds, *origins, border, across, level, third)


def half_of(rows, ext, channels):
    return pltpu.VMEM((rows, ext, channels), jnp.bfloat16)


def cells_of(rows, tiles, ext):
    return pltpu.VMEM((rows, tiles, ext + 2 * PAD, LANES), jnp.float32)


def per_device(state, winds, decay, widths):
    rows, lon, channels = state.shape
    fields = decay.shape[0]
    bands, tiles = lax.axis_size("lat"), lax.axis_size("lon")
    lat, lon_at = lax.axis_index("lat"), lax.axis_index("lon")
    quarter = bands // 4
    ext = round_up(lon + 2 * REACH, 16)
    fill = ext - lon - 2 * REACH
    axes = ("lat", "lon")

    middle = bands // 2

    def is_polar(band):
        return band < quarter or band >= bands - quarter

    def is_plain(band):
        return not is_polar(band)

    def inward(band):
        return band + 1 if band < middle else band - 1

    def outward(band):
        return band - 1 if band < middle else band + 1

    def over_lon(flip):
        return [(b * tiles + l, b * tiles + (l ^ flip)) for b in range(bands) if is_polar(b) for l in range(tiles)]

    def over_lat(to, wanted=lambda band: True):
        return [(b * tiles + l, to(b) * tiles + l) for b in range(bands)
                if wanted(b) and 0 <= to(b) < bands and (to(b) < middle) == (b < middle) for l in range(tiles)]

    across = [(b * tiles + l, inward(b) * tiles + l) for b in (middle - 1, middle) for l in range(tiles)]

    def move(cells, pairs):
        return lax.ppermute(cells, axes, pairs)

    low_half = lat < middle
    at_middle = (lat == middle - 1) | (lat == middle)
    polar = (lat < quarter) | (lat >= bands - quarter)
    outer_from = jnp.where((lat <= quarter) | (lat >= bands - quarter - 1), 0, 1)
    inner_from = jnp.where((lat < quarter - 1) | (lat > bands - quarter), 0, jnp.where(at_middle, 2, 1))
    numbers = [lon_at % 2, polar, outer_from, inner_from, lat < 0, low_half]
    info = jnp.stack([jnp.asarray(n, jnp.int32) for n in numbers])

    count = HALO
    starts = [jnp.where(low_half, f, rows - count - f) for f in (0, rows - count, count, rows - 2 * count)]

    def rows_of(values, i):
        return lax.dynamic_slice_in_dim(values, starts[i], count)

    def ordered(values):
        return jnp.concatenate([rows_of(values, i) for i in range(len(starts))], axis=0)

    def joined(cells, cols):
        return jnp.concatenate([cells.astype(jnp.bfloat16), winds[:, cols]], axis=2)

    east = [(l, (l + 1) % tiles) for l in range(tiles)]
    west = [((l + 1) % tiles, l) for l in range(tiles)]
    first, last = slice(0, REACH), slice(lon - REACH, lon)
    head, rear = tie(state[:, first], state[:, last])
    head, rear, cells = tie(joined(head, first), joined(rear, last), state)
    from_east = lax.ppermute(head, "lon", west)
    from_west = lax.ppermute(rear, "lon", east)

    opp = [None] * len(starts)
    circles = [rows_of(cells, 0).astype(jnp.bfloat16)]
    circles[0], cells = tie(circles[0], cells)
    opp[0] = move(circles[0], over_lon(2))
    circles += [rows_of(cells, i).astype(jnp.bfloat16) for i in range(1, len(starts))]

    edge_w, edge_e = from_west[:, :, :channels], from_east[:, :, :channels]

    def extend(inner, before, after):
        parts = [before, inner, after, jnp.zeros((inner.shape[0], fill, inner.shape[2]), inner.dtype)]
        return jnp.concatenate(parts, axis=1)

    winds_ext = extend(winds, from_west[:, :, channels:], from_east[:, :, channels:])

    def border(i, wind_first):
        wind = lax.dynamic_slice_in_dim(winds_ext, wind_first, 2)
        ends = extend(rows_of(cells, i).astype(jnp.bfloat16), rows_of(edge_w, i), rows_of(edge_e, i))
        return jnp.concatenate([ends, jnp.concatenate([wind[:1], wind[1:]], axis=2)], axis=0)

    outer_rows = border(0, jnp.where(low_half, 0, rows - 2))
    inner_rows = border(1, jnp.where(low_half, rows - 2, 0))
    raw_out = move(outer_rows, over_lat(outward, is_plain))
    raw_in = move(inner_rows, over_lat(inward, is_plain))
    raw_across = move(inner_rows, across)
    behind = outer_rows[HALO:], inner_rows[HALO:]

    circles[1], outer_rows = tie(circles[1], outer_rows)
    sib = move(jnp.concatenate(circles[:2], axis=0), over_lon(1))
    opp[1] = move(circles[1], over_lon(2))

    own_widths = ordered(lax.dynamic_slice_in_dim(widths, lat * rows, rows))
    rate = jnp.repeat(decay, channels // fields)[None, :]
    reach = own_widths.astype(jnp.float32)[:, None]
    q = jnp.exp(-rate)
    back = round_up(HMAX + 1 + REACH, 8)
    seg = max(back + ext - REACH, round_up(ext + HMAX + 1, 8)) // 8
    carry = jnp.exp(-rate * seg)
    far = jnp.exp(-rate * (reach + 1.0))[:, None, :]
    total = (-jnp.expm1(-rate * (reach + 1.0)) - q * jnp.expm1(-rate * reach)) / -jnp.expm1(-rate)
    scale = (1.0 / total)[:, None, :]

    edges = edge_w, edge_e
    smooths, late = [], []

    def smoothed(i, place, own, sib, opp, diag):
        return smooth_piece(i, place, count, ext, info, own_widths, own, sib, opp, diag, q, carry, far, scale, behind[i:i + 1])

    for i in range(2):
        if i == 0:
            opp[0], last_two = tie(opp[0], jnp.concatenate(circles[2:], axis=0))
            last_opp = move(last_two, over_lon(2))
        diag = move(opp[i], over_lon(1))
        smooth, ends = smoothed(i, 0, circles[i], sib, opp[i], diag)
        smooths.append(smooth)
        if i == 1:
            ends, raw_out = tie(ends, raw_out)
        late.append(move(ends, over_lat((outward, inward)[i], is_polar)))
        if i == 0:
            smooth, opp[1] = tie(smooth, opp[1])
        else:
            smooth, last_opp = tie(smooth, last_opp)

    last_opp, late[0], late[1], raw_in = tie(last_opp, late[0], late[1], raw_in)
    last_sib = move(last_two, over_lon(1))
    diag = move(last_opp, over_lon(1))
    smooths += smoothed(2, 0, last_two, last_sib, last_opp, diag)
    outer_rows, level_o, one_o = border_rows(
        True, info, state, edges, winds_ext, (late[1], raw_in, raw_in), smooths[0], smooths[2])
    going_out = move(outer_rows, over_lat(outward))
    smooths += smoothed(3, 1, last_two, last_sib, last_opp, diag)
    inner_origins, outer_origins = (late[0], raw_out, raw_across), (late[1], raw_in, raw_in)
    inner_rows, level_i, one_i = border_rows(
        False, info, state, edges, winds_ext, inner_origins, smooths[1], smooths[3])
    going_in = move(inner_rows, over_lat(inward))
    going_across = move(inner_rows, across)
    out, third_o, third_i = interior(info, state, edges, winds_ext, (level_o, level_i), (one_o, one_i), smooths[2:])
    out = finish(False, info, out, winds_ext, inner_origins, going_out, going_across, level_i, third_i)
    return finish(True, info, out, winds_ext, outer_origins, going_in, going_in, level_o, third_o)


def solution(mesh):
    in_specs = (P("lat", "lon", None), P("lat", "lon", None), P(), P())
    out_specs = P("lat", "lon", None)
    return jax.shard_map(
        per_device, mesh=mesh, in_specs=in_specs, out_specs=out_specs, check_vma=False
    )
```

```python
import functools

import jax
import jax.numpy as jnp
from jax import lax
from jax.experimental import pallas as pl
from jax.experimental.pallas import tpu as pltpu
from jax.sharding import PartitionSpec as P

ADV_STEPS = 4
REACH = 2 * ADV_STEPS
ROUND = 2
HALO = 2 * ROUND
HMAX = 480
LANES = 128
MIB = 1024 * 1024
ODD, POLAR, OUTER_FROM, INNER_FROM, ZERO, LOW_HALF = range(6)
PAD = 8
COLS = 32


def tie(*values):
    return lax.optimization_barrier(values)


def round_up(value, unit):
    return -(-value // unit) * unit


def smooth_kernel(geo, sends, info_ref, widths_ref, own_ref, sib_ref, opp_ref, *refs):
    diag_ref, refs = refs[0], refs[1:]
    ins, extra_refs, outs, scratch = refs[:4], refs[4:4 + sends], refs[4 + sends:5 + 2 * sends], refs[5 + 2 * sends:]
    ins = (own_ref, sib_ref, opp_ref, diag_ref) + ins

    @pl.when(info_ref[POLAR] == 1)
    def _():
        smooth_rows(geo, info_ref[ODD] == 1, widths_ref, *ins, *outs[:1], outs[1:], *scratch)
        for ref, extra_ref in zip(outs[1:], extra_refs):
            ref[HALO] = extra_ref[0]


def smooth_rows(geo, odd, widths_ref, own_ref, sib_ref, opp_ref, diag_ref, q_ref, carry_ref, far_ref, scale_ref,
                level_ref, border_refs, cells, east_sum, west_sum):
    lon, back, span, seg, ext = geo
    rows, tiles = own_ref.shape[0], own_ref.shape[2] // LANES
    chains = [(r, t) for r in range(rows) for t in range(tiles)]

    def put(ref, start, begin, count):
        @pl.loop(0, rows)
        def _(r):
            for t in range(tiles):
                part = ref[r, pl.ds(begin, count), pl.ds(t * LANES, LANES)]
                cells[r * tiles + t, pl.ds(start, count), :] = part.astype(jnp.float32)

    head = back - lon
    put(opp_ref, 0, lon - head, head)
    put(own_ref, back, 0, lon)
    put(opp_ref, back + 2 * lon, 0, span - REACH - 2 * lon)

    @pl.when(odd)
    def _():
        put(sib_ref, back - lon, 0, lon)
        put(diag_ref, back + lon, 0, lon)

    @pl.when(jnp.logical_not(odd))
    def _():
        put(diag_ref, back - lon, 0, lon)
        put(sib_ref, back + lon, 0, lon)

    q = [jnp.broadcast_to(q_ref[0:1, t * LANES:(t + 1) * LANES], (8, LANES)) for t in range(tiles)]
    jump = [carry_ref[0:1, t * LANES:(t + 1) * LANES] for t in range(tiles)]
    zero = jnp.zeros((8, LANES), jnp.float32)
    none = jnp.zeros((1, LANES), jnp.float32)
    east_base = back - REACH

    for base, total, forward in ((east_base, east_sum, False), (0, west_sum, True)):
        def at(i, forward=forward):
            return i if forward else seg - 1 - i

        def totals(i, acc, base=base):
            return tuple(cells[r * tiles + t, pl.ds(base + at(i), 8, stride=seg), :] + q[t] * acc[n]
                         for n, (r, t) in enumerate(chains))

        acc = lax.fori_loop(0, seg, totals, (zero,) * len(chains), unroll=4)
        start = []
        for n, (r, t) in enumerate(chains):
            carry = none
            parts = [None] * 8
            for k in (range(8) if forward else range(7, -1, -1)):
                parts[k] = carry
                carry = acc[n][k:k + 1] + jump[t] * carry
            start.append(jnp.concatenate(parts, axis=0))

        def sums(i, acc, base=base, total=total):
            new = []
            for n, (r, t) in enumerate(chains):
                v = cells[r * tiles + t, pl.ds(base + at(i), 8, stride=seg), :] + q[t] * acc[n]
                total[r * tiles + t, pl.ds(at(i), 8, stride=seg), :] = v
                new.append(v)
            return tuple(new)

        lax.fori_loop(0, seg, sums, tuple(start), unroll=4)

    step = COLS

    def one_row(r, border_ref, border_row):
        width = widths_ref[r]
        for t in range(tiles):
            n = r * tiles + t
            far = jnp.broadcast_to(far_ref[r, 0:1, t * LANES:(t + 1) * LANES], (step, LANES))
            scale = jnp.broadcast_to(scale_ref[r, 0:1, t * LANES:(t + 1) * LANES], (step, LANES))
            for c in range(0, ext, step):
                near = east_sum[n, pl.ds(c, step), :] + west_sum[n, pl.ds(back - REACH + c, step), :]
                cut = east_sum[n, pl.ds(c + 1 + width, step), :] + west_sum[n, pl.ds(back - REACH + c - 1 - width, step), :]
                mid = cells[n, pl.ds(back - REACH + c, step), :]
                value = ((near - mid - far * cut) * scale).astype(jnp.bfloat16)
                level_ref[r, t, pl.ds(c, step), :] = value.astype(jnp.float32)
                if border_ref is not None:
                    border_ref[border_row, pl.ds(c, step), pl.ds(t * LANES, LANES)] = value

    @pl.loop(0, rows)
    def _(r):
        one_row(r, border_refs[0] if border_refs else None, r)


def smooth_piece(piece, place, rows, ext, info, widths, own, sib, opp, diag, q, carry, far, scale, extras):
    lon, channels = own.shape[1:]
    tiles = channels // LANES
    back = round_up(HMAX + 1 + REACH, 8)
    span = round_up(ext + HMAX + 1, 8)
    seg = max(back + ext - REACH, span) // 8
    geo = (lon, back, 8 * seg, seg, ext)
    smem, vmem = pl.BlockSpec(memory_space=pltpu.SMEM), pl.BlockSpec(memory_space=pltpu.VMEM)
    pair = pl.BlockSpec((rows, lon, channels), lambda i: (piece % 2, 0, 0))
    part = pl.BlockSpec((rows, lon, channels), lambda i: (place, 0, 0))
    table = pl.BlockSpec((rows, 1, channels), lambda i: (piece, 0, 0))
    border = jax.ShapeDtypeStruct((HALO + 1, ext, channels), jnp.bfloat16)
    of_rows = slice(piece * rows, (piece + 1) * rows)
    return pl.pallas_call(
        functools.partial(smooth_kernel, geo, len(extras)),
        grid=(1,),
        in_specs=[smem, smem, part, pair, part, part, vmem, vmem, table, table] + [vmem] * len(extras),
        out_specs=[vmem] * (1 + len(extras)),
        out_shape=[jax.ShapeDtypeStruct((rows, tiles, ext, LANES), jnp.float32)] + [border] * len(extras),
        scratch_shapes=[
            pltpu.VMEM((rows * tiles, back - REACH + 8 * seg, LANES), jnp.float32),
            pltpu.VMEM((rows * tiles, 8 * seg, LANES), jnp.float32),
            pltpu.VMEM((rows * tiles, 8 * seg, LANES), jnp.float32),
        ],
        compiler_params=pltpu.CompilerParams(vmem_limit_bytes=28 * MIB),
        cost_estimate=pl.CostEstimate(flops=1000, bytes_accessed=1000, transcendentals=0),
        name="smooth",
    )(info, widths[of_rows], own, sib, opp, diag, q, carry, far, scale, *extras)


def update(src, r, t, c, count, u, v, zero):
    def at(dr, dc):
        return src[r + dr, t, pl.ds(PAD + c + dc + (zero if dc else 0), count), :]

    mid = at(0, 0)
    mid30 = 30.0 * mid
    e1, w1, e2, w2 = at(0, 1), at(0, -1), at(0, 2), at(0, -2)
    n1, s1, n2, s2 = at(1, 0), at(-1, 0), at(2, 0), at(-2, 0)
    first_x = (e2 - w2) - 8.0 * (e1 - w1)
    second_x = 16.0 * (e1 + w1) - (e2 + w2) - mid30
    first_y = (n2 - s2) - 8.0 * (n1 - s1)
    second_y = 16.0 * (n1 + s1) - (n2 + s2) - mid30
    change = u * (first_x + (6.0 * u) * second_x) + v * (first_y + (6.0 * v) * second_y)
    return mid + change


def put_rows(field, ref, base, count, ext):
    @pl.loop(0, count)
    def _(r):
        for t in range(field.shape[1]):
            field[base + r, t, pl.ds(PAD, ext), :] = ref[r, :, pl.ds(t * LANES, LANES)].astype(jnp.float32)


def step_rows(source, winds, zero, first, last, offset, start, stop, store):
    half = LANES // 2
    eastward = lax.broadcasted_iota(jnp.int32, (COLS, LANES), 1) < half

    @pl.loop(first, last)
    def _(r):
        for c in range(start, stop, COLS):
            count = min(COLS, stop - c)
            both = winds[r + offset, pl.ds(c, count), :].astype(jnp.float32) * (1.0 / 12.0)
            swapped = pltpu.roll(both, half, 1)
            u = jnp.where(eastward[:count], both, swapped)
            v = jnp.where(eastward[:count], swapped, both)
            for t in range(source.shape[1]):
                store(r, t, c, count, update(source, r + 2, t, c, count, u, v, zero))


class Copies:
    def __init__(self, sems):
        self.sems, self.used = sems, 0

    def start(self, source, target):
        copy = pltpu.make_async_copy(source, target, self.sems.at[self.used])
        self.used += 1
        copy.start()
        return copy

    def one_of(self, choice, sources, target):
        sem = self.sems.at[self.used]
        self.used += 1
        for i, source in enumerate(sources):
            @pl.when(choice == i)
            def _(source=source):
                pltpu.make_async_copy(source, target, sem).start()

        return pltpu.make_async_copy(sources[0], target, sem)


def store_in(field):
    def store(r, t, c, count, value):
        field[r, t, pl.ds(PAD + c, count), :] = value

    return store


def store_out(ref):
    def store(r, t, c, count, value):
        ref[r, pl.ds(c - REACH, count), pl.ds(t * LANES, LANES)] = value.astype(jnp.bfloat16)

    return store


class OwnRows:
    def __init__(self, polar, lon, ext, state_ref, edge_w_ref, edge_e_ref, parts, field, base, first, sems, started=False):
        tiles, count = field.shape[1], HALO * len(parts)
        self.polar, self.edges = polar, (edge_w_ref, edge_e_ref)
        self.place = (field, base, first, count, lon)
        self.smooth, self.plain = [], []
        for i, (ref, start) in enumerate(parts):
            target = field.at[pl.ds(base + i * HALO, HALO), :, pl.ds(PAD, ext), :]
            self.smooth.append(pltpu.make_async_copy(ref.at[pl.ds(start, HALO)], target, sems.at[i]))
        for t in range(tiles):
            self.plain.append(pltpu.make_async_copy(
                state_ref.at[pl.ds(first, count), :, pl.ds(t * LANES, LANES)],
                field.at[pl.ds(base, count), t, pl.ds(PAD + REACH, lon), :], sems.at[t]))
        if not started:
            self.each(lambda copy: copy.start())

    def each(self, act):
        @pl.when(self.polar)
        def _():
            for copy in self.smooth:
                act(copy)

        @pl.when(jnp.logical_not(self.polar))
        def _():
            for copy in self.plain:
                act(copy)

    def wait(self):
        field, base, first, count, lon = self.place
        edge_w_ref, edge_e_ref = self.edges

        @pl.when(jnp.logical_not(self.polar))
        def _():
            @pl.loop(0, count)
            def _(r):
                for t in range(field.shape[1]):
                    lanes = pl.ds(t * LANES, LANES)
                    field[base + r, t, pl.ds(PAD, REACH), :] = edge_w_ref[first + r, :, lanes].astype(jnp.float32)
                    field[base + r, t, pl.ds(PAD + REACH + lon, REACH), :] = edge_e_ref[first + r, :, lanes].astype(jnp.float32)

        self.each(lambda copy: copy.wait())


def strip(field, base, ext):
    return field.at[pl.ds(base, HALO), :, pl.ds(PAD, ext), :]


def winds_beyond(copies, origin, refs, winds, row):
    return [copies.one_of(origin, [ref.at[HALO, :, pl.ds(i * LANES, LANES)] for ref in refs], winds.at[row + i]) for i in range(2)]


def on_side(info_ref, outer, body):
    @pl.when(info_ref[LOW_HALF] == 1)
    def _():
        body(not outer)

    @pl.when(info_ref[LOW_HALF] == 0)
    def _():
        body(outer)


def border_kernel(outer, rows, lon, ext, info_ref, state_ref, edge_w_ref, edge_e_ref, winds_ref, late_ref, raw_ref, across_ref,
                  near_ref, far_ref, border_ref, level_ref, one_ref, field_a, field_b, halo_rows, winds, own_sem, sems):
    zero = info_ref[ZERO]
    origin, origins = info_ref[OUTER_FROM if outer else INNER_FROM], (late_ref, raw_ref, across_ref)

    def store_both(r, t, c, count, value):
        level_ref[r, t, pl.ds(c, count), :] = value
        border_ref[r, pl.ds(c, count), pl.ds(t * LANES, LANES)] = value.astype(jnp.bfloat16)

    def body(north):
        halo, own, first = (2 * HALO, 0, rows - 2 * HALO) if north else (0, HALO, 0)
        parts = ((far_ref, 0), (near_ref, 0)) if north else ((near_ref, 0), (far_ref, 0))
        copies = Copies(sems)
        halo_copy = copies.one_of(origin, [ref.at[pl.ds(0, HALO)] for ref in origins], halo_rows)
        mine = OwnRows(info_ref[POLAR] == 1, lon, ext, state_ref, edge_w_ref, edge_e_ref, parts, field_a, own, first, own_sem)
        wind_copies = [
            copies.start(winds_ref.at[pl.ds(first + 2 if north else 0, HALO + 2)], winds.at[pl.ds(0 if north else 2, HALO + 2)]),
            *winds_beyond(copies, origin, origins, winds, HALO + 2 if north else 0),
        ]
        halo_copy.wait()
        put_rows(field_a, halo_rows, halo, HALO, ext)
        mine.wait()
        for copy in wind_copies:
            copy.wait()

    def pass_on(north):
        pltpu.make_async_copy(strip(field_b, 0 if north else HALO, ext), one_ref, sems.at[4]).start()

    on_side(info_ref, outer, body)
    step_rows(field_a, winds, zero, 0, 2 * HALO, 0, 0, ext, store_in(field_b))
    on_side(info_ref, outer, pass_on)
    step_rows(field_b, winds, zero, 0, HALO, 2, 0, ext, store_both)
    pltpu.make_async_copy(strip(field_b, 0, ext), one_ref, sems.at[4]).wait()


def border_rows(outer, info, state, edges, winds, origins, near, far):
    rows, lon, channels = state.shape
    ext = winds.shape[1]
    tiles = channels // LANES
    vmem, hbm = pl.BlockSpec(memory_space=pltpu.VMEM), pl.BlockSpec(memory_space=pl.ANY)
    level = jax.ShapeDtypeStruct((HALO, tiles, ext, LANES), jnp.float32)
    return pl.pallas_call(
        functools.partial(border_kernel, outer, rows, lon, ext),
        in_specs=[pl.BlockSpec(memory_space=pltpu.SMEM), hbm, vmem, vmem] + [hbm] * 6,
        out_specs=[vmem, vmem, hbm],
        out_shape=[jax.ShapeDtypeStruct((HALO, ext, channels), jnp.bfloat16), level, level],
        scratch_shapes=[
            cells_of(3 * HALO, tiles, ext), cells_of(2 * HALO, tiles, ext),
            half_of(HALO, ext, channels), half_of(2 * HALO, ext, LANES),
            pltpu.SemaphoreType.DMA((2,)), pltpu.SemaphoreType.DMA((5,)),
        ],
        compiler_params=pltpu.CompilerParams(vmem_limit_bytes=20 * MIB),
        cost_estimate=pl.CostEstimate(flops=1000, bytes_accessed=1000, transcendentals=0),
        name="border_outer" if outer else "border_inner",
    )(info, state, *edges, winds, *origins, near, far)


def interior_kernel(rows, lon, ext, info_ref, state_ref, edge_w_ref, edge_e_ref, winds_ref, level_o_ref, level_i_ref,
                    one_o_ref, one_i_ref, smooth_o_ref, smooth_i_ref, out_ref, third_o_ref, third_i_ref,
                    field_a, field_b, field_c, part_ref, winds, sem, in_sem, out_sem):
    inner = rows - 4
    zero, low_half = info_ref[ZERO], info_ref[LOW_HALF] == 1

    def start(south, north):
        OwnRows(info_ref[POLAR] == 1, lon, ext, state_ref, edge_w_ref, edge_e_ref,
                ((south[0], 0), (north[0], 0)), field_a, 0, HALO, sem)
        copies = Copies(in_sem)
        copies.start(winds_ref.at[pl.ds(2, inner)], winds)
        for one, two, at_one, at_two in ((south[1], south[2], 0, 0), (north[1], north[2], inner - HALO, rows - HALO)):
            copies.start(one, strip(field_b, at_one, ext))
            copies.start(two, strip(field_c, at_two, ext))

    outer_refs, inner_refs = (smooth_o_ref, one_o_ref, level_o_ref), (smooth_i_ref, one_i_ref, level_i_ref)

    @pl.when(low_half)
    def _():
        start(outer_refs, inner_refs)

    @pl.when(jnp.logical_not(low_half))
    def _():
        start(inner_refs, outer_refs)

    OwnRows(info_ref[POLAR] == 1, lon, ext, state_ref, edge_w_ref, edge_e_ref,
            ((smooth_o_ref, 0), (smooth_i_ref, 0)), field_a, 0, HALO, sem, started=True).wait()
    pltpu.make_async_copy(winds_ref.at[pl.ds(2, inner)], winds, in_sem.at[0]).wait()

    def store(r, t, c, count, value):
        field_b[HALO + r, t, pl.ds(PAD + c, count), :] = value

    step_rows(field_a, winds, zero, 0, inner - 2 * HALO, HALO, 0, ext, store)
    for i in range(4):
        pltpu.make_async_copy(one_o_ref, strip(field_b, 0, ext), in_sem.at[1 + i]).wait()

    def store(r, t, c, count, value):
        field_c[HALO + r, t, pl.ds(PAD + c, count), :] = value

    step_rows(field_b, winds, zero, 0, inner - 4, 2, 0, ext, store)
    step_rows(field_c, winds, zero, 0, inner, 0, 0, ext, store_in(field_b))

    def hand_on(south_ref, north_ref):
        for i, (ref, base) in enumerate(((south_ref, 0), (north_ref, inner - HALO))):
            pltpu.make_async_copy(strip(field_b, base, ext), ref, out_sem.at[i]).start()

    @pl.when(low_half)
    def _():
        hand_on(third_o_ref, third_i_ref)

    @pl.when(jnp.logical_not(low_half))
    def _():
        hand_on(third_i_ref, third_o_ref)

    half = (rows - 2 * HALO) // 2
    results = []
    for i in range(2):
        step_rows(field_b, winds, zero, i * half, (i + 1) * half, 2, REACH, REACH + lon, store_out(part_ref))
        results.append(pltpu.make_async_copy(
            part_ref.at[pl.ds(i * half, half)], out_ref.at[pl.ds(HALO + i * half, half)], out_sem.at[2 + i]))
        results[i].start()
    for i in range(2):
        pltpu.make_async_copy(strip(field_b, 0, ext), third_o_ref, out_sem.at[i]).wait()
    for copy in results:
        copy.wait()


def interior(info, state, edges, winds, levels, ones, smooths):
    rows, lon, channels = state.shape
    ext = winds.shape[1]
    tiles = channels // LANES
    vmem, hbm = pl.BlockSpec(memory_space=pltpu.VMEM), pl.BlockSpec(memory_space=pl.ANY)
    third = jax.ShapeDtypeStruct((HALO, tiles, ext, LANES), jnp.float32)
    return pl.pallas_call(
        functools.partial(interior_kernel, rows, lon, ext),
        in_specs=[pl.BlockSpec(memory_space=pltpu.SMEM), hbm, vmem, vmem] + [hbm] * 7,
        out_specs=[hbm, hbm, hbm],
        out_shape=[jax.ShapeDtypeStruct((rows, lon, channels), jnp.bfloat16), third, third],
        scratch_shapes=[
            cells_of(rows - 2 * HALO, tiles, ext), cells_of(rows - 4, tiles, ext), cells_of(rows, tiles, ext),
            half_of(rows - 2 * HALO, lon, channels), half_of(rows - 4, ext, LANES),
            pltpu.SemaphoreType.DMA((2,)), pltpu.SemaphoreType.DMA((5,)), pltpu.SemaphoreType.DMA((4,)),
        ],
        compiler_params=pltpu.CompilerParams(vmem_limit_bytes=24 * MIB),
        cost_estimate=pl.CostEstimate(flops=1000, bytes_accessed=1000, transcendentals=0),
        name="interior",
    )(info, state, *edges, winds, *levels, *ones, *smooths)


def finish_kernel(outer, rows, lon, ext, _, info_ref, winds_ref, late_ref, raw_ref, across_raw_ref, border_ref, across_ref, level_ref, third_ref,
                  out_ref, near, last, winds, halo_rows, part_ref, in_sem, out_sem):
    zero = info_ref[ZERO]

    def body(north):
        mine, other = (0, HALO) if north else (HALO, 0)
        copies = Copies(in_sem)
        origin = info_ref[OUTER_FROM if outer else INNER_FROM]
        halo_copy = copies.one_of(origin, (border_ref, border_ref, across_ref), halo_rows)
        incoming = [
            copies.start(level_ref, strip(near, mine, ext)),
            copies.start(third_ref, strip(last, mine, ext)),
            copies.start(winds_ref.at[pl.ds(rows - HALO if north else 0, HALO)], winds.at[pl.ds(0 if north else 2, HALO)]),
            *winds_beyond(copies, origin, (late_ref, raw_ref, across_raw_ref), winds, HALO if north else 0),
        ]
        halo_copy.wait()
        put_rows(near, halo_rows, other, HALO, ext)
        for copy in incoming:
            copy.wait()

        def store(r, t, c, count, value):
            last[r + other, t, pl.ds(PAD + c, count), :] = value

        step_rows(near, winds, zero, 0, HALO, 2 if north else 0, 0, ext, store)
        results, half = [], HALO // 2
        for i in range(2):
            step_rows(last, winds, zero, i * half, (i + 1) * half, 0 if north else 2, REACH, REACH + lon, store_out(part_ref))
            place = out_ref.at[pl.ds((rows - HALO if north else 0) + i * half, half)]
            results.append(pltpu.make_async_copy(part_ref.at[pl.ds(i * half, half)], place, out_sem.at[i]))
            results[i].start()
        for copy in results:
            copy.wait()

    on_side(info_ref, outer, body)


def finish(outer, info, out, winds, origins, border, across, level, third):
    rows, lon, channels = out.shape
    ext = winds.shape[1]
    tiles = channels // LANES
    hbm = pl.BlockSpec(memory_space=pl.ANY)
    return pl.pallas_call(
        functools.partial(finish_kernel, outer, rows, lon, ext),
        in_specs=[hbm, pl.BlockSpec(memory_space=pltpu.SMEM)] + [hbm] * 8,
        out_specs=hbm,
        out_shape=jax.ShapeDtypeStruct(out.shape, out.dtype),
        input_output_aliases={0: 0},
        scratch_shapes=[
            cells_of(2 * HALO, tiles, ext), cells_of(2 * HALO, tiles, ext),
            half_of(HALO + 2, ext, LANES), half_of(HALO, ext, channels), half_of(HALO, lon, channels),
            pltpu.SemaphoreType.DMA((6,)),
            pltpu.SemaphoreType.DMA((2,)),
        ],
        compiler_params=pltpu.CompilerParams(vmem_limit_bytes=16 * MIB),
        cost_estimate=pl.CostEstimate(flops=1000, bytes_accessed=1000, transcendentals=0),
        name="finish_outer" if outer else "finish_inner",
    )(out, info, winds, *origins, border, across, level, third)


def half_of(rows, ext, channels):
    return pltpu.VMEM((rows, ext, channels), jnp.bfloat16)


def cells_of(rows, tiles, ext):
    return pltpu.VMEM((rows, tiles, ext + 2 * PAD, LANES), jnp.float32)


def per_device(state, winds, decay, widths):
    rows, lon, channels = state.shape
    fields = decay.shape[0]
    bands, tiles = lax.axis_size("lat"), lax.axis_size("lon")
    lat, lon_at = lax.axis_index("lat"), lax.axis_index("lon")
    quarter = bands // 4
    ext = round_up(lon + 2 * REACH, 16)
    fill = ext - lon - 2 * REACH
    axes = ("lat", "lon")

    middle = bands // 2

    def is_polar(band):
        return band < quarter or band >= bands - quarter

    def is_plain(band):
        return not is_polar(band)

    def inward(band):
        return band + 1 if band < middle else band - 1

    def outward(band):
        return band - 1 if band < middle else band + 1

    def over_lon(flip):
        return [(b * tiles + l, b * tiles + (l ^ flip)) for b in range(bands) if is_polar(b) for l in range(tiles)]

    def over_lat(to, wanted=lambda band: True):
        return [(b * tiles + l, to(b) * tiles + l) for b in range(bands)
                if wanted(b) and 0 <= to(b) < bands and (to(b) < middle) == (b < middle) for l in range(tiles)]

    across = [(b * tiles + l, inward(b) * tiles + l) for b in (middle - 1, middle) for l in range(tiles)]

    def move(cells, pairs):
        return lax.ppermute(cells, axes, pairs)

    low_half = lat < middle
    at_middle = (lat == middle - 1) | (lat == middle)
    polar = (lat < quarter) | (lat >= bands - quarter)
    outer_from = jnp.where((lat <= quarter) | (lat >= bands - quarter - 1), 0, 1)
    inner_from = jnp.where((lat < quarter - 1) | (lat > bands - quarter), 0, jnp.where(at_middle, 2, 1))
    numbers = [lon_at % 2, polar, outer_from, inner_from, lat < 0, low_half]
    info = jnp.stack([jnp.asarray(n, jnp.int32) for n in numbers])

    count = HALO
    starts = [jnp.where(low_half, f, rows - count - f) for f in (0, rows - count, count, rows - 2 * count)]

    def rows_of(values, i):
        return lax.dynamic_slice_in_dim(values, starts[i], count)

    def ordered(values):
        return jnp.concatenate([rows_of(values, i) for i in range(len(starts))], axis=0)

    def joined(cells, cols):
        return jnp.concatenate([cells.astype(jnp.bfloat16), winds[:, cols]], axis=2)

    east = [(l, (l + 1) % tiles) for l in range(tiles)]
    west = [((l + 1) % tiles, l) for l in range(tiles)]
    first, last = slice(0, REACH), slice(lon - REACH, lon)
    head, rear = tie(state[:, first], state[:, last])
    head, rear, cells = tie(joined(head, first), joined(rear, last), state)
    from_east = lax.ppermute(head, "lon", west)
    from_west = lax.ppermute(rear, "lon", east)

    opp = [None] * len(starts)
    circles = [rows_of(cells, 0).astype(jnp.bfloat16)]
    circles[0], cells = tie(circles[0], cells)
    opp[0] = move(circles[0], over_lon(2))
    circles += [rows_of(cells, i).astype(jnp.bfloat16) for i in range(1, len(starts))]

    edge_w, edge_e = from_west[:, :, :channels], from_east[:, :, :channels]

    def extend(inner, before, after):
        parts = [before, inner, after, jnp.zeros((inner.shape[0], fill, inner.shape[2]), inner.dtype)]
        return jnp.concatenate(parts, axis=1)

    winds_ext = extend(winds, from_west[:, :, channels:], from_east[:, :, channels:])

    def border(i, wind_first):
        wind = lax.dynamic_slice_in_dim(winds_ext, wind_first, 2)
        ends = extend(rows_of(cells, i).astype(jnp.bfloat16), rows_of(edge_w, i), rows_of(edge_e, i))
        return jnp.concatenate([ends, jnp.concatenate([wind[:1], wind[1:]], axis=2)], axis=0)

    outer_rows = border(0, jnp.where(low_half, 0, rows - 2))
    inner_rows = border(1, jnp.where(low_half, rows - 2, 0))
    raw_out = move(outer_rows, over_lat(outward, is_plain))
    raw_in = move(inner_rows, over_lat(inward, is_plain))
    raw_across = move(inner_rows, across)
    behind = outer_rows[HALO:], inner_rows[HALO:]

    circles[1], outer_rows = tie(circles[1], outer_rows)
    sib = move(jnp.concatenate(circles[:2], axis=0), over_lon(1))
    opp[1] = move(circles[1], over_lon(2))

    own_widths = ordered(lax.dynamic_slice_in_dim(widths, lat * rows, rows))
    rate = jnp.repeat(decay, channels // fields)[None, :]
    reach = own_widths.astype(jnp.float32)[:, None]
    q = jnp.exp(-rate)
    back = round_up(HMAX + 1 + REACH, 8)
    seg = max(back + ext - REACH, round_up(ext + HMAX + 1, 8)) // 8
    carry = jnp.exp(-rate * seg)
    far = jnp.exp(-rate * (reach + 1.0))[:, None, :]
    total = (-jnp.expm1(-rate * (reach + 1.0)) - q * jnp.expm1(-rate * reach)) / -jnp.expm1(-rate)
    scale = (1.0 / total)[:, None, :]

    edges = edge_w, edge_e
    smooths, late = [], []

    def smoothed(i, place, own, sib, opp, diag):
        return smooth_piece(i, place, count, ext, info, own_widths, own, sib, opp, diag, q, carry, far, scale, behind[i:i + 1])

    for i in range(2):
        if i == 0:
            opp[0], last_two = tie(opp[0], jnp.concatenate(circles[2:], axis=0))
            last_opp = move(last_two, over_lon(2))
        diag = move(opp[i], over_lon(1))
        smooth, ends = smoothed(i, 0, circles[i], sib, opp[i], diag)
        smooths.append(smooth)
        if i == 1:
            ends, raw_out = tie(ends, raw_out)
        late.append(move(ends, over_lat((outward, inward)[i], is_polar)))
        if i == 0:
            smooth, opp[1] = tie(smooth, opp[1])
        else:
            smooth, last_opp = tie(smooth, last_opp)

    last_opp, late[0], late[1], raw_in = tie(last_opp, late[0], late[1], raw_in)
    last_sib = move(last_two, over_lon(1))
    diag = move(last_opp, over_lon(1))
    smooths += smoothed(2, 0, last_two, last_sib, last_opp, diag)
    outer_rows, level_o, one_o = border_rows(
        True, info, state, edges, winds_ext, (late[1], raw_in, raw_in), smooths[0], smooths[2])
    going_out = move(outer_rows, over_lat(outward))
    smooths += smoothed(3, 1, last_two, last_sib, last_opp, diag)
    inner_origins, outer_origins = (late[0], raw_out, raw_across), (late[1], raw_in, raw_in)
    inner_rows, level_i, one_i = border_rows(
        False, info, state, edges, winds_ext, inner_origins, smooths[1], smooths[3])
    going_in = move(inner_rows, over_lat(inward))
    going_across = move(inner_rows, across)
    out, third_o, third_i = interior(info, state, edges, winds_ext, (level_o, level_i), (one_o, one_i), smooths[2:])
    out = finish(False, info, out, winds_ext, inner_origins, going_out, going_across, level_i, third_i)
    return finish(True, info, out, winds_ext, outer_origins, going_in, going_in, level_o, third_o)


def solution(mesh):
    in_specs = (P("lat", "lon", None), P("lat", "lon", None), P(), P())
    out_specs = P("lat", "lon", None)
    return jax.shard_map(
        per_device, mesh=mesh, in_specs=in_specs, out_specs=out_specs, check_vma=False
    )
```

```python
import functools

import jax
import jax.numpy as jnp
from jax import lax
from jax.experimental import pallas as pl
from jax.experimental.pallas import tpu as pltpu
from jax.sharding import PartitionSpec as P

ADV_STEPS = 4
REACH = 2 * ADV_STEPS
ROUND = 2
HALO = 2 * ROUND
HMAX = 480
LANES = 128
MIB = 1024 * 1024
ODD, POLAR, OUTER_FROM, INNER_FROM, ZERO, LOW_HALF = range(6)
PAD = 8
COLS = 48


def tie(*values):
    return lax.optimization_barrier(values)


def round_up(value, unit):
    return -(-value // unit) * unit


def smooth_kernel(geo, sends, info_ref, widths_ref, own_ref, sib_ref, opp_ref, *refs):
    diag_ref, refs = refs[0], refs[1:]
    ins, extra_refs, outs, scratch = refs[:4], refs[4:4 + sends], refs[4 + sends:5 + 2 * sends], refs[5 + 2 * sends:]
    ins = (own_ref, sib_ref, opp_ref, diag_ref) + ins

    @pl.when(info_ref[POLAR] == 1)
    def _():
        smooth_rows(geo, info_ref[ODD] == 1, widths_ref, *ins, *outs[:1], outs[1:], *scratch)
        for ref, extra_ref in zip(outs[1:], extra_refs):
            ref[HALO] = extra_ref[0]


def smooth_rows(geo, odd, widths_ref, own_ref, sib_ref, opp_ref, diag_ref, q_ref, carry_ref, far_ref, scale_ref,
                level_ref, border_refs, cells, east_sum, west_sum):
    lon, back, span, seg, ext = geo
    rows, tiles = own_ref.shape[0], own_ref.shape[2] // LANES
    chains = [(r, t) for r in range(rows) for t in range(tiles)]

    def put(ref, start, begin, count):
        @pl.loop(0, rows)
        def _(r):
            for t in range(tiles):
                part = ref[r, pl.ds(begin, count), pl.ds(t * LANES, LANES)]
                cells[r * tiles + t, pl.ds(start, count), :] = part.astype(jnp.float32)

    head = back - lon
    put(opp_ref, 0, lon - head, head)
    put(own_ref, back, 0, lon)
    put(opp_ref, back + 2 * lon, 0, span - REACH - 2 * lon)

    @pl.when(odd)
    def _():
        put(sib_ref, back - lon, 0, lon)
        put(diag_ref, back + lon, 0, lon)

    @pl.when(jnp.logical_not(odd))
    def _():
        put(diag_ref, back - lon, 0, lon)
        put(sib_ref, back + lon, 0, lon)

    q = [jnp.broadcast_to(q_ref[0:1, t * LANES:(t + 1) * LANES], (8, LANES)) for t in range(tiles)]
    jump = [carry_ref[0:1, t * LANES:(t + 1) * LANES] for t in range(tiles)]
    zero = jnp.zeros((8, LANES), jnp.float32)
    none = jnp.zeros((1, LANES), jnp.float32)
    east_base = back - REACH

    for base, total, forward in ((east_base, east_sum, False), (0, west_sum, True)):
        def at(i, forward=forward):
            return i if forward else seg - 1 - i

        def totals(i, acc, base=base):
            return tuple(cells[r * tiles + t, pl.ds(base + at(i), 8, stride=seg), :] + q[t] * acc[n]
                         for n, (r, t) in enumerate(chains))

        acc = lax.fori_loop(0, seg, totals, (zero,) * len(chains), unroll=4)
        start = []
        for n, (r, t) in enumerate(chains):
            carry = none
            parts = [None] * 8
            for k in (range(8) if forward else range(7, -1, -1)):
                parts[k] = carry
                carry = acc[n][k:k + 1] + jump[t] * carry
            start.append(jnp.concatenate(parts, axis=0))

        def sums(i, acc, base=base, total=total):
            new = []
            for n, (r, t) in enumerate(chains):
                v = cells[r * tiles + t, pl.ds(base + at(i), 8, stride=seg), :] + q[t] * acc[n]
                total[r * tiles + t, pl.ds(at(i), 8, stride=seg), :] = v
                new.append(v)
            return tuple(new)

        lax.fori_loop(0, seg, sums, tuple(start), unroll=4)

    step = COLS

    def one_row(r, border_ref, border_row):
        width = widths_ref[r]
        for t in range(tiles):
            n = r * tiles + t
            far = jnp.broadcast_to(far_ref[r, 0:1, t * LANES:(t + 1) * LANES], (step, LANES))
            scale = jnp.broadcast_to(scale_ref[r, 0:1, t * LANES:(t + 1) * LANES], (step, LANES))
            for c in range(0, ext, step):
                near = east_sum[n, pl.ds(c, step), :] + west_sum[n, pl.ds(back - REACH + c, step), :]
                cut = east_sum[n, pl.ds(c + 1 + width, step), :] + west_sum[n, pl.ds(back - REACH + c - 1 - width, step), :]
                mid = cells[n, pl.ds(back - REACH + c, step), :]
                value = ((near - mid - far * cut) * scale).astype(jnp.bfloat16)
                level_ref[r, t, pl.ds(c, step), :] = value.astype(jnp.float32)
                if border_ref is not None:
                    border_ref[border_row, pl.ds(c, step), pl.ds(t * LANES, LANES)] = value

    @pl.loop(0, rows)
    def _(r):
        one_row(r, border_refs[0] if border_refs else None, r)


def smooth_piece(piece, place, rows, ext, info, widths, own, sib, opp, diag, q, carry, far, scale, extras):
    lon, channels = own.shape[1:]
    tiles = channels // LANES
    back = round_up(HMAX + 1 + REACH, 8)
    span = round_up(ext + HMAX + 1, 8)
    seg = max(back + ext - REACH, span) // 8
    geo = (lon, back, 8 * seg, seg, ext)
    smem, vmem = pl.BlockSpec(memory_space=pltpu.SMEM), pl.BlockSpec(memory_space=pltpu.VMEM)
    pair = pl.BlockSpec((rows, lon, channels), lambda i: (piece % 2, 0, 0))
    part = pl.BlockSpec((rows, lon, channels), lambda i: (place, 0, 0))
    table = pl.BlockSpec((rows, 1, channels), lambda i: (piece, 0, 0))
    border = jax.ShapeDtypeStruct((HALO + 1, ext, channels), jnp.bfloat16)
    of_rows = slice(piece * rows, (piece + 1) * rows)
    return pl.pallas_call(
        functools.partial(smooth_kernel, geo, len(extras)),
        grid=(1,),
        in_specs=[smem, smem, part, pair, part, part, vmem, vmem, table, table] + [vmem] * len(extras),
        out_specs=[vmem] * (1 + len(extras)),
        out_shape=[jax.ShapeDtypeStruct((rows, tiles, ext, LANES), jnp.float32)] + [border] * len(extras),
        scratch_shapes=[
            pltpu.VMEM((rows * tiles, round_up(back - REACH + 9 * seg, 8), LANES), jnp.float32),
            pltpu.VMEM((rows * tiles, round_up(9 * seg, 8), LANES), jnp.float32),
            pltpu.VMEM((rows * tiles, round_up(9 * seg, 8), LANES), jnp.float32),
        ],
        compiler_params=pltpu.CompilerParams(vmem_limit_bytes=28 * MIB),
        cost_estimate=pl.CostEstimate(flops=1000, bytes_accessed=1000, transcendentals=0),
        name="smooth",
    )(info, widths[of_rows], own, sib, opp, diag, q, carry, far, scale, *extras)


def update(src, r, t, c, count, u, v, zero):
    def at(dr, dc):
        return src[r + dr, t, pl.ds(PAD + c + dc + (zero if dc else 0), count), :]

    mid = at(0, 0)
    mid30 = 30.0 * mid
    e1, w1, e2, w2 = at(0, 1), at(0, -1), at(0, 2), at(0, -2)
    n1, s1, n2, s2 = at(1, 0), at(-1, 0), at(2, 0), at(-2, 0)
    first_x = (e2 - w2) - 8.0 * (e1 - w1)
    second_x = 16.0 * (e1 + w1) - (e2 + w2) - mid30
    first_y = (n2 - s2) - 8.0 * (n1 - s1)
    second_y = 16.0 * (n1 + s1) - (n2 + s2) - mid30
    change = u * (first_x + (6.0 * u) * second_x) + v * (first_y + (6.0 * v) * second_y)
    return mid + change


def put_rows(field, ref, base, count, ext):
    @pl.loop(0, count)
    def _(r):
        for t in range(field.shape[1]):
            field[base + r, t, pl.ds(PAD, ext), :] = ref[r, :, pl.ds(t * LANES, LANES)].astype(jnp.float32)


def step_rows(source, winds, zero, first, last, offset, start, stop, store):
    half = LANES // 2
    eastward = lax.broadcasted_iota(jnp.int32, (COLS, LANES), 1) < half

    @pl.loop(first, last)
    def _(r):
        for c in range(start, stop, COLS):
            count = min(COLS, stop - c)
            both = winds[r + offset, pl.ds(c, count), :].astype(jnp.float32) * (1.0 / 12.0)
            swapped = pltpu.roll(both, half, 1)
            u = jnp.where(eastward[:count], both, swapped)
            v = jnp.where(eastward[:count], swapped, both)
            for t in range(source.shape[1]):
                store(r, t, c, count, update(source, r + 2, t, c, count, u, v, zero))


class Copies:
    def __init__(self, sems):
        self.sems, self.used = sems, 0

    def start(self, source, target):
        copy = pltpu.make_async_copy(source, target, self.sems.at[self.used])
        self.used += 1
        copy.start()
        return copy

    def one_of(self, choice, sources, target):
        sem = self.sems.at[self.used]
        self.used += 1
        for i, source in enumerate(sources):
            @pl.when(choice == i)
            def _(source=source):
                pltpu.make_async_copy(source, target, sem).start()

        return pltpu.make_async_copy(sources[0], target, sem)


def store_in(field):
    def store(r, t, c, count, value):
        field[r, t, pl.ds(PAD + c, count), :] = value

    return store


def store_out(ref):
    def store(r, t, c, count, value):
        ref[r, pl.ds(c - REACH, count), pl.ds(t * LANES, LANES)] = value.astype(jnp.bfloat16)

    return store


class OwnRows:
    def __init__(self, polar, lon, ext, state_ref, edge_w_ref, edge_e_ref, parts, field, base, first, sems, started=False):
        tiles, count = field.shape[1], HALO * len(parts)
        self.polar, self.edges = polar, (edge_w_ref, edge_e_ref)
        self.place = (field, base, first, count, lon)
        self.smooth, self.plain = [], []
        for i, (ref, start) in enumerate(parts):
            target = field.at[pl.ds(base + i * HALO, HALO), :, pl.ds(PAD, ext), :]
            self.smooth.append(pltpu.make_async_copy(ref.at[pl.ds(start, HALO)], target, sems.at[i]))
        for t in range(tiles):
            self.plain.append(pltpu.make_async_copy(
                state_ref.at[pl.ds(first, count), :, pl.ds(t * LANES, LANES)],
                field.at[pl.ds(base, count), t, pl.ds(PAD + REACH, lon), :], sems.at[t]))
        if not started:
            self.each(lambda copy: copy.start())

    def each(self, act):
        @pl.when(self.polar)
        def _():
            for copy in self.smooth:
                act(copy)

        @pl.when(jnp.logical_not(self.polar))
        def _():
            for copy in self.plain:
                act(copy)

    def wait(self):
        field, base, first, count, lon = self.place
        edge_w_ref, edge_e_ref = self.edges

        @pl.when(jnp.logical_not(self.polar))
        def _():
            @pl.loop(0, count)
            def _(r):
                for t in range(field.shape[1]):
                    lanes = pl.ds(t * LANES, LANES)
                    field[base + r, t, pl.ds(PAD, REACH), :] = edge_w_ref[first + r, :, lanes].astype(jnp.float32)
                    field[base + r, t, pl.ds(PAD + REACH + lon, REACH), :] = edge_e_ref[first + r, :, lanes].astype(jnp.float32)

        self.each(lambda copy: copy.wait())


def strip(field, base, ext):
    return field.at[pl.ds(base, HALO), :, pl.ds(PAD, ext), :]


def winds_beyond(copies, origin, refs, winds, row):
    return [copies.one_of(origin, [ref.at[HALO, :, pl.ds(i * LANES, LANES)] for ref in refs], winds.at[row + i]) for i in range(2)]


def on_side(info_ref, outer, body):
    @pl.when(info_ref[LOW_HALF] == 1)
    def _():
        body(not outer)

    @pl.when(info_ref[LOW_HALF] == 0)
    def _():
        body(outer)


def border_kernel(outer, rows, lon, ext, info_ref, state_ref, edge_w_ref, edge_e_ref, winds_ref, late_ref, raw_ref, across_ref,
                  near_ref, far_ref, border_ref, level_ref, one_ref, field_a, field_b, halo_rows, winds, own_sem, sems):
    zero = info_ref[ZERO]
    origin, origins = info_ref[OUTER_FROM if outer else INNER_FROM], (late_ref, raw_ref, across_ref)

    def store_both(r, t, c, count, value):
        level_ref[r, t, pl.ds(c, count), :] = value
        border_ref[r, pl.ds(c, count), pl.ds(t * LANES, LANES)] = value.astype(jnp.bfloat16)

    def body(north):
        halo, own, first = (2 * HALO, 0, rows - 2 * HALO) if north else (0, HALO, 0)
        parts = ((far_ref, 0), (near_ref, 0)) if north else ((near_ref, 0), (far_ref, 0))
        copies = Copies(sems)
        halo_copy = copies.one_of(origin, [ref.at[pl.ds(0, HALO)] for ref in origins], halo_rows)
        mine = OwnRows(info_ref[POLAR] == 1, lon, ext, state_ref, edge_w_ref, edge_e_ref, parts, field_a, own, first, own_sem)
        wind_copies = [
            copies.start(winds_ref.at[pl.ds(first + 2 if north else 0, HALO + 2)], winds.at[pl.ds(0 if north else 2, HALO + 2)]),
            *winds_beyond(copies, origin, origins, winds, HALO + 2 if north else 0),
        ]
        halo_copy.wait()
        put_rows(field_a, halo_rows, halo, HALO, ext)
        mine.wait()
        for copy in wind_copies:
            copy.wait()

    def pass_on(north):
        pltpu.make_async_copy(strip(field_b, 0 if north else HALO, ext), one_ref, sems.at[4]).start()

    on_side(info_ref, outer, body)
    step_rows(field_a, winds, zero, 0, 2 * HALO, 0, 0, ext, store_in(field_b))
    on_side(info_ref, outer, pass_on)
    step_rows(field_b, winds, zero, 0, HALO, 2, 0, ext, store_both)
    pltpu.make_async_copy(strip(field_b, 0, ext), one_ref, sems.at[4]).wait()


def border_rows(outer, info, state, edges, winds, origins, near, far):
    rows, lon, channels = state.shape
    ext = winds.shape[1]
    tiles = channels // LANES
    vmem, hbm = pl.BlockSpec(memory_space=pltpu.VMEM), pl.BlockSpec(memory_space=pl.ANY)
    level = jax.ShapeDtypeStruct((HALO, tiles, ext, LANES), jnp.float32)
    return pl.pallas_call(
        functools.partial(border_kernel, outer, rows, lon, ext),
        in_specs=[pl.BlockSpec(memory_space=pltpu.SMEM), hbm, vmem, vmem] + [hbm] * 6,
        out_specs=[vmem, vmem, hbm],
        out_shape=[jax.ShapeDtypeStruct((HALO, ext, channels), jnp.bfloat16), level, level],
        scratch_shapes=[
            cells_of(3 * HALO, tiles, ext), cells_of(2 * HALO, tiles, ext),
            half_of(HALO, ext, channels), half_of(2 * HALO, ext, LANES),
            pltpu.SemaphoreType.DMA((2,)), pltpu.SemaphoreType.DMA((5,)),
        ],
        compiler_params=pltpu.CompilerParams(vmem_limit_bytes=20 * MIB),
        cost_estimate=pl.CostEstimate(flops=1000, bytes_accessed=1000, transcendentals=0),
        name="border_outer" if outer else "border_inner",
    )(info, state, *edges, winds, *origins, near, far)


def interior_kernel(rows, lon, ext, info_ref, state_ref, edge_w_ref, edge_e_ref, winds_ref, level_o_ref, level_i_ref,
                    one_o_ref, one_i_ref, smooth_o_ref, smooth_i_ref, out_ref, third_o_ref, third_i_ref,
                    field_a, field_b, field_c, part_ref, winds, sem, in_sem, out_sem):
    inner = rows - 4
    zero, low_half = info_ref[ZERO], info_ref[LOW_HALF] == 1

    def start(south, north):
        OwnRows(info_ref[POLAR] == 1, lon, ext, state_ref, edge_w_ref, edge_e_ref,
                ((south[0], 0), (north[0], 0)), field_a, 0, HALO, sem)
        copies = Copies(in_sem)
        copies.start(winds_ref.at[pl.ds(2, inner)], winds)
        for one, two, at_one, at_two in ((south[1], south[2], 0, 0), (north[1], north[2], inner - HALO, rows - HALO)):
            copies.start(one, strip(field_b, at_one, ext))
            copies.start(two, strip(field_c, at_two, ext))

    outer_refs, inner_refs = (smooth_o_ref, one_o_ref, level_o_ref), (smooth_i_ref, one_i_ref, level_i_ref)

    @pl.when(low_half)
    def _():
        start(outer_refs, inner_refs)

    @pl.when(jnp.logical_not(low_half))
    def _():
        start(inner_refs, outer_refs)

    OwnRows(info_ref[POLAR] == 1, lon, ext, state_ref, edge_w_ref, edge_e_ref,
            ((smooth_o_ref, 0), (smooth_i_ref, 0)), field_a, 0, HALO, sem, started=True).wait()
    pltpu.make_async_copy(winds_ref.at[pl.ds(2, inner)], winds, in_sem.at[0]).wait()

    def store(r, t, c, count, value):
        field_b[HALO + r, t, pl.ds(PAD + c, count), :] = value

    step_rows(field_a, winds, zero, 0, inner - 2 * HALO, HALO, 0, ext, store)
    for i in range(4):
        pltpu.make_async_copy(one_o_ref, strip(field_b, 0, ext), in_sem.at[1 + i]).wait()

    def store(r, t, c, count, value):
        field_c[HALO + r, t, pl.ds(PAD + c, count), :] = value

    step_rows(field_b, winds, zero, 0, inner - 4, 2, 0, ext, store)
    step_rows(field_c, winds, zero, 0, inner, 0, 0, ext, store_in(field_b))

    def hand_on(south_ref, north_ref):
        for i, (ref, base) in enumerate(((south_ref, 0), (north_ref, inner - HALO))):
            pltpu.make_async_copy(strip(field_b, base, ext), ref, out_sem.at[i]).start()

    @pl.when(low_half)
    def _():
        hand_on(third_o_ref, third_i_ref)

    @pl.when(jnp.logical_not(low_half))
    def _():
        hand_on(third_i_ref, third_o_ref)

    half = (rows - 2 * HALO) // 2
    results = []
    for i in range(2):
        step_rows(field_b, winds, zero, i * half, (i + 1) * half, 2, REACH, REACH + lon, store_out(part_ref))
        results.append(pltpu.make_async_copy(
            part_ref.at[pl.ds(i * half, half)], out_ref.at[pl.ds(HALO + i * half, half)], out_sem.at[2 + i]))
        results[i].start()
    for i in range(2):
        pltpu.make_async_copy(strip(field_b, 0, ext), third_o_ref, out_sem.at[i]).wait()
    for copy in results:
        copy.wait()


def interior(info, state, edges, winds, levels, ones, smooths):
    rows, lon, channels = state.shape
    ext = winds.shape[1]
    tiles = channels // LANES
    vmem, hbm = pl.BlockSpec(memory_space=pltpu.VMEM), pl.BlockSpec(memory_space=pl.ANY)
    third = jax.ShapeDtypeStruct((HALO, tiles, ext, LANES), jnp.float32)
    return pl.pallas_call(
        functools.partial(interior_kernel, rows, lon, ext),
        in_specs=[pl.BlockSpec(memory_space=pltpu.SMEM), hbm, vmem, vmem] + [hbm] * 7,
        out_specs=[hbm, hbm, hbm],
        out_shape=[jax.ShapeDtypeStruct((rows, lon, channels), jnp.bfloat16), third, third],
        scratch_shapes=[
            cells_of(rows - 2 * HALO, tiles, ext), cells_of(rows - 4, tiles, ext), cells_of(rows, tiles, ext),
            half_of(rows - 2 * HALO, lon, channels), half_of(rows - 4, ext, LANES),
            pltpu.SemaphoreType.DMA((2,)), pltpu.SemaphoreType.DMA((5,)), pltpu.SemaphoreType.DMA((4,)),
        ],
        compiler_params=pltpu.CompilerParams(vmem_limit_bytes=24 * MIB),
        cost_estimate=pl.CostEstimate(flops=1000, bytes_accessed=1000, transcendentals=0),
        name="interior",
    )(info, state, *edges, winds, *levels, *ones, *smooths)


def finish_kernel(outer, rows, lon, ext, _, info_ref, winds_ref, late_ref, raw_ref, across_raw_ref, border_ref, across_ref, level_ref, third_ref,
                  out_ref, near, last, winds, halo_rows, part_ref, in_sem, out_sem):
    zero = info_ref[ZERO]

    def body(north):
        mine, other = (0, HALO) if north else (HALO, 0)
        copies = Copies(in_sem)
        origin = info_ref[OUTER_FROM if outer else INNER_FROM]
        halo_copy = copies.one_of(origin, (border_ref, border_ref, across_ref), halo_rows)
        incoming = [
            copies.start(level_ref, strip(near, mine, ext)),
            copies.start(third_ref, strip(last, mine, ext)),
            copies.start(winds_ref.at[pl.ds(rows - HALO if north else 0, HALO)], winds.at[pl.ds(0 if north else 2, HALO)]),
            *winds_beyond(copies, origin, (late_ref, raw_ref, across_raw_ref), winds, HALO if north else 0),
        ]
        halo_copy.wait()
        put_rows(near, halo_rows, other, HALO, ext)
        for copy in incoming:
            copy.wait()

        def store(r, t, c, count, value):
            last[r + other, t, pl.ds(PAD + c, count), :] = value

        step_rows(near, winds, zero, 0, HALO, 2 if north else 0, 0, ext, store)
        results, half = [], HALO // 2
        for i in range(2):
            step_rows(last, winds, zero, i * half, (i + 1) * half, 0 if north else 2, REACH, REACH + lon, store_out(part_ref))
            place = out_ref.at[pl.ds((rows - HALO if north else 0) + i * half, half)]
            results.append(pltpu.make_async_copy(part_ref.at[pl.ds(i * half, half)], place, out_sem.at[i]))
            results[i].start()
        for copy in results:
            copy.wait()

    on_side(info_ref, outer, body)


def finish(outer, info, out, winds, origins, border, across, level, third):
    rows, lon, channels = out.shape
    ext = winds.shape[1]
    tiles = channels // LANES
    hbm = pl.BlockSpec(memory_space=pl.ANY)
    return pl.pallas_call(
        functools.partial(finish_kernel, outer, rows, lon, ext),
        in_specs=[hbm, pl.BlockSpec(memory_space=pltpu.SMEM)] + [hbm] * 8,
        out_specs=hbm,
        out_shape=jax.ShapeDtypeStruct(out.shape, out.dtype),
        input_output_aliases={0: 0},
        scratch_shapes=[
            cells_of(2 * HALO, tiles, ext), cells_of(2 * HALO, tiles, ext),
            half_of(HALO + 2, ext, LANES), half_of(HALO, ext, channels), half_of(HALO, lon, channels),
            pltpu.SemaphoreType.DMA((6,)),
            pltpu.SemaphoreType.DMA((2,)),
        ],
        compiler_params=pltpu.CompilerParams(vmem_limit_bytes=16 * MIB),
        cost_estimate=pl.CostEstimate(flops=1000, bytes_accessed=1000, transcendentals=0),
        name="finish_outer" if outer else "finish_inner",
    )(out, info, winds, *origins, border, across, level, third)


def half_of(rows, ext, channels):
    return pltpu.VMEM((rows, ext, channels), jnp.bfloat16)


def cells_of(rows, tiles, ext):
    return pltpu.VMEM((rows, tiles, ext + 2 * PAD, LANES), jnp.float32)


def per_device(state, winds, decay, widths):
    rows, lon, channels = state.shape
    fields = decay.shape[0]
    bands, tiles = lax.axis_size("lat"), lax.axis_size("lon")
    lat, lon_at = lax.axis_index("lat"), lax.axis_index("lon")
    quarter = bands // 4
    ext = round_up(lon + 2 * REACH, 16)
    fill = ext - lon - 2 * REACH
    axes = ("lat", "lon")

    middle = bands // 2

    def is_polar(band):
        return band < quarter or band >= bands - quarter

    def is_plain(band):
        return not is_polar(band)

    def inward(band):
        return band + 1 if band < middle else band - 1

    def outward(band):
        return band - 1 if band < middle else band + 1

    def over_lon(flip):
        return [(b * tiles + l, b * tiles + (l ^ flip)) for b in range(bands) if is_polar(b) for l in range(tiles)]

    def over_lat(to, wanted=lambda band: True):
        return [(b * tiles + l, to(b) * tiles + l) for b in range(bands)
                if wanted(b) and 0 <= to(b) < bands and (to(b) < middle) == (b < middle) for l in range(tiles)]

    across = [(b * tiles + l, inward(b) * tiles + l) for b in (middle - 1, middle) for l in range(tiles)]

    def move(cells, pairs):
        return lax.ppermute(cells, axes, pairs)

    low_half = lat < middle
    at_middle = (lat == middle - 1) | (lat == middle)
    polar = (lat < quarter) | (lat >= bands - quarter)
    outer_from = jnp.where((lat <= quarter) | (lat >= bands - quarter - 1), 0, 1)
    inner_from = jnp.where((lat < quarter - 1) | (lat > bands - quarter), 0, jnp.where(at_middle, 2, 1))
    numbers = [lon_at % 2, polar, outer_from, inner_from, lat < 0, low_half]
    info = jnp.stack([jnp.asarray(n, jnp.int32) for n in numbers])

    count = HALO
    starts = [jnp.where(low_half, f, rows - count - f) for f in (0, rows - count, count, rows - 2 * count)]

    def rows_of(values, i):
        return lax.dynamic_slice_in_dim(values, starts[i], count)

    def ordered(values):
        return jnp.concatenate([rows_of(values, i) for i in range(len(starts))], axis=0)

    def joined(cells, cols):
        return jnp.concatenate([cells.astype(jnp.bfloat16), winds[:, cols]], axis=2)

    east = [(l, (l + 1) % tiles) for l in range(tiles)]
    west = [((l + 1) % tiles, l) for l in range(tiles)]
    first, last = slice(0, REACH), slice(lon - REACH, lon)
    head, rear = tie(state[:, first], state[:, last])
    head, rear, cells = tie(joined(head, first), joined(rear, last), state)
    from_east = lax.ppermute(head, "lon", west)
    from_west = lax.ppermute(rear, "lon", east)

    opp = [None] * len(starts)
    circles = [rows_of(cells, 0).astype(jnp.bfloat16)]
    circles[0], cells = tie(circles[0], cells)
    opp[0] = move(circles[0], over_lon(2))
    circles += [rows_of(cells, i).astype(jnp.bfloat16) for i in range(1, len(starts))]

    edge_w, edge_e = from_west[:, :, :channels], from_east[:, :, :channels]

    def extend(inner, before, after):
        parts = [before, inner, after, jnp.zeros((inner.shape[0], fill, inner.shape[2]), inner.dtype)]
        return jnp.concatenate(parts, axis=1)

    winds_ext = extend(winds, from_west[:, :, channels:], from_east[:, :, channels:])

    def border(i, wind_first):
        wind = lax.dynamic_slice_in_dim(winds_ext, wind_first, 2)
        ends = extend(rows_of(cells, i).astype(jnp.bfloat16), rows_of(edge_w, i), rows_of(edge_e, i))
        return jnp.concatenate([ends, jnp.concatenate([wind[:1], wind[1:]], axis=2)], axis=0)

    outer_rows = border(0, jnp.where(low_half, 0, rows - 2))
    inner_rows = border(1, jnp.where(low_half, rows - 2, 0))
    raw_out = move(outer_rows, over_lat(outward, is_plain))
    raw_in = move(inner_rows, over_lat(inward, is_plain))
    raw_across = move(inner_rows, across)
    behind = outer_rows[HALO:], inner_rows[HALO:]

    circles[1], outer_rows = tie(circles[1], outer_rows)
    sib = move(jnp.concatenate(circles[:2], axis=0), over_lon(1))
    opp[1] = move(circles[1], over_lon(2))

    own_widths = ordered(lax.dynamic_slice_in_dim(widths, lat * rows, rows))
    rate = jnp.repeat(decay, channels // fields)[None, :]
    reach = own_widths.astype(jnp.float32)[:, None]
    q = jnp.exp(-rate)
    back = round_up(HMAX + 1 + REACH, 8)
    seg = max(back + ext - REACH, round_up(ext + HMAX + 1, 8)) // 8
    carry = jnp.exp(-rate * seg)
    far = jnp.exp(-rate * (reach + 1.0))[:, None, :]
    total = (-jnp.expm1(-rate * (reach + 1.0)) - q * jnp.expm1(-rate * reach)) / -jnp.expm1(-rate)
    scale = (1.0 / total)[:, None, :]

    edges = edge_w, edge_e
    smooths, late = [], []

    def smoothed(i, place, own, sib, opp, diag):
        return smooth_piece(i, place, count, ext, info, own_widths, own, sib, opp, diag, q, carry, far, scale, behind[i:i + 1])

    for i in range(2):
        if i == 0:
            opp[0], last_two = tie(opp[0], jnp.concatenate(circles[2:], axis=0))
            last_opp = move(last_two, over_lon(2))
        diag = move(opp[i], over_lon(1))
        smooth, ends = smoothed(i, 0, circles[i], sib, opp[i], diag)
        smooths.append(smooth)
        if i == 1:
            ends, raw_out = tie(ends, raw_out)
        late.append(move(ends, over_lat((outward, inward)[i], is_polar)))
        if i == 0:
            smooth, opp[1] = tie(smooth, opp[1])
        else:
            smooth, last_opp = tie(smooth, last_opp)

    last_opp, late[0], late[1], raw_in = tie(last_opp, late[0], late[1], raw_in)
    last_sib = move(last_two, over_lon(1))
    diag = move(last_opp, over_lon(1))
    smooths += smoothed(2, 0, last_two, last_sib, last_opp, diag)
    outer_rows, level_o, one_o = border_rows(
        True, info, state, edges, winds_ext, (late[1], raw_in, raw_in), smooths[0], smooths[2])
    going_out = move(outer_rows, over_lat(outward))
    smooths += smoothed(3, 1, last_two, last_sib, last_opp, diag)
    inner_origins, outer_origins = (late[0], raw_out, raw_across), (late[1], raw_in, raw_in)
    inner_rows, level_i, one_i = border_rows(
        False, info, state, edges, winds_ext, inner_origins, smooths[1], smooths[3])
    going_in = move(inner_rows, over_lat(inward))
    going_across = move(inner_rows, across)
    out, third_o, third_i = interior(info, state, edges, winds_ext, (level_o, level_i), (one_o, one_i), smooths[2:])
    out = finish(False, info, out, winds_ext, inner_origins, going_out, going_across, level_i, third_i)
    return finish(True, info, out, winds_ext, outer_origins, going_in, going_in, level_o, third_o)


def solution(mesh):
    in_specs = (P("lat", "lon", None), P("lat", "lon", None), P(), P())
    out_specs = P("lat", "lon", None)
    return jax.shard_map(
        per_device, mesh=mesh, in_specs=in_specs, out_specs=out_specs, check_vma=False
    )
```
